32 devices in a mesh: dp: 8 (over y, x, core), code: 4 (over z).
Axes of the slice: x: 2, y: 2, z: 4, core: 2. Of those that a mesh axis runs over, the one named last changes fastest.
Arguments:
- patches: bfloat16 [8, 496, 256], P('dp'), may hold values from -6 to 6
- lengths: int32 [8], P('dp'), may hold values from 248 to 496, as said below
- patch_masks: int32 [8, 496], P('dp'), may hold values from 0 to 1, as said below
- targets: int32 [8, 496], P('dp'), may hold values from 0 to 1023
- codebook: bfloat16 [1024, 256], P('code'), may hold values from -0.47851562 to 0.47851562
- params: float32 [19296256], P(('dp', 'code')), as said below
- first_moment: float32 [19296256], P(('dp', 'code')), may hold values from -7.581117e-07 to 7.581117e-07
- second_moment: float32 [19296256], P(('dp', 'code')), may hold values from 6.478701e-16 to 1.03659214e-14
- step_count: int32 [1], replicated, may hold values from 1 to 20
Outputs:
- new_params: float32 [19296256], P(('dp', 'code'))
- new_first: float32 [19296256], P(('dp', 'code'))
- new_second: float32 [19296256], P(('dp', 'code'))
- params_low: bfloat16 [19296256], P(('dp', 'code'))
- mean_loss: float32 [], replicated
- grad_norm: float32 [], replicated
- rel_grad: float32 [320, 12], replicated
The draws below stay inside these ranges and needn't reach their ends.
Inputs may be any that keep to these rules, and one draw needn't show every extreme that they name: `lengths`: each length is 248 or 496, and both occur. `patch_masks`: in each clip exactly 3 / 4 of its first length positions are 1, all others 0. `targets`: read only where patch_masks is 1. `params`: entries past 19293992 are zero.
All inputs are finite; a program needn't handle non-finite values.
Results may differ from the reference program's by a relative error of at most 0.024.
Values may be sent and summed in bfloat16 or wider, within the bound.
No kernel may reach another device: no remote copies, remote signals or barrier semaphores. Data moves between devices by JAX's collectives and lax.ppermute only.
A program may use at most 448 MiB of HBM per device.

```python
import math
import jax
import jax.numpy as jnp
import numpy as np
from jax import lax

D = 768
HEADS = 12
HEAD_DIM = 64
FF = 3072
PATCH_IN = 256
PROJ = 256
CODES = 1024
KERNEL = 128
GROUPS = 16
BUCKETS = 320
MAX_DIST = 800
LAYERS = 2
LONG = 496
SHORT = 248
VISIBLE = 124
CLIPS = 8
PARAMS = 19293992
FLAT = 19296256


def layout_list():
    return [('w_patch', (PATCH_IN, D)), ('glob_vec', (4, D)), ('conv_w', (KERNEL, D // GROUPS, D)), ('w_qkv', (LAYERS, D, 3 * D)), ('w_out', (LAYERS, D, D)), ('w_up', (LAYERS, D, FF)), ('w_down', (LAYERS, FF, D)), ('layer_vec', (LAYERS, 8 * D + FF)), ('gate_proj', (LAYERS, HEAD_DIM + 1, 8)), ('gate_scale', (LAYERS, HEADS)), ('rel_table', (BUCKETS, HEADS)), ('w_head', (D, PROJ))]


def segment_values(seg_name, base_draw):
    if seg_name == 'w_patch':
        return base_draw / math.sqrt(PATCH_IN)
    if seg_name == 'glob_vec':
        spread = np.repeat(np.array([0.2, 0.3, 0.3, 1.0], np.float32), D)
        centre = np.repeat(np.array([1.0, 0.0, 0.0, 0.0], np.float32), D)
        return base_draw * jnp.asarray(spread) + jnp.asarray(centre)
    if seg_name == 'conv_w':
        return base_draw / math.sqrt(KERNEL * (D // GROUPS))
    if seg_name == 'w_qkv' or seg_name == 'w_up':
        return base_draw / math.sqrt(D)
    if seg_name == 'w_out':
        return base_draw * 3.0 / math.sqrt(D)
    if seg_name == 'w_down':
        return base_draw * 2.0 / math.sqrt(FF)
    if seg_name == 'layer_vec':
        spread = np.concatenate([np.repeat(np.array([0.3, 0.3, 0.3, 0.2, 0.3, 0.3, 0.2, 0.3], np.float32), D), np.full(FF, 0.3, np.float32)])
        centre = np.concatenate([np.repeat(np.array([0, 0, 0, 1, 0, 0, 1, 0], np.float32), D), np.zeros(FF, np.float32)])
        return base_draw * jnp.asarray(np.tile(spread, LAYERS)) + jnp.asarray(np.tile(centre, LAYERS))
    if seg_name == 'gate_proj':
        spread = np.concatenate([np.full(HEAD_DIM * 8, 1.0 / math.sqrt(HEAD_DIM), np.float32), np.full(8, 0.3, np.float32)])
        return base_draw * jnp.asarray(np.tile(spread, LAYERS))
    if seg_name == 'gate_scale':
        return 1.0 + 0.3 * base_draw
    if seg_name == 'rel_table':
        return base_draw
    return base_draw / math.sqrt(D)


def draw_params(key, part):
    base_key = jax.random.fold_in(key, 11)
    pieces = []
    for seg_index, (seg_name, extent) in enumerate(layout_list()):
        amount = math.prod(extent)
        sub_key = jax.random.fold_in(base_key, seg_index)
        base_draw = jax.random.normal(sub_key, (amount,), jnp.float32)
        pieces.append(segment_values(seg_name, base_draw).astype(jnp.float32))
    flat_vals = jnp.concatenate(pieces)
    return jnp.concatenate([flat_vals, jnp.zeros((FLAT - PARAMS,), jnp.float32)])


def clip_draw(key):
    sub_key = jax.random.fold_in(key, 5)
    long_flag = jax.random.randint(jax.random.fold_in(sub_key, 1), (CLIPS,), 0, 2)
    long_flag = long_flag.at[0].set(1).at[1].set(0)
    lengths = (SHORT * (1 + long_flag)).astype(jnp.int32)
    shuffled = jax.vmap(lambda one_key: jax.random.permutation(one_key, LONG))(jax.random.split(jax.random.fold_in(sub_key, 2), CLIPS)).astype(jnp.int32)
    places = jnp.arange(LONG, dtype=jnp.int32)[None, :]
    live_slot = places < lengths[:, None]
    ranking = jnp.argsort(jnp.argsort(jnp.where(live_slot, shuffled, shuffled + LONG), axis=1, stable=True), axis=1, stable=True)
    masked = ranking < (3 * lengths // 4)[:, None]
    return (lengths, masked.astype(jnp.int32))


def draw_lengths(key, part):
    return clip_draw(key)[0]


def draw_patch_masks(key, part):
    return clip_draw(key)[1]


def with_ends(values, key, least, top_value):
    shape = values.shape
    place = [jax.random.randint(jax.random.fold_in(key, axis), (), 0, shape[axis]) for axis in range(len(shape))]
    values = values.at[tuple(place)].set(least)
    longest = shape.index(max(shape))
    place[longest] = (place[longest] + 1) % shape[longest]
    return values.at[tuple(place)].set(top_value)


def block_levels(key, dims, shards, least, top_value):
    loudness, own = 1.0, jax.random.fold_in(key, 6)
    for dim, parts in shards:
        heights = jnp.exp(jax.random.uniform(jax.random.fold_in(own, dim), (parts,), jnp.float32, least / len(shards), top_value / len(shards)))
        loudness = loudness * jnp.repeat(heights, dims[dim] // parts).reshape([-1 if axis == dim else 1 for axis in range(len(dims))])
    return loudness


def scatter_about(rng, shape, scale, limit, shards=(), kind=jnp.bfloat16):
    gain = block_levels(rng, shape, shards, -0.22, 0.18) if shards else 1.0
    result = jax.random.normal(rng, shape, jnp.float32) * scale * gain
    return jnp.minimum(jnp.maximum(result, -limit), limit).astype(kind)


def setup_inputs(seed: int = 0) -> dict:
    key_of = jax.random.split(jax.random.key(seed), 10)
    return {
        "patches": scatter_about(key_of[0], (CLIPS, LONG, PATCH_IN), 1.0, 6.0, ((0, 8),)),
        "lengths": draw_lengths(jax.random.fold_in(key_of[9], 71), 0),
        "patch_masks": draw_patch_masks(jax.random.fold_in(key_of[9], 71), 0),
        "targets": with_ends(jax.random.randint(key_of[3], (CLIPS, LONG), 0, CODES), jax.random.fold_in(key_of[3], 1), 0, CODES - 1).astype(jnp.int32),
        "codebook": scatter_about(key_of[4], (CODES, PROJ), 0.08, 0.47851562, ((0, 4),)),
        "params": draw_params(jax.random.fold_in(key_of[9], 71), 0),
        "first_moment": scatter_about(key_of[6], (FLAT,), (0.000555 / PARAMS ** 0.5), 7.581116960864165e-07, ((0, 32),), jnp.float32),
        "second_moment": jnp.clip(jnp.exp(math.log(1.0365921445862347e-14) - 2.7725887 * jax.random.uniform(key_of[7], (FLAT,), jnp.float32) ** block_levels(key_of[7], (FLAT,), ((0, 32),), -0.2, 0.2)), 6.478700903663967e-16, 1.0365921445862347e-14),
        "step_count": jax.random.randint(key_of[8], (1,), 1, 21).astype(jnp.int32),
    }


NORM_EPSILON = 1e-05
UNIT_EPSILON = 1e-06
DEEP_ALPHA = 2.2133638394006434
LOGIT_SCALE = 25.0
CLIP_NORM = 0.005
LEARN_RATE = 0.02
BETA_ONE = 0.9
BETA_TWO = 0.999
ADAM_EPSILON = 1e-10
WEIGHT_DECAY = 0.01
MASK_FILL = -1000000000.0
HIGHEST = lax.Precision.HIGHEST

@jax.custom_vjp
def low(v):
    return lax.optimization_barrier(v.astype(jnp.bfloat16)).astype(jnp.float32)

@jax.custom_vjp
def low_back(v):
    return v

def low_keep(v):
    return (low(v), None)

def low_pass(kept, grad):
    return (grad,)

def back_keep(v):
    return (v, None)

def back_low(kept, grad):
    return (low(grad),)
low.defvjp(low_keep, low_pass)
low_back.defvjp(back_keep, back_low)

def layout():
    return [('w_patch', (PATCH_IN, D)), ('glob_vec', (4, D)), ('conv_w', (KERNEL, D // GROUPS, D)), ('w_qkv', (LAYERS, D, 3 * D)), ('w_out', (LAYERS, D, D)), ('w_up', (LAYERS, D, FF)), ('w_down', (LAYERS, FF, D)), ('layer_vec', (LAYERS, 8 * D + FF)), ('gate_proj', (LAYERS, HEAD_DIM + 1, 8)), ('gate_scale', (LAYERS, HEADS)), ('rel_table', (BUCKETS, HEADS)), ('w_head', (D, PROJ))]

def unpack(flat_vals):
    pieces = {}
    offset = 0
    for seg_name, extent in layout():
        amount = math.prod(extent)
        pieces[seg_name] = flat_vals[offset:offset + amount].reshape(extent)
        offset += amount
    return pieces

def bucket_onehot():
    offsets = np.arange(-(LONG - 1), LONG)
    half_count = BUCKETS // 2
    exact_count = half_count // 2
    distance = np.abs(offsets)
    scaled = np.log(np.maximum(distance, 1) / exact_count) / np.log(MAX_DIST / exact_count) * (half_count - exact_count)
    larger = np.minimum(exact_count + np.maximum(scaled, 0.0).astype(np.int64), half_count - 1)
    bucket = (offsets > 0) * half_count + np.where(distance < exact_count, distance, larger)
    return (bucket[:, None] == np.arange(BUCKETS)[None, :]).astype(np.float32)

def clip_layout(lengths, patch_masks):
    places = jnp.arange(LONG, dtype=jnp.int32)
    live_slot = places[None, :] < lengths[:, None]
    visible = live_slot & (patch_masks == 0)
    sort_order = jnp.argsort(jnp.where(visible, 0, 1).astype(jnp.int32), axis=1, stable=True).astype(jnp.int32)
    inverse = jnp.argsort(sort_order, axis=1, stable=True).astype(jnp.int32)
    seen_place = sort_order[:, :VISIBLE]
    seen_valid = places[None, :VISIBLE] < (lengths // 4)[:, None]
    rank_place = jnp.minimum(inverse, VISIBLE - 1)
    return (live_slot, visible, seen_place, seen_valid, rank_place)

def position_bias(rel_offsets, positions):
    offset_idx = positions[:, None, :] - positions[:, :, None] + (LONG - 1)
    head_table = jnp.transpose(rel_offsets)
    return jnp.transpose(jnp.take(head_table, offset_idx, axis=1), (1, 0, 2, 3))

def layer_norm(before, norm_gain, norm_shift):
    centred = before - lax.optimization_barrier(jnp.mean(before, axis=-1, keepdims=True))
    return centred * lax.rsqrt(lax.optimization_barrier(jnp.mean(centred * centred, axis=-1, keepdims=True)) + NORM_EPSILON) * norm_gain + norm_shift

def vec_part(vector, slot_index):
    return vector[slot_index * D:(slot_index + 1) * D]

def layer_weights(pieces, layer_index):
    return {seg_name: pieces[seg_name][layer_index] for seg_name in ('w_qkv', 'w_out', 'w_up', 'w_down', 'layer_vec', 'gate_proj', 'gate_scale')}

def layer_apply(hidden, positions, key_valid, weights, rel_offsets):
    batch_size, length = (hidden.shape[0], hidden.shape[1])
    vector = weights['layer_vec']
    in_low = low(hidden)
    qkv_proj = low_back(jnp.einsum('bld,de->ble', in_low, weights['w_qkv'], precision=HIGHEST))
    query_low = low((qkv_proj[..., :D] + vec_part(vector, 0)) * HEAD_DIM ** (-0.5)).reshape(batch_size, length, HEADS, HEAD_DIM)
    key_low = low(qkv_proj[..., D:2 * D]).reshape(batch_size, length, HEADS, HEAD_DIM)
    value_low = low(qkv_proj[..., 2 * D:] + vec_part(vector, 1)).reshape(batch_size, length, HEADS, HEAD_DIM)
    heads_in = in_low.reshape(batch_size, length, HEADS, HEAD_DIM)
    gate_logit = jnp.einsum('blhd,de->blhe', heads_in, weights['gate_proj'][:HEAD_DIM], precision=HIGHEST) + weights['gate_proj'][HEAD_DIM]
    gate_pair = jax.nn.sigmoid(lax.optimization_barrier(jnp.sum(gate_logit.reshape(batch_size, length, HEADS, 2, 4), axis=-1)))
    gate_vals = gate_pair[..., 0] * (gate_pair[..., 1] * weights['gate_scale'] - 1.0) + 2.0
    pos_bias = position_bias(rel_offsets, positions)
    scores = low_back(jnp.einsum('bqhd,bkhd->bhqk', query_low, key_low, precision=HIGHEST))
    scores = scores + jnp.transpose(gate_vals, (0, 2, 1))[..., None] * pos_bias
    scores = scores + jnp.where(key_valid, 0.0, MASK_FILL)[:, None, None, :]
    attn_probs = jax.nn.softmax(scores, axis=-1)
    attended = low(low_back(jnp.einsum('bhqk,bkhd->bqhd', low(attn_probs), value_low, precision=HIGHEST))).reshape(batch_size, length, D)
    attn_out = low_back(jnp.einsum('bld,de->ble', attended, weights['w_out'], precision=HIGHEST)) + vec_part(vector, 2)
    mid_rows = layer_norm(DEEP_ALPHA * hidden + attn_out, vec_part(vector, 3), vec_part(vector, 4))
    pre_act = low_back(jnp.einsum('bld,df->blf', low(mid_rows), weights['w_up'], precision=HIGHEST)) + vector[8 * D:]
    act_low = low(jax.nn.gelu(pre_act, approximate=False))
    ffn_out = low_back(jnp.einsum('blf,fd->bld', act_low, weights['w_down'], precision=HIGHEST)) + vec_part(vector, 5)
    return layer_norm(DEEP_ALPHA * mid_rows + ffn_out, vec_part(vector, 6), vec_part(vector, 7))

def group_loss(flat_vals, patch_rows, lengths, patch_masks, targets, code_rows):
    pieces = unpack(low(flat_vals))
    clip_count = patch_rows.shape[0]
    live_slot, visible, seen_place, seen_valid, rank_place = clip_layout(lengths, patch_masks)
    rel_offsets = jnp.dot(jnp.asarray(bucket_onehot()), pieces['rel_table'], precision=HIGHEST)
    glob_vec = pieces['glob_vec']
    embedded = low_back(jnp.einsum('btp,pd->btd', patch_rows, pieces['w_patch'], precision=HIGHEST))
    start_rows = layer_norm(embedded, glob_vec[0], glob_vec[1]) * live_slot[..., None].astype(jnp.float32)
    conv_raw = low_back(lax.conv_general_dilated(low(start_rows), pieces['conv_w'], (1,), [(KERNEL // 2, KERNEL // 2 - 1)], dimension_numbers=('NWC', 'WIO', 'NWC'), feature_group_count=GROUPS, precision=HIGHEST))
    full_rows = start_rows + jax.nn.gelu(conv_raw + glob_vec[2], approximate=False)
    seen_rows = jnp.take_along_axis(full_rows, seen_place[..., None], axis=1)
    encoded = layer_apply(seen_rows, seen_place, seen_valid, layer_weights(pieces, 0), rel_offsets)
    placed = jnp.take_along_axis(encoded, rank_place[..., None], axis=1)
    hidden = jnp.where(visible[..., None], placed, glob_vec[3])
    positions = jnp.broadcast_to(jnp.arange(LONG, dtype=jnp.int32)[None, :], (clip_count, LONG))
    for layer_index in range(1, LAYERS):
        hidden = layer_apply(hidden, positions, live_slot, layer_weights(pieces, layer_index), rel_offsets)
    row_low = low(hidden.reshape(-1, D))
    projected = low_back(jnp.dot(row_low, pieces['w_head'], precision=HIGHEST))
    unit_rows = projected * lax.rsqrt(lax.optimization_barrier(jnp.sum(projected * projected, axis=-1, keepdims=True)) + UNIT_EPSILON)
    logits = LOGIT_SCALE * low_back(jnp.dot(low(unit_rows), jnp.transpose(code_rows), precision=HIGHEST))
    target_flat = jnp.clip(targets.reshape(-1), 0, CODES - 1).astype(jnp.int32)
    picked = jnp.take_along_axis(logits, target_flat[:, None], axis=1)[:, 0]
    live_rows = (patch_masks.reshape(-1) == 1).astype(jnp.float32)
    return jnp.sum((jax.scipy.special.logsumexp(logits, axis=1) - picked) * live_rows)

def reference(patches, lengths, patch_masks, targets, codebook, params, first_moment, second_moment, step_count):
    code_rows = codebook.astype(jnp.float32)
    group_clips = 8
    group_count = CLIPS // group_clips
    patch_groups = patches.astype(jnp.float32).reshape(group_count, group_clips, LONG, PATCH_IN)
    length_groups = lengths.reshape(group_count, group_clips)
    mask_groups = patch_masks.reshape(group_count, group_clips, LONG)
    target_groups = targets.reshape(group_count, group_clips, LONG)

    def one_group(carry, batch_part):
        patch_rows, length_part, mask_part, target_part = batch_part
        loss_part, pullback = jax.vjp(lambda flat_vals: group_loss(flat_vals, patch_rows, length_part, mask_part, target_part, code_rows), params)
        grad_part, = pullback(jnp.ones((), jnp.float32))
        return ((carry[0] + grad_part, carry[1] + loss_part), None)
    (grad_sum, loss_sum), _ = lax.scan(one_group, (jnp.zeros_like(params), jnp.zeros((), jnp.float32)), (patch_groups, length_groups, mask_groups, target_groups))
    count = jnp.sum((patch_masks == 1).astype(jnp.float32))
    grads = grad_sum / count
    grad_norm = jnp.sqrt(jnp.sum(grads * grads))
    clipped = grads * jnp.minimum(1.0, CLIP_NORM / grad_norm)
    rel_grad = unpack(clipped)['rel_table']
    step_value = step_count[0].astype(jnp.float32)
    new_first = BETA_ONE * first_moment + (1.0 - BETA_ONE) * clipped
    new_second = BETA_TWO * second_moment + (1.0 - BETA_TWO) * clipped * clipped
    first_hat = new_first / (1.0 - BETA_ONE ** step_value)
    second_hat = new_second / (1.0 - BETA_TWO ** step_value)
    new_params = params - LEARN_RATE * (first_hat / (jnp.sqrt(second_hat) + ADAM_EPSILON) + WEIGHT_DECAY * params)
    return (new_params, new_first, new_second, new_params.astype(jnp.bfloat16), loss_sum / count, grad_norm, rel_grad)
```

```python
import functools
import math

import jax
import jax.numpy as jnp
import numpy as np
from jax import lax
from jax.experimental import pallas as pl
from jax.experimental.pallas import tpu as pltpu
from jax.sharding import PartitionSpec as P

D = 768
HEADS = 12
HEAD_DIM = 64
FF = 3072
PATCH_IN = 256
PROJ = 256
KERNEL = 128
GROUPS = 16
WIDTH = D // GROUPS
BUCKETS = 320
MAX_DIST = 800
LAYERS = 2
LONG = 496
VISIBLE = 124
ROWS = 512
SEEN = 128
SPAN = 1024

NORM_EPSILON = 1e-05
UNIT_EPSILON = 1e-06
DEEP_ALPHA = 2.2133638394006434
LOGIT_SCALE = 25.0
CLIP_NORM = 0.005
LEARN_RATE = 0.02
BETA_ONE = 0.9
BETA_TWO = 0.999
ADAM_EPSILON = 1e-10
WEIGHT_DECAY = 0.01
MASK_FILL = -1000000000.0
HIGHEST = lax.Precision.HIGHEST
BF = jnp.bfloat16
F32 = jnp.float32
VMEM_LIMIT = 56 << 20


def layout():
    return [
        ("w_patch", (PATCH_IN, D)),
        ("glob_vec", (4, D)),
        ("conv_w", (KERNEL, WIDTH, D)),
        ("w_qkv", (LAYERS, D, 3 * D)),
        ("w_out", (LAYERS, D, D)),
        ("w_up", (LAYERS, D, FF)),
        ("w_down", (LAYERS, FF, D)),
        ("layer_vec", (LAYERS, 8 * D + FF)),
        ("gate_proj", (LAYERS, HEAD_DIM + 1, 8)),
        ("gate_scale", (LAYERS, HEADS)),
        ("rel_table", (BUCKETS, HEADS)),
        ("w_head", (D, PROJ)),
    ]


def starts():
    where = {}
    offset = 0
    for seg_name, extent in layout():
        where[seg_name] = offset
        offset += math.prod(extent)
    return where


def bucket_onehot():
    offsets = np.arange(-(LONG - 1), LONG)
    half_count = BUCKETS // 2
    exact_count = half_count // 2
    distance = np.abs(offsets)
    scaled = (
        np.log(np.maximum(distance, 1) / exact_count)
        / np.log(MAX_DIST / exact_count)
        * (half_count - exact_count)
    )
    larger = np.minimum(exact_count + np.maximum(scaled, 0.0).astype(np.int64), half_count - 1)
    bucket = (offsets > 0) * half_count + np.where(distance < exact_count, distance, larger)
    return (bucket[:, None] == np.arange(BUCKETS)[None, :]).astype(np.float32)


def span_onehot():
    shift = SPAN // 2 - (LONG - 1)
    table = np.zeros((SPAN, BUCKETS), np.float32)
    table[shift : shift + 2 * LONG - 1] = bucket_onehot()
    return table


def params_of(grid_rank=1):
    return pltpu.CompilerParams(
        dimension_semantics=("arbitrary",) * grid_rank, vmem_limit_bytes=VMEM_LIMIT
    )


def dot_nn(left, right):
    return lax.dot_general(left, right, (((1,), (0,)), ((), ())), preferred_element_type=F32)


def dot_nt(left, right):
    return lax.dot_general(left, right, (((1,), (1,)), ((), ())), preferred_element_type=F32)


def dot_tn(left, right):
    return lax.dot_general(left, right, (((0,), (0,)), ((), ())), preferred_element_type=F32)


TAPS = 16
SLOT = 256


def lane_masks(width):
    group = np.arange(width)[None, :] // WIDTH
    return (group == np.arange(width // WIDTH)[:, None]).astype(np.float32)


def shifted_taps(source_ref, target_ref, count):
    for tap in range(TAPS):
        target_ref[:, tap * SLOT : (tap + 1) * SLOT] = source_ref[tap : tap + count, :].astype(BF)


def conv_forward_kernel(in_ref, weight_ref, mask_ref, out_ref, taps_ref, block_ref):
    step = pl.program_id(0)
    width = weight_ref.shape[1]

    @pl.when(step == 0)
    def _():
        shifted_taps(in_ref, taps_ref, taps_ref.shape[0])
        block_ref[...] = jnp.zeros_like(block_ref)

    for tap in range(TAPS):
        piece = weight_ref[tap * WIDTH : (tap + 1) * WIDTH, :]
        for group in range(width // WIDTH):
            low = tap * SLOT + group * WIDTH
            block_ref[low : low + WIDTH, :] = piece * mask_ref[group : group + 1, :]
    begin = pl.multiple_of(step * TAPS, TAPS)
    term = dot_nn(taps_ref[pl.ds(begin, ROWS), :], block_ref[...])

    @pl.when(step == 0)
    def _():
        out_ref[...] = term

    @pl.when(step > 0)
    def _():
        out_ref[...] += term


def conv_input_kernel(in_ref, weight_ref, mask_ref, out_ref, taps_ref, block_ref):
    step = pl.program_id(0)
    width = weight_ref.shape[1]

    @pl.when(step == 0)
    def _():
        shifted_taps(in_ref, taps_ref, taps_ref.shape[0])
        block_ref[...] = jnp.zeros_like(block_ref)

    for tap in range(TAPS):
        piece = weight_ref[tap * WIDTH : (tap + 1) * WIDTH, :]
        low = (TAPS - 1 - tap) * SLOT
        for group in range(width // WIDTH):
            block_ref[group * WIDTH : (group + 1) * WIDTH, low : low + width] = (
                piece * mask_ref[group : group + 1, :]
            )
    begin = pl.multiple_of((pl.num_programs(0) - 1 - step) * TAPS, TAPS)
    term = dot_nt(taps_ref[pl.ds(begin, ROWS), :], block_ref[...])

    @pl.when(step == 0)
    def _():
        out_ref[...] = term

    @pl.when(step > 0)
    def _():
        out_ref[...] += term


def conv_call(kernel, conv_in, weight, front, nt):
    width = weight.shape[1]
    steps = KERNEL // TAPS
    count = ROWS + KERNEL - TAPS
    padded = jnp.pad(
        conv_in.astype(F32),
        ((front, count + TAPS - front - conv_in.shape[0]), (0, SLOT - width)),
    )
    block = (width, TAPS * SLOT) if nt else (TAPS * SLOT, width)
    return pl.pallas_call(
        kernel,
        grid=(steps,),
        in_specs=[
            pl.BlockSpec(padded.shape, lambda i: (0, 0)),
            pl.BlockSpec((TAPS * WIDTH, width), lambda i: (i, 0)),
            pl.BlockSpec((width // WIDTH, width), lambda i: (0, 0)),
        ],
        out_specs=pl.BlockSpec((ROWS, width), lambda i: (0, 0)),
        out_shape=jax.ShapeDtypeStruct((ROWS, width), F32),
        scratch_shapes=[pltpu.VMEM((count, TAPS * SLOT), BF), pltpu.VMEM(block, BF)],
        compiler_params=params_of(),
    )(padded, weight, jnp.asarray(lane_masks(width), BF))


def conv_weight_kernel(in_ref, grad_ref, mask_ref, out_ref, taps_ref):
    width = grad_ref.shape[2]

    @pl.when(pl.program_id(1) == 0)
    def _():
        shifted_taps(in_ref.at[0], taps_ref, taps_ref.shape[0])

    begin = pl.multiple_of(pl.program_id(1) * TAPS, TAPS)
    term = dot_tn(taps_ref[pl.ds(begin, ROWS), :], grad_ref[0])
    for tap in range(TAPS):
        total = None
        for group in range(width // WIDTH):
            low = tap * SLOT + group * WIDTH
            piece = term[low : low + WIDTH, :] * mask_ref[group : group + 1, :]
            total = piece if total is None else total + piece
        out_ref[0, tap * WIDTH : (tap + 1) * WIDTH, :] = total.astype(BF)


def conv_weight_grad(conv_in, grad_low):
    width = 4 * WIDTH
    parts = D // width
    count = ROWS + KERNEL - TAPS
    front = KERNEL // 2
    padded = jnp.pad(
        conv_in.astype(F32), ((front, count + TAPS - front - conv_in.shape[0]), (0, 0))
    )
    padded = jnp.pad(
        jnp.transpose(padded.reshape(-1, parts, width), (1, 0, 2)),
        ((0, 0), (0, 0), (0, SLOT - width)),
    )
    grads = jnp.transpose(grad_low.reshape(ROWS, parts, width), (1, 0, 2))
    out = pl.pallas_call(
        conv_weight_kernel,
        grid=(parts, KERNEL // TAPS),
        in_specs=[
            pl.BlockSpec((1,) + padded.shape[1:], lambda p, i: (p, 0, 0)),
            pl.BlockSpec((1, ROWS, width), lambda p, i: (p, 0, 0)),
            pl.BlockSpec((width // WIDTH, width), lambda p, i: (0, 0)),
        ],
        out_specs=pl.BlockSpec((1, TAPS * WIDTH, width), lambda p, i: (p, i, 0)),
        out_shape=jax.ShapeDtypeStruct((parts, KERNEL * WIDTH, width), BF),
        scratch_shapes=[pltpu.VMEM((count, TAPS * SLOT), BF)],
        compiler_params=params_of(2),
    )(padded, grads, jnp.asarray(lane_masks(width), F32))
    return jnp.transpose(out, (1, 0, 2)).reshape(KERNEL * WIDTH, D)


BLOCK = 128


def head_column(table, head):
    lane = lax.broadcasted_iota(jnp.int32, (1, BLOCK), 1)
    return jnp.sum(jnp.where(lane == head, table, 0.0), axis=1, keepdims=True)


def toeplitz(span_ref, head):
    row = jnp.broadcast_to(span_ref[pl.ds(head, 1), :], (BLOCK, SPAN))
    return pltpu.roll(row, 0, 1, stride=1, stride_axis=0)


def seen_bias(turned, select):
    rows = [turned[:, ROWS - low : SPAN - low] for low in range(0, ROWS, BLOCK)]
    table = jnp.concatenate(rows, axis=0).astype(BF)
    return dot_nt(dot_nn(select, table).astype(BF), select)


def attention_forward_kernel(*refs, picked):
    if picked:
        q_ref, k_ref, v_ref, gate_ref, span_ref, fill_ref, pick_ref, out_ref, lse_ref = refs
    else:
        q_ref, k_ref, v_ref, gate_ref, span_ref, fill_ref, out_ref, lse_ref = refs
    step = pl.program_id(0)
    length = q_ref.shape[0]
    lane = lax.broadcasted_iota(jnp.int32, (1, BLOCK), 1)

    @pl.when(step == 0)
    def _():
        lse_ref[...] = jnp.zeros_like(lse_ref)

    fill = fill_ref[0:1, :]
    for side in range(2):
        head = step * 2 + side
        cols = slice(side * HEAD_DIM, (side + 1) * HEAD_DIM)
        keys = k_ref[:, cols]
        vals = v_ref[:, cols]
        turned = toeplitz(span_ref, head)
        if picked:
            single = seen_bias(turned, pick_ref[...])
        for low in range(0, length, BLOCK):
            rows = slice(low, low + BLOCK)
            bias = single if picked else turned[:, ROWS - low : SPAN - low]
            gate = head_column(gate_ref[rows, :], head)
            scores = dot_nt(q_ref[rows, cols], keys) + gate * bias + fill
            top = jnp.max(scores, axis=1, keepdims=True)
            weights = jnp.exp(scores - top)
            total = jnp.sum(weights, axis=1, keepdims=True)
            probs = (weights * (1.0 / total)).astype(BF)
            out_ref[rows, cols] = dot_nn(probs, vals).astype(BF)
            lse_ref[rows, :] += jnp.where(lane == head, top + jnp.log(total), 0.0)


def pair_spec(length):
    return pl.BlockSpec((length, 2 * HEAD_DIM), lambda i: (0, i))


def whole_spec(shape):
    return pl.BlockSpec(shape, lambda i: (0,) * len(shape))


def attention_forward(query, keyv, value, gate, span, fill, pick):
    length = query.shape[0]
    args = [query, keyv, value, gate, span, fill] + ([] if pick is None else [pick])
    return pl.pallas_call(
        functools.partial(attention_forward_kernel, picked=pick is not None),
        grid=(HEADS // 2,),
        in_specs=[pair_spec(length)] * 3 + [whole_spec(a.shape) for a in args[3:]],
        out_specs=[pair_spec(length), whole_spec((length, BLOCK))],
        out_shape=[
            jax.ShapeDtypeStruct((length, D), BF),
            jax.ShapeDtypeStruct((length, BLOCK), F32),
        ],
        compiler_params=params_of(),
    )(*args)


def attention_backward_kernel(*refs, picked):
    if picked:
        (q_ref, k_ref, v_ref, up_ref, gate_ref, span_ref, fill_ref, lse_ref, pick_ref) = refs[:9]
    else:
        (q_ref, k_ref, v_ref, up_ref, gate_ref, span_ref, fill_ref, lse_ref) = refs[:8]
    out_ref, sum_ref, dgate_ref, dspan_ref, key_ref, val_ref, diag_ref = refs[-7:]
    step = pl.program_id(0)
    length = q_ref.shape[0]
    lane = lax.broadcasted_iota(jnp.int32, (1, BLOCK), 1)

    @pl.when(step == 0)
    def _():
        dgate_ref[...] = jnp.zeros_like(dgate_ref)
        dspan_ref[...] = jnp.zeros_like(dspan_ref)

    fill = fill_ref[0:1, :]
    for side in range(2):
        head = step * 2 + side
        cols = slice(side * HEAD_DIM, (side + 1) * HEAD_DIM)
        keys = k_ref[:, cols]
        vals = v_ref[:, cols]
        turned = toeplitz(span_ref, head)
        if picked:
            single = seen_bias(turned, pick_ref[...])
        query_sum = jnp.zeros((1, HEAD_DIM), F32)
        diag_ref[...] = jnp.zeros_like(diag_ref)
        for low in range(0, length, BLOCK):
            rows = slice(low, low + BLOCK)
            query = q_ref[rows, cols]
            upstream = up_ref[rows, cols]
            bias = single if picked else turned[:, ROWS - low : SPAN - low]
            gate = head_column(gate_ref[rows, :], head)
            lse = head_column(lse_ref[rows, :], head)
            probs = jnp.exp(dot_nt(query, keys) + gate * bias + fill - lse)
            grad_probs = dot_nt(upstream, vals)
            grad_scores = probs * (
                grad_probs - jnp.sum(probs * grad_probs, axis=1, keepdims=True)
            )
            dgate = jnp.sum(grad_scores * bias, axis=1, keepdims=True)
            dgate_ref[rows, :] += jnp.where(lane == head, dgate, 0.0)
            grad_bias = grad_scores * gate
            if picked:
                select = pick_ref[...]
                high = grad_bias.astype(BF)
                rest = (grad_bias - high.astype(F32)).astype(BF)
                table = dot_tn(select, dot_nn(high, select).astype(BF)) + dot_tn(
                    select, dot_nn(rest, select).astype(BF)
                )
                for base in range(0, ROWS, BLOCK):
                    diag_ref[:, ROWS - base : SPAN - base] += table[base : base + BLOCK, :]
            else:
                diag_ref[:, ROWS - low : SPAN - low] += grad_bias
            low_scores = grad_scores.astype(BF)
            grad_query = dot_nn(low_scores, keys) * HEAD_DIM ** (-0.5)
            query_sum += jnp.sum(grad_query, axis=0, keepdims=True)
            out_ref[0, rows, cols] = grad_query.astype(BF)
            key_term = dot_tn(low_scores, query)
            val_term = dot_tn(probs.astype(BF), upstream)
            if low == 0:
                key_ref[...] = key_term
                val_ref[...] = val_term
            else:
                key_ref[...] += key_term
                val_ref[...] += val_term
        out_ref[1, :, cols] = key_ref[...].astype(BF)
        out_ref[2, :, cols] = val_ref[...].astype(BF)
        sum_ref[0:1, cols] = query_sum
        sum_ref[1:2, cols] = jnp.sum(val_ref[...], axis=0, keepdims=True)
        turn = diag_ref[...]
        half = BLOCK // 2
        while half:
            turn = turn[:half, :] + pltpu.roll(turn[half:, :], SPAN - half, 1)
            half //= 2
        dspan_ref[pl.ds(head, 1), :] = turn


def attention_backward(query, keyv, value, upstream, gate, span, fill, lse, pick):
    length = query.shape[0]
    args = [query, keyv, value, upstream, gate, span, fill, lse]
    args = args + ([] if pick is None else [pick])
    return pl.pallas_call(
        functools.partial(attention_backward_kernel, picked=pick is not None),
        grid=(HEADS // 2,),
        in_specs=[pair_spec(length)] * 4 + [whole_spec(a.shape) for a in args[4:]],
        out_specs=[
            pl.BlockSpec((3, length, 2 * HEAD_DIM), lambda i: (0, 0, i)),
            pl.BlockSpec((8, 2 * HEAD_DIM), lambda i: (0, i)),
            whole_spec((length, BLOCK)),
            whole_spec((16, SPAN)),
        ],
        out_shape=[
            jax.ShapeDtypeStruct((3, length, D), BF),
            jax.ShapeDtypeStruct((8, D), F32),
            jax.ShapeDtypeStruct((length, BLOCK), F32),
            jax.ShapeDtypeStruct((16, SPAN), F32),
        ],
        scratch_shapes=[
            pltpu.VMEM((length, HEAD_DIM), F32),
            pltpu.VMEM((length, HEAD_DIM), F32),
            pltpu.VMEM((BLOCK, SPAN), F32),
        ],
        compiler_params=params_of(),
    )(*args)


def weight_grad_kernel(left_ref, right_ref, out_ref, turn_ref):
    rows = left_ref.shape[1]
    strips = right_ref.shape[1] // 128
    grad = dot_tn(left_ref[...], right_ref[...])
    for strip in range(strips):
        turn_ref[pl.ds(strip, rows, stride=strips), :] = grad[:, strip * 128 : (strip + 1) * 128]
    out_ref[...] = turn_ref[...].astype(BF)


def weight_grad(left, right, rows=128):
    length, depth = left.shape
    strips = right.shape[1] // 128
    return pl.pallas_call(
        weight_grad_kernel,
        grid=(depth // rows,),
        in_specs=[
            pl.BlockSpec((length, rows), lambda i: (0, i)),
            pl.BlockSpec(right.shape, lambda i: (0, 0)),
        ],
        out_specs=pl.BlockSpec((rows * strips, 128), lambda i: (i, 0)),
        out_shape=jax.ShapeDtypeStruct((depth * strips, 128), BF),
        scratch_shapes=[pltpu.VMEM((rows * strips, 128), F32)],
        compiler_params=params_of(),
    )(left, right)


def norm_forward(before, norm_gain, norm_shift):
    centred = before - jnp.mean(before, axis=-1, keepdims=True)
    inv_std = lax.rsqrt(jnp.mean(centred * centred, axis=-1, keepdims=True) + NORM_EPSILON)
    normed = centred * inv_std
    return (normed * norm_gain + norm_shift, normed, inv_std)


def norm_backward(upstream, normed, inv_std, norm_gain):
    scaled = upstream * norm_gain
    centred_grad = (
        scaled
        - jnp.mean(scaled, axis=-1, keepdims=True)
        - normed * jnp.mean(scaled * normed, axis=-1, keepdims=True)
    )
    return (
        centred_grad * inv_std,
        jnp.sum(upstream * normed, axis=0),
        jnp.sum(upstream, axis=0),
    )


def gelu_grad(pre_act):
    return (
        0.5 * (1.0 + lax.erf(pre_act * 0.7071067811865476))
        + pre_act * jnp.exp(-0.5 * pre_act * pre_act) * 0.3989422804014327
    )


def vec_part(vector, slot_index):
    return vector[slot_index * D : (slot_index + 1) * D]


def head_spread():
    return (np.arange(D)[:, None] // HEAD_DIM == np.arange(HEADS)[None, :]).astype(np.float32)


def gate_forward(in_low, weights):
    gate_weight = weights["gate_proj"]
    spread = jnp.asarray(head_spread(), BF)
    columns = jnp.concatenate(
        [jnp.tile(gate_weight[:HEAD_DIM, e], HEADS)[:, None] * spread for e in range(8)], axis=1
    )
    logit = dot_nn(in_low, columns) + jnp.repeat(gate_weight[HEAD_DIM].astype(F32), HEADS)
    parts = [logit[:, e * HEADS : (e + 1) * HEADS] for e in range(8)]
    first = jax.nn.sigmoid(parts[0] + parts[1] + parts[2] + parts[3])
    second = jax.nn.sigmoid(parts[4] + parts[5] + parts[6] + parts[7])
    gate_vals = first * (second * weights["gate_scale"].astype(F32) - 1.0) + 2.0
    return (gate_vals, first, second)


def gate_backward(grad_gate, first, second, in_low, weights):
    scale_vec = weights["gate_scale"].astype(F32)
    grad_scale = jnp.sum(grad_gate * first * second, axis=0)
    grad_one = grad_gate * (second * scale_vec - 1.0) * first * (1.0 - first)
    grad_two = grad_gate * first * scale_vec * second * (1.0 - second)
    both = jnp.concatenate([grad_one, grad_two], axis=1)
    spread = jnp.asarray(head_spread())
    product = lax.dot_general(
        in_low.astype(F32), both, (((0,), (0,)), ((), ())), precision=HIGHEST
    )
    proj_one = jnp.sum((product[:, :HEADS] * spread).reshape(HEADS, HEAD_DIM, HEADS), axis=(0, 2))
    proj_two = jnp.sum((product[:, HEADS:] * spread).reshape(HEADS, HEAD_DIM, HEADS), axis=(0, 2))
    grad_proj = jnp.concatenate(
        [jnp.tile(proj_one[:, None], (1, 4)), jnp.tile(proj_two[:, None], (1, 4))], axis=1
    )
    grad_bias = jnp.concatenate(
        [jnp.full((4,), jnp.sum(grad_one)), jnp.full((4,), jnp.sum(grad_two))]
    )
    gate_weight = weights["gate_proj"][:HEAD_DIM].astype(F32)
    weight_one = jnp.tile(jnp.sum(gate_weight[:, :4], axis=1), HEADS)[:, None] * spread
    weight_two = jnp.tile(jnp.sum(gate_weight[:, 4:], axis=1), HEADS)[:, None] * spread
    grad_heads = lax.dot_general(
        both,
        jnp.concatenate([weight_one, weight_two], axis=1),
        (((1,), (1,)), ((), ())),
        precision=HIGHEST,
    )
    return (grad_heads, jnp.concatenate([grad_proj, grad_bias[None, :]], axis=0), grad_scale)


def layer_forward(hidden, fill, weights, span, pick):
    vector = weights["layer_vec"].astype(F32)
    in_low = hidden.astype(BF)
    qkv_proj = dot_nn(in_low, weights["w_qkv"])
    query_low = ((qkv_proj[:, :D] + vec_part(vector, 0)) * HEAD_DIM ** (-0.5)).astype(BF)
    key_low = qkv_proj[:, D : 2 * D].astype(BF)
    value_low = (qkv_proj[:, 2 * D :] + vec_part(vector, 1)).astype(BF)
    gate_vals, first, second = gate_forward(in_low, weights)
    gate_wide = jnp.pad(gate_vals, ((0, 0), (0, BLOCK - HEADS)))
    attended, lse = attention_forward(query_low, key_low, value_low, gate_wide, span, fill, pick)
    attn_out = dot_nn(attended, weights["w_out"]) + vec_part(vector, 2)
    mid_rows, normed_one, inv_one = norm_forward(
        DEEP_ALPHA * hidden + attn_out, vec_part(vector, 3), vec_part(vector, 4)
    )
    mid_low = mid_rows.astype(BF)
    pre_act = dot_nn(mid_low, weights["w_up"]) + vector[8 * D :]
    act_low = jax.nn.gelu(pre_act, approximate=False).astype(BF)
    ffn_out = dot_nn(act_low, weights["w_down"]) + vec_part(vector, 5)
    final_rows, normed_two, inv_two = norm_forward(
        DEEP_ALPHA * mid_rows + ffn_out, vec_part(vector, 6), vec_part(vector, 7)
    )
    kept = (in_low, query_low, key_low, value_low, gate_wide, first, second, lse, attended)
    kept += (mid_low, pre_act, act_low, normed_one, inv_one, normed_two, inv_two)
    return (final_rows, kept)


def layer_backward(upstream, kept, fill, weights, span, pick):
    in_low, query_low, key_low, value_low, gate_wide, first, second, lse, attended = kept[:9]
    mid_low, pre_act, act_low, normed_one, inv_one, normed_two, inv_two = kept[9:]
    vector = weights["layer_vec"].astype(F32)
    grad_res_two, grad_gain_two, grad_shift_two = norm_backward(
        upstream, normed_two, inv_two, vec_part(vector, 6)
    )
    ffn_low = grad_res_two.astype(BF)
    grad_down = weight_grad(act_low, ffn_low, 384)
    grad_pre = dot_nt(ffn_low, weights["w_down"]) * gelu_grad(pre_act)
    pre_low = grad_pre.astype(BF)
    grad_up = weight_grad(mid_low, pre_low)
    grad_mid = DEEP_ALPHA * grad_res_two + dot_nt(pre_low, weights["w_up"])
    grad_res_one, grad_gain_one, grad_shift_one = norm_backward(
        grad_mid, normed_one, inv_one, vec_part(vector, 3)
    )
    out_low = grad_res_one.astype(BF)
    grad_out = weight_grad(attended, out_low)
    grad_att = dot_nt(out_low, weights["w_out"]).astype(BF)
    parts, part_sums, grad_gate, grad_span = attention_backward(
        query_low, key_low, value_low, grad_att, gate_wide, span, fill, lse, pick
    )
    grad_heads, grad_gate_proj, grad_gate_scale = gate_backward(
        grad_gate[:, :HEADS], first, second, in_low, weights
    )
    proj_low = jnp.concatenate([parts[0], parts[1], parts[2]], axis=1)
    grad_qkv = weight_grad(in_low, proj_low)
    grad_hidden = DEEP_ALPHA * grad_res_one + dot_nt(proj_low, weights["w_qkv"]) + grad_heads
    grad_vec = jnp.concatenate(
        [
            part_sums[0],
            part_sums[1],
            jnp.sum(grad_res_one, axis=0),
            grad_gain_one,
            grad_shift_one,
            jnp.sum(grad_res_two, axis=0),
            grad_gain_two,
            grad_shift_two,
            jnp.sum(grad_pre, axis=0),
        ]
    )
    grad_map = {
        "w_qkv": grad_qkv,
        "w_out": grad_out,
        "w_up": grad_up,
        "w_down": grad_down,
        "layer_vec": grad_vec,
        "gate_proj": grad_gate_proj,
        "gate_scale": grad_gate_scale,
    }
    return (grad_hidden, grad_map, grad_span)


def head_pass(hidden, w_head, codebook, target_codes):
    row_low = hidden.astype(BF)
    projected = dot_nn(row_low, w_head)
    inv_len = lax.rsqrt(jnp.sum(projected * projected, axis=-1, keepdims=True) + UNIT_EPSILON)
    unit_rows = projected * inv_len
    live_rows = (target_codes >= 0).astype(F32)[:, None]
    logits = LOGIT_SCALE * dot_nt(unit_rows.astype(BF), codebook)
    codes = lax.broadcasted_iota(jnp.int32, (1, codebook.shape[0]), 1)
    hits = (target_codes[:, None] == codes).astype(F32)
    top = jnp.max(logits, axis=1, keepdims=True)
    log_total = top + jnp.log(jnp.sum(jnp.exp(logits - top), axis=1, keepdims=True))
    picked = jnp.sum(logits * hits, axis=1, keepdims=True)
    loss_local = jnp.sum((log_total - picked) * live_rows)
    grad_logits = ((jnp.exp(logits - log_total) - hits) * live_rows * LOGIT_SCALE).astype(BF)
    grad_unit = dot_nn(grad_logits, codebook)
    grad_proj = (
        grad_unit - unit_rows * jnp.sum(unit_rows * grad_unit, axis=-1, keepdims=True)
    ) * inv_len
    proj_low = grad_proj.astype(BF)
    grad_head = dot_tn(row_low, proj_low)
    grad_rows = dot_nt(proj_low, w_head)
    return (loss_local, grad_rows, grad_head)


def local(
    patches,
    lengths,
    patch_masks,
    targets,
    codebook,
    params,
    first_moment,
    second_moment,
    step_count,
):
    dp_count = lax.axis_size("dp")
    code_count = lax.axis_size("code")
    code_index = lax.axis_index("code")
    shard_len = params.shape[0]
    shard_rows = shard_len // 128
    own_low = params.astype(BF).reshape(shard_rows, 128)
    full_low = lax.all_gather(own_low, ("dp", "code"), axis=0, tiled=False)
    flat = full_low.reshape(-1, 128)
    all_codes = lax.all_gather(codebook, "code", axis=0, tiled=True)
    where = starts()

    def piece(seg_name, index=0, count=None):
        extent = dict(layout())[seg_name]
        if count is None:
            amount, shape = math.prod(extent), (-1, extent[-1])
        else:
            amount, shape = math.prod(extent[1:]), (-1, extent[-1])
        begin = where[seg_name] + index * amount
        return flat[begin // 128 : (begin + amount) // 128].reshape(shape)

    tail_row = where["gate_proj"] // 128
    tail = flat[tail_row : tail_row + 2048].reshape(-1)

    def tail_piece(seg_name):
        extent = dict(layout())[seg_name]
        begin = where[seg_name] - tail_row * 128
        return tail[begin : begin + math.prod(extent)].reshape(extent)

    w_patch = piece("w_patch")
    glob_vec = piece("glob_vec").astype(F32)
    gate_proj = tail_piece("gate_proj")
    gate_scale = tail_piece("gate_scale")
    rel_table = tail_piece("rel_table")
    w_head = tail_piece("w_head")
    vec_row = where["layer_vec"] // 128
    vec_len = 8 * D + FF
    layer_vec = flat[vec_row : vec_row + LAYERS * vec_len // 128].reshape(LAYERS, vec_len)
    weights = [
        {
            "w_qkv": piece("w_qkv", index, True),
            "w_out": piece("w_out", index, True),
            "w_up": piece("w_up", index, True),
            "w_down": piece("w_down", index, True),
            "layer_vec": layer_vec[index],
            "gate_proj": gate_proj[index],
            "gate_scale": gate_scale[index],
        }
        for index in range(LAYERS)
    ]

    places = jnp.arange(ROWS, dtype=jnp.int32)
    mask_row = jnp.pad(patch_masks[0], (0, ROWS - LONG))
    live_slot = places < jnp.minimum(lengths[0], LONG)
    visible = live_slot & (mask_row == 0)
    rank = jnp.cumsum(visible.astype(jnp.int32)) - 1
    pick = (
        visible[None, :] & (rank[None, :] == jnp.arange(SEEN, dtype=jnp.int32)[:, None])
    )
    pick_low = pick.astype(BF)
    pick_full = pick.astype(F32)
    seen_valid = jnp.arange(SEEN, dtype=jnp.int32) < lengths[0] // 4
    seen_fill = jnp.where(seen_valid, 0.0, MASK_FILL)[None, :]
    live_fill = jnp.where(live_slot, 0.0, MASK_FILL)[None, :]
    live_float = live_slot.astype(F32)[:, None]
    span_table = jnp.asarray(span_onehot())
    span = jnp.pad(
        lax.dot_general(
            rel_table.astype(F32), span_table, (((0,), (1,)), ((), ())), precision=HIGHEST
        ),
        ((0, 16 - HEADS), (0, 0)),
    )

    patch_rows = jnp.pad(patches[0], ((0, ROWS - LONG), (0, 0)))
    embedded = dot_nn(patch_rows, w_patch)
    normed_rows, normed_zero, inv_zero = norm_forward(embedded, glob_vec[0], glob_vec[1])
    start_rows = normed_rows * live_float
    conv_in = start_rows.astype(BF)
    width = D // code_count
    own_cols = code_index * width
    conv_weight = lax.dynamic_slice_in_dim(piece("conv_w"), own_cols, width, 1)
    own_in = lax.dynamic_slice_in_dim(conv_in, own_cols, width, 1)
    half = KERNEL // 2
    conv_own = conv_call(conv_forward_kernel, own_in[:LONG], conv_weight, half, False)
    seen_own = lax.dot_general(
        pick_full, conv_own, (((1,), (0,)), ((), ())), precision=HIGHEST
    )
    seen_raw = jnp.transpose(lax.all_gather(seen_own, "code", axis=0), (1, 0, 2)).reshape(SEEN, D)
    seen_pre = seen_raw + glob_vec[2]
    seen_start = lax.dot_general(
        pick_full, start_rows, (((1,), (0,)), ((), ())), precision=HIGHEST
    )
    seen_rows = seen_start + jax.nn.gelu(seen_pre, approximate=False)
    encoded, kept_first = layer_forward(seen_rows, seen_fill, weights[0], span, pick_low)
    placed = lax.dot_general(
        pick_full, encoded, (((0,), (0,)), ((), ())), precision=HIGHEST
    )
    hidden = jnp.where(visible[:, None], placed, glob_vec[3])
    final, kept_second = layer_forward(hidden, live_fill, weights[1], span, None)
    target_codes = jnp.where(mask_row == 1, jnp.pad(targets[0], (0, ROWS - LONG)), -1)
    loss_local, upstream, grad_head = head_pass(final, w_head, all_codes, target_codes)

    upstream, map_second, span_second = layer_backward(
        upstream, kept_second, live_fill, weights[1], span, None
    )
    grad_mask_emb = jnp.sum(jnp.where(visible[:, None], 0.0, upstream), axis=0)
    grad_encoded = lax.dot_general(
        pick_full, upstream, (((1,), (0,)), ((), ())), precision=HIGHEST
    )
    grad_seen, map_first, span_first = layer_backward(
        grad_encoded, kept_first, seen_fill, weights[0], span, pick_low
    )
    grad_seen = grad_seen * seen_valid[:, None].astype(F32)
    grad_conv_seen = grad_seen * gelu_grad(seen_pre)
    grad_conv = dot_tn(pick_low, grad_conv_seen.astype(BF)).astype(BF)
    grad_full = lax.dot_general(
        pick_full, grad_seen, (((0,), (0,)), ((), ())), precision=HIGHEST
    )
    grad_kernel = conv_weight_grad(conv_in[:LONG], grad_conv)
    own_grad = lax.dynamic_slice_in_dim(grad_conv, own_cols, width, 1)
    grad_in_own = conv_call(conv_input_kernel, own_grad[:LONG], conv_weight, half - 1, True)
    grad_conv_in = jnp.transpose(
        lax.all_gather(grad_in_own.astype(BF), "code", axis=0), (1, 0, 2)
    ).reshape(ROWS, D)
    grad_start = (grad_full + grad_conv_in.astype(F32)) * live_float
    grad_embedded, grad_gain_zero, grad_shift_zero = norm_backward(
        grad_start, normed_zero, inv_zero, glob_vec[0]
    )
    grad_patch = dot_tn(patch_rows, grad_embedded.astype(BF))
    grad_glob = jnp.stack(
        [grad_gain_zero, grad_shift_zero, jnp.sum(grad_conv_seen, axis=0), grad_mask_emb]
    )
    grad_rel = lax.dot_general(
        span_table, (span_first + span_second)[:HEADS], (((0,), (1,)), ((), ())), precision=HIGHEST
    )
    both = (map_first, map_second)
    pieces = [grad_patch.astype(BF).reshape(-1, 128), grad_glob.astype(BF).reshape(-1, 128)]
    pieces.append(grad_kernel.reshape(-1, 128))
    for seg_name in ("w_qkv", "w_out", "w_up", "w_down"):
        pieces += [layer_map[seg_name] for layer_map in both]
    tail_parts = []
    for seg_name in ("layer_vec", "gate_proj", "gate_scale"):
        tail_parts += [layer_map[seg_name].reshape(-1) for layer_map in both]
    tail_grad = jnp.concatenate(tail_parts + [grad_rel.reshape(-1), grad_head.reshape(-1)])
    tail_rows = shard_rows * dp_count * code_count - vec_row
    tail_grad = jnp.pad(tail_grad, (0, tail_rows * 128 - tail_grad.shape[0])).astype(BF)
    pieces.append(tail_grad.reshape(-1, 128))
    flat_grad = jnp.concatenate(pieces, axis=0)
    arranged = flat_grad.reshape(dp_count, code_count, shard_rows, 128)
    own_part = lax.dynamic_index_in_dim(arranged, code_index, 1, False)
    reduced = (
        lax.psum_scatter(own_part, "dp", scatter_dimension=0, tiled=False)
        .astype(F32)
        .reshape(shard_len)
    )
    leader = (code_index == 0).astype(F32)
    count_local = jnp.sum((target_codes >= 0).astype(F32))
    loss_all, squares_all, count_all, rel_all = lax.psum(
        (
            loss_local * leader,
            jnp.sum(reduced * reduced),
            count_local * leader,
            grad_rel * leader,
        ),
        ("dp", "code"),
    )
    grad_norm = jnp.sqrt(squares_all) / count_all
    clip_factor = jnp.minimum(1.0, CLIP_NORM / grad_norm)
    clipped = reduced / count_all * clip_factor
    rel_grad = rel_all / count_all * clip_factor
    step_value = step_count[0].astype(F32)
    new_first = BETA_ONE * first_moment + (1.0 - BETA_ONE) * clipped
    new_second = BETA_TWO * second_moment + (1.0 - BETA_TWO) * clipped * clipped
    first_hat = new_first / (1.0 - BETA_ONE**step_value)
    second_hat = new_second / (1.0 - BETA_TWO**step_value)
    new_params = params - LEARN_RATE * (
        first_hat / (jnp.sqrt(second_hat) + ADAM_EPSILON) + WEIGHT_DECAY * params
    )
    return (
        new_params,
        new_first,
        new_second,
        new_params.astype(BF),
        loss_all / count_all,
        grad_norm,
        rel_grad,
    )


def solution(mesh):
    placed = (
        P("dp", None, None),
        P("dp"),
        P("dp", None),
        P("dp", None),
        P("code", None),
        P(("dp", "code")),
        P(("dp", "code")),
        P(("dp", "code")),
        P(),
    )
    return jax.shard_map(
        local,
        mesh=mesh,
        in_specs=placed,
        out_specs=(
            P(("dp", "code")),
            P(("dp", "code")),
            P(("dp", "code")),
            P(("dp", "code")),
            P(),
            P(),
            P(),
        ),
        check_vma=False,
    )
```

```python
import functools
import math

import jax
import jax.numpy as jnp
import numpy as np
from jax import lax
from jax.experimental import pallas as pl
from jax.experimental.pallas import tpu as pltpu
from jax.sharding import PartitionSpec as P

D = 768
HEADS = 12
HEAD_DIM = 64
FF = 3072
PATCH_IN = 256
PROJ = 256
KERNEL = 128
GROUPS = 16
WIDTH = D // GROUPS
BUCKETS = 320
MAX_DIST = 800
LAYERS = 2
LONG = 496
VISIBLE = 124
ROWS = 512
SEEN = 128
SPAN = 1024

NORM_EPSILON = 1e-05
UNIT_EPSILON = 1e-06
DEEP_ALPHA = 2.2133638394006434
LOGIT_SCALE = 25.0
CLIP_NORM = 0.005
LEARN_RATE = 0.02
BETA_ONE = 0.9
BETA_TWO = 0.999
ADAM_EPSILON = 1e-10
WEIGHT_DECAY = 0.01
MASK_FILL = -1000000000.0
HIGHEST = lax.Precision.HIGHEST
BF = jnp.bfloat16
F32 = jnp.float32
VMEM_LIMIT = 56 << 20


def layout():
    return [
        ("w_patch", (PATCH_IN, D)),
        ("glob_vec", (4, D)),
        ("conv_w", (KERNEL, WIDTH, D)),
        ("w_qkv", (LAYERS, D, 3 * D)),
        ("w_out", (LAYERS, D, D)),
        ("w_up", (LAYERS, D, FF)),
        ("w_down", (LAYERS, FF, D)),
        ("layer_vec", (LAYERS, 8 * D + FF)),
        ("gate_proj", (LAYERS, HEAD_DIM + 1, 8)),
        ("gate_scale", (LAYERS, HEADS)),
        ("rel_table", (BUCKETS, HEADS)),
        ("w_head", (D, PROJ)),
    ]


def starts():
    where = {}
    offset = 0
    for seg_name, extent in layout():
        where[seg_name] = offset
        offset += math.prod(extent)
    return where


TILE = 16


class Geometry:
    def __init__(self, dp_count, code_count, shard_rows):
        self.dp_count, self.code_count, self.shard_rows = dp_count, code_count, shard_rows
        self.shards = dp_count * code_count
        self.phase = -(starts()["conv_w"] // 128) % TILE
        self.window = -(-(shard_rows + TILE - 1) // TILE) * TILE
        self.begins = [(shard_rows * s + self.phase) // TILE * TILE for s in range(self.shards)]
        self.offsets = [(shard_rows * s + self.phase) % TILE for s in range(self.shards)]

    def place(self, seg_name, index=0):
        extent = dict(layout())[seg_name]
        amount = math.prod(extent[1:]) if index else 0
        return (starts()[seg_name] + index * amount) // 128 + self.phase

    def pieces(self, low, high):
        main, edges = [], []
        row = low
        while row < high:
            shard = max(s for s in range(self.shards) if self.begins[s] <= row)
            begin = self.begins[shard]
            if row == begin and shard > 0 and self.offsets[shard]:
                main.append((shard - 1, row - self.begins[shard - 1], row - low, TILE))
                edges.append((shard, row - low))
                row += TILE
                continue
            stop = self.begins[shard + 1] if shard + 1 < self.shards else high
            count = min(stop, high) - row
            main.append((shard, row - begin, row - low, count))
            row += count
        merged = []
        for item in main:
            last = merged[-1] if merged else None
            if last and last[0] == item[0] and last[1] + last[3] == item[1]:
                merged[-1] = last[:3] + (last[3] + item[3],)
            else:
                merged.append(item)
        return merged, edges

    def exact(self, windows, low, high):
        parts = []
        row = low
        while row < high:
            shard = row // self.shard_rows
            stop = min(high, (shard + 1) * self.shard_rows)
            begin = self.offsets[shard] + row - shard * self.shard_rows
            parts.append(windows[shard, begin : begin + stop - row])
            row = stop
        return parts[0] if len(parts) == 1 else jnp.concatenate(parts, axis=0)


def bucket_onehot():
    offsets = np.arange(-(LONG - 1), LONG)
    half_count = BUCKETS // 2
    exact_count = half_count // 2
    distance = np.abs(offsets)
    scaled = (
        np.log(np.maximum(distance, 1) / exact_count)
        / np.log(MAX_DIST / exact_count)
        * (half_count - exact_count)
    )
    larger = np.minimum(exact_count + np.maximum(scaled, 0.0).astype(np.int64), half_count - 1)
    bucket = (offsets > 0) * half_count + np.where(distance < exact_count, distance, larger)
    return (bucket[:, None] == np.arange(BUCKETS)[None, :]).astype(np.float32)


def span_onehot():
    shift = SPAN // 2 - (LONG - 1)
    table = np.zeros((SPAN, BUCKETS), np.float32)
    table[shift : shift + 2 * LONG - 1] = bucket_onehot()[::-1]
    return table


def params_of(grid_rank=1):
    return pltpu.CompilerParams(
        dimension_semantics=("arbitrary",) * grid_rank, vmem_limit_bytes=VMEM_LIMIT
    )


def dot_nn(left, right):
    return lax.dot_general(left, right, (((1,), (0,)), ((), ())), preferred_element_type=F32)


def dot_nt(left, right):
    return lax.dot_general(left, right, (((1,), (1,)), ((), ())), preferred_element_type=F32)


def dot_tn(left, right):
    return lax.dot_general(left, right, (((0,), (0,)), ((), ())), preferred_element_type=F32)


TAPS = 16


def lane_masks(width):
    group = np.arange(width)[None, :] // WIDTH
    return (group == np.arange(width // WIDTH)[:, None]).astype(np.float32)


def shifted_taps(source_ref, target_ref, count):
    width = source_ref.shape[1]
    for tap in range(TAPS):
        target_ref[:, tap * width : (tap + 1) * width] = source_ref[tap : tap + count, :].astype(BF)


def conv_forward_kernel(in_ref, weight_ref, mask_ref, out_ref, taps_ref, block_ref):
    step = pl.program_id(0)
    width = weight_ref.shape[1]

    @pl.when(step == 0)
    def _():
        shifted_taps(in_ref, taps_ref, taps_ref.shape[0])
        block_ref[...] = jnp.zeros_like(block_ref)

    for tap in range(TAPS):
        piece = weight_ref[tap * WIDTH : (tap + 1) * WIDTH, :]
        for group in range(width // WIDTH):
            low = tap * width + group * WIDTH
            block_ref[low : low + WIDTH, :] = piece * mask_ref[group : group + 1, :]
    begin = pl.multiple_of(step * TAPS, TAPS)
    term = dot_nn(taps_ref[pl.ds(begin, ROWS), :], block_ref[...])

    @pl.when(step == 0)
    def _():
        out_ref[...] = term

    @pl.when(step > 0)
    def _():
        out_ref[...] += term


def conv_input_kernel(in_ref, weight_ref, mask_ref, out_ref, taps_ref, block_ref):
    step = pl.program_id(0)
    width = weight_ref.shape[1]

    @pl.when(step == 0)
    def _():
        shifted_taps(in_ref, taps_ref, taps_ref.shape[0])
        block_ref[...] = jnp.zeros_like(block_ref)

    for tap in range(TAPS):
        piece = weight_ref[tap * WIDTH : (tap + 1) * WIDTH, :]
        low = (TAPS - 1 - tap) * width
        for group in range(width // WIDTH):
            block_ref[group * WIDTH : (group + 1) * WIDTH, low : low + width] = (
                piece * mask_ref[group : group + 1, :]
            )
    begin = pl.multiple_of((pl.num_programs(0) - 1 - step) * TAPS, TAPS)
    term = dot_nt(taps_ref[pl.ds(begin, ROWS), :], block_ref[...])

    @pl.when(step == 0)
    def _():
        out_ref[...] = term

    @pl.when(step > 0)
    def _():
        out_ref[...] += term


def conv_call(kernel, conv_in, weight, front, nt):
    width = weight.shape[1]
    steps = KERNEL // TAPS
    count = ROWS + KERNEL - TAPS
    padded = jnp.pad(
        conv_in.astype(F32),
        ((front, count + TAPS - front - conv_in.shape[0]), (0, 0)),
    )
    block = (width, TAPS * width) if nt else (TAPS * width, width)
    return pl.pallas_call(
        kernel,
        grid=(steps,),
        in_specs=[
            pl.BlockSpec(padded.shape, lambda i: (0, 0)),
            pl.BlockSpec((TAPS * WIDTH, width), lambda i: (i, 0)),
            pl.BlockSpec((width // WIDTH, width), lambda i: (0, 0)),
        ],
        out_specs=pl.BlockSpec((ROWS, width), lambda i: (0, 0)),
        out_shape=jax.ShapeDtypeStruct((ROWS, width), F32),
        scratch_shapes=[pltpu.VMEM((count, TAPS * width), BF), pltpu.VMEM(block, BF)],
        compiler_params=params_of(),
    )(padded, weight, jnp.asarray(lane_masks(width), BF))


CHUNK = 6


def conv_weight_kernel(tap_ref, in_ref, grad_ref, mask_ref, out_ref, taps_ref, turn_ref):
    parts = in_ref.shape[0]
    begin = tap_ref[pl.program_id(0)]
    strips = D // 128
    rows = CHUNK * WIDTH
    for part in range(parts):
        turned = pltpu.roll(in_ref[part], in_ref.shape[2] - begin, 1)
        for tap in range(CHUNK):
            taps_ref[part, tap * PART : (tap + 1) * PART, :] = turned[:, tap : tap + ROWS].astype(
                BF
            )
    sums = []
    for part in range(parts):
        term = dot_nn(taps_ref[part], grad_ref[part])
        pieces = []
        for tap in range(CHUNK):
            total = None
            for group in range(mask_ref.shape[0]):
                low = tap * PART + group * WIDTH
                piece = term[low : low + WIDTH, :] * mask_ref[group : group + 1, :]
                total = piece if total is None else total + piece
            pieces.append(total)
        sums.append(jnp.concatenate(pieces, axis=0))
    for strip in range(strips):
        part, low = divmod(strip * 128, PART)
        columns = sums[part][:, low : min(low + 128, PART)]
        if low + 128 > PART:
            columns = jnp.concatenate([columns, sums[part + 1][:, : low + 128 - PART]], axis=1)
        turn_ref[pl.ds(strip, rows, stride=strips), :] = columns
    out_ref[...] = turn_ref[...].astype(BF)


PART = 4 * WIDTH


def conv_chunks(geometry):
    base, tap_rows = geometry.place("conv_w"), WIDTH * D // 128
    tables = []
    for slot in range(geometry.dp_count):
        needs = []
        for code in range(geometry.code_count):
            begin = geometry.begins[slot * geometry.code_count + code] - base
            low = max(begin // tap_rows, 0)
            high = min(-(-(begin + geometry.window) // tap_rows), KERNEL)
            needs.append((low, high))
        count = max(-(-(high - low) // CHUNK) for low, high in needs)
        for number in range(max(count, 0)):
            tables.append(
                [min(max(low, 0), KERNEL) + number * CHUNK for low, _ in needs]
            )
    clipped = [[min(tap, KERNEL - CHUNK) for tap in row] for row in tables]
    return [list(column) for column in zip(*clipped)]


def conv_weight_grad(conv_in, grad_low, geometry, code_index):
    parts = D // PART
    front = KERNEL // 2
    padded = jnp.pad(
        jnp.transpose(conv_in).astype(F32),
        ((0, 0), (front, ROWS + KERNEL - front - conv_in.shape[0])),
    ).reshape(parts, PART, ROWS + KERNEL)
    grads = jnp.transpose(grad_low.reshape(ROWS, parts, PART), (1, 0, 2))
    masks = jnp.asarray(lane_masks(PART), F32)
    chunks = conv_chunks(geometry)
    table = lax.dynamic_index_in_dim(jnp.asarray(chunks, jnp.int32), code_index, 0, False)
    rows = CHUNK * WIDTH * D // 128
    out = pl.pallas_call(
        conv_weight_kernel,
        grid_spec=pltpu.PrefetchScalarGridSpec(
            num_scalar_prefetch=1,
            grid=(len(chunks[0]),),
            in_specs=[
                pl.BlockSpec(padded.shape, lambda i, t: (0, 0, 0)),
                pl.BlockSpec(grads.shape, lambda i, t: (0, 0, 0)),
                pl.BlockSpec(masks.shape, lambda i, t: (0, 0)),
            ],
            out_specs=pl.BlockSpec((rows, 128), lambda i, t: (i, 0)),
            scratch_shapes=[
                pltpu.VMEM((parts, CHUNK * PART, ROWS), BF),
                pltpu.VMEM((rows, 128), F32),
            ],
        ),
        out_shape=jax.ShapeDtypeStruct((len(chunks[0]) * rows, 128), BF),
        compiler_params=params_of(),
    )(table, padded, grads, masks)
    return out, chunks


BLOCK = 128


def half_mask(side):
    lane = lax.broadcasted_iota(jnp.int32, (1, BLOCK), 1)
    return jnp.where(lane // HEAD_DIM == side, 1.0, 0.0).astype(BF)


def toeplitz(span_ref, head):
    row = jnp.broadcast_to(span_ref[pl.ds(head, 1), :], (BLOCK, SPAN))
    return pltpu.roll(row, 0, 1, stride=1, stride_axis=0)


def hop_columns(hop):
    return [hop[:, index : index + 1] for index in range(ROWS // BLOCK)]


def seen_biases(turned, pick, near, hop):
    moved = [dot_nn(near, item.astype(BF)) for item in turned]
    columns = [jnp.broadcast_to(column, (SEEN, ROWS)) for column in hop_columns(hop)]
    tables = []
    for item in moved:
        table = None
        for index, column in enumerate(columns):
            low = index * BLOCK
            part = column * item[:, ROWS - low : SPAN - low]
            table = part if table is None else table + part
        tables.append(table.astype(BF))
    return [dot_nt(table, pick) for table in tables]


def wide(column, length):
    return jnp.concatenate([column] * (length // BLOCK), axis=1)


def attention_forward_kernel(
    q_ref, k_ref, v_ref, gate_ref, span_ref, fill_ref, out_ref, lse_ref, score_ref, turn_ref
):
    step = pl.program_id(0)
    length = q_ref.shape[0]
    values = jnp.transpose(v_ref[...])
    sides = range(2)
    turned = [toeplitz(span_ref, step * 2 + side) for side in sides]
    for side in sides:
        score_ref[side] = dot_nt(k_ref[...] * half_mask(side), q_ref[...])
    tops = []
    for side in sides:
        gate = gate_ref[pl.ds(step * 2 + side, 1), :]
        top = None
        for low in range(0, length, BLOCK):
            rows = slice(low, low + BLOCK)
            bias = turned[side][:, ROWS - low : SPAN - low]
            scores = score_ref[side, rows, :] + gate * bias + wide(fill_ref[rows, :], length)
            score_ref[side, rows, :] = scores
            most = jnp.max(scores, axis=0, keepdims=True)
            top = most if top is None else jnp.maximum(top, most)
        tops.append(top)
    totals = []
    for side in sides:
        total = None
        for low in range(0, length, BLOCK):
            rows = slice(low, low + BLOCK)
            weights = jnp.exp(score_ref[side, rows, :] - tops[side])
            part = jnp.sum(weights, axis=0, keepdims=True)
            total = part if total is None else total + part
            turn_ref[side, rows, :] = weights.astype(BF)
        totals.append(total)
    mixed = []
    for side in sides:
        lse_ref[pl.ds(step * 2 + side, 1), :] = tops[side] + jnp.log(totals[side])
        part = dot_nn(values[side * HEAD_DIM : (side + 1) * HEAD_DIM, :], turn_ref[side])
        mixed.append(part * (1.0 / totals[side]))
    out_ref[...] = jnp.transpose(jnp.concatenate(mixed, axis=0)).astype(BF)


SEEN_HEADS = 12


def seen_forward_kernel(
    q_ref, k_ref, v_ref, gate_ref, span_ref, fill_ref, pick_ref, near_ref, hop_ref,
    out_ref, lse_ref, bias_ref,
):
    heads = range(SEEN_HEADS)
    base = pl.program_id(0) * SEEN_HEADS
    pick, near, hop = pick_ref[...], near_ref[...], hop_ref[...]
    pairs = range(SEEN_HEADS // 2)
    query = [q_ref[:, pair * BLOCK : (pair + 1) * BLOCK] for pair in pairs]
    keyv = [k_ref[:, pair * BLOCK : (pair + 1) * BLOCK] for pair in pairs]
    values = [jnp.transpose(v_ref[:, pair * BLOCK : (pair + 1) * BLOCK]) for pair in pairs]
    turned = [toeplitz(span_ref, base + head) for head in heads]
    bias = seen_biases(turned, pick, near, hop)
    scores = [dot_nt(keyv[head // 2] * half_mask(head % 2), query[head // 2]) for head in heads]
    for head in heads:
        bias_ref[head * BLOCK : (head + 1) * BLOCK, :] = bias[head].astype(BF)
    scores = [
        scores[head] + gate_ref[pl.ds(base + head, 1), :] * bias[head] + fill_ref[...]
        for head in heads
    ]
    tops = [jnp.max(item, axis=0, keepdims=True) for item in scores]
    weights = [jnp.exp(scores[head] - tops[head]) for head in heads]
    totals = [jnp.sum(item, axis=0, keepdims=True) for item in weights]
    mixed = []
    for head in heads:
        lse_ref[pl.ds(base + head, 1), :] = tops[head] + jnp.log(totals[head])
        low = (head % 2) * HEAD_DIM
        part = dot_nn(values[head // 2][low : low + HEAD_DIM, :], weights[head].astype(BF))
        mixed.append(part * (1.0 / totals[head]))
    for pair in pairs:
        both = jnp.concatenate(mixed[2 * pair : 2 * pair + 2], axis=0)
        out_ref[:, pair * BLOCK : (pair + 1) * BLOCK] = jnp.transpose(both).astype(BF)


def pair_spec(length):
    return pl.BlockSpec((length, 2 * HEAD_DIM), lambda i: (0, i))


def whole_spec(shape):
    return pl.BlockSpec(shape, lambda i: (0,) * len(shape))


def attention_forward(query, keyv, value, gate, span, fill, pick):
    length = query.shape[0]
    args = [query, keyv, value, gate, span, fill] + list(pick or ())
    shapes = [
        jax.ShapeDtypeStruct((length, D), BF),
        jax.ShapeDtypeStruct((16, length), F32),
    ]
    if pick is None:
        found = pl.pallas_call(
            attention_forward_kernel,
            grid=(HEADS // 2,),
            in_specs=[pair_spec(length)] * 3 + [whole_spec(a.shape) for a in args[3:]],
            out_specs=[pair_spec(length), whole_spec((16, length))],
            out_shape=shapes,
            scratch_shapes=[
                pltpu.VMEM((2, length, length), F32),
                pltpu.VMEM((2, length, length), BF),
            ],
            compiler_params=params_of(),
        )(*args)
        return found[0], found[1], None
    columns = pl.BlockSpec((length, SEEN_HEADS * HEAD_DIM), lambda i: (0, i))
    return pl.pallas_call(
        seen_forward_kernel,
        grid=(HEADS // SEEN_HEADS,),
        in_specs=[columns] * 3 + [whole_spec(a.shape) for a in args[3:]],
        out_specs=[
            columns,
            whole_spec((16, length)),
            pl.BlockSpec((SEEN_HEADS * BLOCK, BLOCK), lambda i: (i, 0)),
        ],
        out_shape=shapes + [jax.ShapeDtypeStruct((HEADS * BLOCK, BLOCK), BF)],
        compiler_params=params_of(),
    )(*args)


def diagonal_sums(turn):
    half = BLOCK // 2
    while half:
        turn = turn[:half, :] + pltpu.roll(turn[half:, :], SPAN - half, 1)
        half //= 2
    return turn


def attention_backward_kernel(
    q_ref, k_ref, v_ref, up_ref, gate_ref, span_ref, fill_ref, lse_ref,
    out_ref, sum_ref, dgate_ref, dspan_ref, prob_ref, grad_ref, turn_ref, low_ref, diag_ref,
):
    step = pl.program_id(0)
    length = q_ref.shape[0]
    sides = range(2)

    @pl.when(step == 0)
    def _():
        dspan_ref[...] = jnp.zeros_like(dspan_ref)
        dgate_ref[...] = jnp.zeros_like(dgate_ref)

    keys = jnp.transpose(k_ref[...])
    turned = [toeplitz(span_ref, step * 2 + side) for side in sides]
    for side in sides:
        prob_ref[side] = dot_nt(k_ref[...] * half_mask(side), q_ref[...])
        grad_ref[side] = dot_nt(v_ref[...] * half_mask(side), up_ref[...])
        diag_ref[side] = jnp.zeros_like(diag_ref[side])
    shared = []
    for side in sides:
        gate = gate_ref[pl.ds(step * 2 + side, 1), :]
        lse = lse_ref[pl.ds(step * 2 + side, 1), :]
        total = None
        for low in range(0, length, BLOCK):
            rows = slice(low, low + BLOCK)
            bias = turned[side][:, ROWS - low : SPAN - low]
            scores = prob_ref[side, rows, :] + gate * bias + wide(fill_ref[rows, :], length)
            probs = jnp.exp(scores - lse)
            prob_ref[side, rows, :] = probs
            low_ref[side, rows, :] = probs.astype(BF)
            part = jnp.sum(probs * grad_ref[side, rows, :], axis=0, keepdims=True)
            total = part if total is None else total + part
        shared.append(total)
    val_total = sum(dot_nn(low_ref[side], up_ref[...] * half_mask(side)) for side in sides)
    for side in sides:
        gate = gate_ref[pl.ds(step * 2 + side, 1), :]
        dgate = None
        for low in range(0, length, BLOCK):
            rows = slice(low, low + BLOCK)
            bias = turned[side][:, ROWS - low : SPAN - low]
            grad_scores = prob_ref[side, rows, :] * (grad_ref[side, rows, :] - shared[side])
            turn_ref[side, rows, :] = grad_scores.astype(BF)
            part = jnp.sum(grad_scores * bias, axis=0, keepdims=True)
            dgate = part if dgate is None else dgate + part
            diag_ref[side, :, ROWS - low : SPAN - low] += grad_scores * gate
        dgate_ref[pl.ds(step * 2 + side, 1), :] = dgate
    key_total = sum(dot_nn(turn_ref[side], q_ref[...] * half_mask(side)) for side in sides)
    halves = [
        dot_nn(keys[side * HEAD_DIM : (side + 1) * HEAD_DIM, :], turn_ref[side]) for side in sides
    ]
    for side in sides:
        dspan_ref[pl.ds(step * 2 + side, 1), :] = diagonal_sums(diag_ref[side])
    grad_query = jnp.transpose(jnp.concatenate(halves, axis=0)) * HEAD_DIM ** (-0.5)
    out_ref[0] = grad_query.astype(BF)
    out_ref[1] = key_total.astype(BF)
    out_ref[2] = val_total.astype(BF)
    sum_ref[0:1, :] = jnp.sum(grad_query, axis=0, keepdims=True)
    sum_ref[1:2, :] = jnp.sum(val_total, axis=0, keepdims=True)


def split_low(value):
    high = value.astype(BF)
    return high, (value - high.astype(F32)).astype(BF)


def seen_backward_kernel(
    q_ref, k_ref, v_ref, up_ref, gate_ref, fill_ref, lse_ref, pick_ref, hop_ref, flip_ref,
    bias_ref, out_ref, sum_ref, dgate_ref, dspan_ref, diag_ref,
):
    heads, pairs = range(SEEN_HEADS), range(SEEN_HEADS // 2)
    base = pl.program_id(0) * SEEN_HEADS

    @pl.when(base == 0)
    def _():
        dspan_ref[...] = jnp.zeros_like(dspan_ref)
        dgate_ref[...] = jnp.zeros_like(dgate_ref)

    def pair_of(ref):
        return [ref[:, pair * BLOCK : (pair + 1) * BLOCK] for pair in pairs]

    query, keyv, value, upstream = (pair_of(ref) for ref in (q_ref, k_ref, v_ref, up_ref))
    keys = [jnp.transpose(item) for item in keyv]
    gate = [gate_ref[pl.ds(base + head, 1), :] for head in heads]
    bias = [bias_ref[head * BLOCK : (head + 1) * BLOCK, :].astype(F32) for head in heads]
    scores = [dot_nt(keyv[head // 2] * half_mask(head % 2), query[head // 2]) for head in heads]
    grads = [dot_nt(value[head // 2] * half_mask(head % 2), upstream[head // 2]) for head in heads]
    probs = [
        jnp.exp(
            scores[head]
            + gate[head] * bias[head]
            + fill_ref[...]
            - lse_ref[pl.ds(base + head, 1), :]
        )
        for head in heads
    ]
    shared = [jnp.sum(probs[head] * grads[head], axis=0, keepdims=True) for head in heads]
    moves = [probs[head] * (grads[head] - shared[head]) for head in heads]
    val_terms = [
        dot_nn(probs[head].astype(BF), upstream[head // 2] * half_mask(head % 2)) for head in heads
    ]
    low = [item.astype(BF) for item in moves]
    key_terms = [dot_nn(low[head], query[head // 2] * half_mask(head % 2)) for head in heads]
    halves = [
        dot_nn(keys[head // 2][(head % 2) * HEAD_DIM : (head % 2 + 1) * HEAD_DIM, :], low[head])
        for head in heads
    ]
    for head in heads:
        dgate_ref[pl.ds(base + head, 1), :] = jnp.sum(
            moves[head] * bias[head], axis=0, keepdims=True
        )
    pieces = [jnp.concatenate(split_low(moves[head] * gate[head]), axis=0) for head in heads]
    placed = [dot_nn(piece, pick_ref[...]) for piece in pieces]
    columns = [jnp.broadcast_to(column, (SEEN, ROWS)) for column in hop_columns(hop_ref[...])]
    for head in heads:
        both = placed[head][:BLOCK, :] + placed[head][BLOCK:, :]
        diag_ref[head] = jnp.zeros_like(diag_ref[head])
        for index, column in enumerate(columns):
            begin = ROWS - index * BLOCK
            diag_ref[head, :, begin : begin + ROWS] += column * both
    turns = [
        dot_nn(flip_ref[...], jnp.concatenate(split_low(diag_ref[head]), axis=0)) for head in heads
    ]
    for head in heads:
        dspan_ref[pl.ds(base + head, 1), :] = diagonal_sums(turns[head])
    for pair in pairs:
        cols = slice(pair * BLOCK, (pair + 1) * BLOCK)
        grad_query = jnp.transpose(jnp.concatenate(halves[2 * pair : 2 * pair + 2], axis=0))
        grad_query = grad_query * HEAD_DIM ** (-0.5)
        val_total = val_terms[2 * pair] + val_terms[2 * pair + 1]
        out_ref[0, :, cols] = grad_query.astype(BF)
        out_ref[1, :, cols] = (key_terms[2 * pair] + key_terms[2 * pair + 1]).astype(BF)
        out_ref[2, :, cols] = val_total.astype(BF)
        sum_ref[0:1, cols] = jnp.sum(grad_query, axis=0, keepdims=True)
        sum_ref[1:2, cols] = jnp.sum(val_total, axis=0, keepdims=True)


def attention_backward(query, keyv, value, upstream, gate, span, fill, lse, pick, bias):
    length = query.shape[0]
    heads = 2 if pick is None else SEEN_HEADS
    columns = pl.BlockSpec((length, heads * HEAD_DIM), lambda i: (0, i))
    shapes = [
        jax.ShapeDtypeStruct((3, length, D), BF),
        jax.ShapeDtypeStruct((8, D), F32),
        jax.ShapeDtypeStruct((16, length), F32),
        jax.ShapeDtypeStruct((16, SPAN), F32),
    ]
    out_specs = [
        pl.BlockSpec((3, length, heads * HEAD_DIM), lambda i: (0, 0, i)),
        pl.BlockSpec((8, heads * HEAD_DIM), lambda i: (0, i)),
        whole_spec((16, length)),
        whole_spec((16, SPAN)),
    ]
    if pick is None:
        args = [query, keyv, value, upstream, gate, span, fill, lse]
        kernel, more = attention_backward_kernel, []
        scratch = [
            pltpu.VMEM((2, length, length), F32),
            pltpu.VMEM((2, length, length), F32),
            pltpu.VMEM((2, length, length), BF),
            pltpu.VMEM((2, length, length), BF),
            pltpu.VMEM((2, BLOCK, SPAN), F32),
        ]
    else:
        turned = jnp.transpose(pick[1])
        flip = jnp.concatenate([turned, turned], axis=1)
        args = [query, keyv, value, upstream, gate, fill, lse, pick[0], pick[2], flip, bias]
        kernel = seen_backward_kernel
        more = [pl.BlockSpec((heads * BLOCK, BLOCK), lambda i: (i, 0))]
        scratch = [pltpu.VMEM((heads, BLOCK, SPAN), F32)]
    return pl.pallas_call(
        kernel,
        grid=(HEADS // heads,),
        in_specs=[columns] * 4 + [whole_spec(a.shape) for a in args[4 : len(args) - len(more)]] + more,
        out_specs=out_specs,
        out_shape=shapes,
        scratch_shapes=scratch,
        compiler_params=params_of(),
    )(*args)


def weight_grad_kernel(left_ref, right_ref, out_ref, turn_ref):
    rows = left_ref.shape[1]
    strips = right_ref.shape[1] // 128
    grad = dot_tn(left_ref[...], right_ref[...])
    for strip in range(strips):
        turn_ref[pl.ds(strip, rows, stride=strips), :] = grad[:, strip * 128 : (strip + 1) * 128]
    out_ref[...] = turn_ref[...].astype(BF)


def weight_grad(left, right, rows=384):
    length, depth = left.shape
    strips = right.shape[1] // 128
    return pl.pallas_call(
        weight_grad_kernel,
        grid=(depth // rows,),
        in_specs=[
            pl.BlockSpec((length, rows), lambda i: (0, i)),
            pl.BlockSpec(right.shape, lambda i: (0, 0)),
        ],
        out_specs=pl.BlockSpec((rows * strips, 128), lambda i: (i, 0)),
        out_shape=jax.ShapeDtypeStruct((depth * strips, 128), BF),
        scratch_shapes=[pltpu.VMEM((rows * strips, 128), F32)],
        compiler_params=params_of(),
    )(left, right)


def unpack_jobs(geometry, specs):
    jobs = []
    for target, (base, depth, strips, rows) in enumerate(specs):
        for low in range(0, depth, rows):
            begin = base + low * strips
            jobs.append((target, low, rows, strips) + geometry.pieces(begin, begin + rows * strips))
    return jobs


def stream_jobs(jobs, source_ref, buffer_ref, edge_ref, sems, work):
    def copies(number):
        main, edges = jobs[number][4:6]
        slot = number % 2
        found = []
        for shard, begin, low, count in main:
            found.append(
                (source_ref.at[shard, pl.ds(begin, count)], buffer_ref.at[slot, pl.ds(low, count)])
            )
        for place, (shard, _) in enumerate(edges):
            found.append((source_ref.at[shard, pl.ds(0, TILE)], edge_ref.at[slot, place]))
        return [
            pltpu.make_async_copy(source, target, sems.at[slot, index])
            for index, (source, target) in enumerate(found)
        ]

    for copy in copies(0):
        copy.start()
    for number, job in enumerate(jobs):
        if number + 1 < len(jobs):
            for copy in copies(number + 1):
                copy.start()
        for copy in copies(number):
            copy.wait()
        slot = number % 2
        for place, (_, low) in enumerate(job[5]):
            buffer_ref[slot, low : low + TILE, :] += edge_ref[slot, place]
        work(number, job, slot)


def unpack_kernel(*refs, jobs, stages):
    source_ref = refs[0]
    targets = refs[1 : 1 + len(stages)]
    buffer_ref, edge_ref, turn_ref, sems, out_sems = refs[1 + len(stages) : 6 + len(stages)]
    stage_refs = refs[6 + len(stages) :]
    pending = {}

    def work(number, job, slot):
        target, low, rows, strips = job[:4]
        stage_ref, key = stage_refs[stages[target]], (stages[target], slot)
        if key in pending:
            pending.pop(key).wait()
        turn_ref[: rows * strips, :] = buffer_ref[slot, : rows * strips, :].astype(F32)
        for strip in range(strips):
            stage_ref[slot, :rows, strip * 128 : (strip + 1) * 128] = turn_ref[
                pl.ds(strip, rows, stride=strips), :
            ].astype(BF)
        copy = pltpu.make_async_copy(
            stage_ref.at[slot, pl.ds(0, rows)],
            targets[target].at[pl.ds(low, rows)],
            out_sems.at[stages[target], slot],
        )
        copy.start()
        pending[key] = copy

    stream_jobs(jobs, source_ref, buffer_ref, edge_ref, sems, work)
    for copy in pending.values():
        copy.wait()


def unpack(geometry, windows, specs):
    jobs = unpack_jobs(geometry, specs)
    kinds = sorted({spec[2] for spec in specs})
    stages = [kinds.index(spec[2]) for spec in specs]
    most = max(job[2] * job[3] for job in jobs)
    copies = max(len(job[4]) + len(job[5]) for job in jobs)
    edges = max([1] + [len(job[5]) for job in jobs])
    return pl.pallas_call(
        functools.partial(unpack_kernel, jobs=jobs, stages=stages),
        in_specs=[pl.BlockSpec(memory_space=pl.ANY)],
        out_specs=[pl.BlockSpec(memory_space=pl.ANY)] * len(specs),
        out_shape=[jax.ShapeDtypeStruct((s[1], s[2] * 128), BF) for s in specs],
        scratch_shapes=[
            pltpu.VMEM((2, most, 128), BF),
            pltpu.VMEM((2, edges, TILE, 128), BF),
            pltpu.VMEM((most, 128), F32),
            pltpu.SemaphoreType.DMA((2, copies)),
            pltpu.SemaphoreType.DMA((len(kinds), 2)),
        ]
        + [
            pltpu.VMEM((2, max(s[3] for s in specs if s[2] == kind), kind * 128), BF)
            for kind in kinds
        ],
        compiler_params=pltpu.CompilerParams(vmem_limit_bytes=VMEM_LIMIT),
    )(windows)


def unpack_conv_kernel(
    code_ref, source_ref, target_ref, buffer_ref, edge_ref, turn_ref, stage_ref, sems, out_sems, *,
    jobs, width
):
    first = code_ref[0] * width
    strip = first // 128
    strips = D // 128
    lead = first - strip * 128
    pending = {}

    def work(number, job, slot):
        low, rows = job[1], job[2]
        if slot in pending:
            pending.pop(slot).wait()
        turn_ref[...] = buffer_ref[slot].astype(F32)
        one = turn_ref[pl.ds(strip, rows, stride=strips), :]
        two = turn_ref[pl.ds(jnp.minimum(strip + 1, strips - 1), rows, stride=strips), :]
        pair = pltpu.roll(jnp.concatenate([one, two], axis=1), lax.rem(256 - lead, 256), 1)
        stage_ref[slot] = pair[:, :width].astype(BF)
        copy = pltpu.make_async_copy(
            stage_ref.at[slot], target_ref.at[pl.ds(low, rows)], out_sems.at[slot]
        )
        copy.start()
        pending[slot] = copy

    stream_jobs(jobs, source_ref, buffer_ref, edge_ref, sems, work)
    for copy in pending.values():
        copy.wait()


def unpack_conv(geometry, windows, code_index, rows=768):
    width = D // geometry.code_count
    depth = KERNEL * WIDTH
    jobs = unpack_jobs(geometry, [(geometry.place("conv_w"), depth, D // 128, rows)])
    copies = max(len(job[4]) + len(job[5]) for job in jobs)
    edges = max([1] + [len(job[5]) for job in jobs])
    return pl.pallas_call(
        functools.partial(unpack_conv_kernel, jobs=jobs, width=width),
        in_specs=[
            pl.BlockSpec(memory_space=pltpu.SMEM),
            pl.BlockSpec(memory_space=pl.ANY),
        ],
        out_specs=pl.BlockSpec(memory_space=pl.ANY),
        out_shape=jax.ShapeDtypeStruct((depth, width), BF),
        scratch_shapes=[
            pltpu.VMEM((2, rows * D // 128, 128), BF),
            pltpu.VMEM((2, edges, TILE, 128), BF),
            pltpu.VMEM((rows * D // 128, 128), F32),
            pltpu.VMEM((2, rows, width), BF),
            pltpu.SemaphoreType.DMA((2, copies)),
            pltpu.SemaphoreType.DMA((2,)),
        ],
        compiler_params=pltpu.CompilerParams(vmem_limit_bytes=VMEM_LIMIT),
    )(jnp.full((1,), code_index, jnp.int32), windows)


def pack_kernel(code_ref, *refs, plans):
    sources, out_ref, sems = refs[:-2], refs[-2], refs[-1]
    for code, plan in enumerate(plans):

        @pl.when(code_ref[0] == code)
        def _():
            copies = [
                pltpu.make_async_copy(
                    sources[source].at[pl.ds(begin, count)],
                    out_ref.at[slot, pl.ds(low, count)],
                    sems.at[index],
                )
                for index, (source, begin, slot, low, count) in enumerate(plan)
            ]
            for copy in copies:
                copy.start()
            for copy in copies:
                copy.wait()


def pack_plans(geometry, spans):
    plans = []
    for code in range(geometry.code_count):
        plan = []
        for slot in range(geometry.dp_count):
            begin = geometry.begins[slot * geometry.code_count + code]
            stop = begin + geometry.window
            row = begin
            while row < stop:
                place, rows, source, inner = next(
                    item for item in spans[code] if item[0] <= row < item[0] + item[1]
                )
                count = min(stop, place + rows) - row
                plan.append((source, inner + row - place, slot, row - begin, count))
                row += count
        plans.append(plan)
    return plans


def pack(geometry, code_index, sources, spans):
    plans = pack_plans(geometry, spans)
    return pl.pallas_call(
        functools.partial(pack_kernel, plans=plans),
        in_specs=[pl.BlockSpec(memory_space=pltpu.SMEM)]
        + [pl.BlockSpec(memory_space=pl.ANY)] * len(sources),
        out_specs=pl.BlockSpec(memory_space=pltpu.VMEM),
        out_shape=jax.ShapeDtypeStruct((geometry.dp_count, geometry.window, 128), BF),
        scratch_shapes=[pltpu.SemaphoreType.DMA((max(len(plan) for plan in plans),))],
        compiler_params=pltpu.CompilerParams(vmem_limit_bytes=VMEM_LIMIT),
    )(jnp.full((1,), code_index, jnp.int32), *sources)


def blocks_of_code(block):
    count = lax.axis_size("code")
    return [block] + [
        lax.ppermute(block, "code", [(i, (i + step) % count) for i in range(count)])
        for step in range(1, count)
    ]


def side_kernel(code_ref, *refs):
    blocks, out_ref = refs[:-1], refs[-1]
    count, width = len(blocks), blocks[0].shape[1]
    for code in range(count):

        @pl.when(code_ref[0] == code)
        def _():
            for source in range(count):
                out_ref[:, source * width : (source + 1) * width] = blocks[
                    (code - source) % count
                ][...]


def side_by_side(block, code_index):
    blocks = blocks_of_code(block)
    rows, width = block.shape
    return pl.pallas_call(
        side_kernel,
        in_specs=[pl.BlockSpec(memory_space=pltpu.SMEM)]
        + [pl.BlockSpec(memory_space=pltpu.VMEM)] * len(blocks),
        out_specs=pl.BlockSpec(memory_space=pltpu.VMEM),
        out_shape=jax.ShapeDtypeStruct((rows, width * len(blocks)), block.dtype),
    )(jnp.full((1,), code_index, jnp.int32), *blocks)


def sum_over(value, axis):
    count = lax.axis_size(axis)
    if count & (count - 1):
        return lax.psum(value, axis)
    bit = 1
    while bit < count:
        value = value + lax.ppermute(value, axis, [(i, i ^ bit) for i in range(count)])
        bit *= 2
    return value


def norm_forward(before, norm_gain, norm_shift):
    centred = before - jnp.mean(before, axis=-1, keepdims=True)
    inv_std = lax.rsqrt(jnp.mean(centred * centred, axis=-1, keepdims=True) + NORM_EPSILON)
    normed = centred * inv_std
    return (normed * norm_gain + norm_shift, normed, inv_std)


def norm_backward(upstream, normed, inv_std, norm_gain):
    scaled = upstream * norm_gain
    centred_grad = (
        scaled
        - jnp.mean(scaled, axis=-1, keepdims=True)
        - normed * jnp.mean(scaled * normed, axis=-1, keepdims=True)
    )
    return (
        centred_grad * inv_std,
        jnp.sum(upstream * normed, axis=0),
        jnp.sum(upstream, axis=0),
    )


def gelu(pre_act):
    return 0.5 * pre_act * (1.0 + lax.erf(pre_act * 0.7071067811865476))


def gelu_grad(pre_act):
    return (
        0.5 * (1.0 + lax.erf(pre_act * 0.7071067811865476))
        + pre_act * jnp.exp(-0.5 * pre_act * pre_act) * 0.3989422804014327
    )


def vec_part(vector, slot_index):
    return vector[slot_index * D : (slot_index + 1) * D]


def gate_maps():
    rows = (np.arange(D)[:, None] % HEAD_DIM == np.arange(HEAD_DIM)[None, :]).astype(np.float32)
    groups = np.arange(8)[:, None] // 4 == np.arange(2 * HEADS)[None, :] // HEADS
    own = np.arange(D)[:, None] // HEAD_DIM == np.arange(2 * HEADS)[None, :] % HEADS
    return rows, groups.astype(np.float32), own.astype(np.float32)


def exact_dot(left, right, dims=((1,), (0,))):
    return lax.dot_general(left, right, (dims, ((), ())), precision=HIGHEST)


def gate_columns(gate_weight):
    rows, groups, own = gate_maps()
    wide = gate_weight.astype(F32)
    sums = exact_dot(wide, jnp.asarray(groups))
    return exact_dot(jnp.asarray(rows), sums[:HEAD_DIM]) * own, sums[HEAD_DIM:]


def gate_forward(in_low, weights):
    columns, bias = weights["gate_columns"]
    high = columns.astype(BF)
    rest = (columns - high.astype(F32)).astype(BF)
    logit = dot_nn(in_low, jnp.concatenate([high, rest], axis=1))
    logit = logit[:, : 2 * HEADS] + logit[:, 2 * HEADS :] + bias
    pair = jax.nn.sigmoid(logit)
    first, second = pair[:, :HEADS], pair[:, HEADS:]
    gate_vals = first * (second * weights["gate_scale"].astype(F32) - 1.0) + 2.0
    return (gate_vals, first, second)


def gate_backward(grad_gate, first, second, in_low, weights):
    scale_vec = weights["gate_scale"].astype(F32)
    grad_scale = jnp.sum(grad_gate * first * second, axis=0)
    grad_one = grad_gate * (second * scale_vec - 1.0) * first * (1.0 - first)
    grad_two = grad_gate * first * scale_vec * second * (1.0 - second)
    both = jnp.concatenate([grad_one, grad_two], axis=1)
    rows, groups, own = gate_maps()
    high = both.astype(BF)
    rest = (both - high.astype(F32)).astype(BF)
    product = dot_tn(in_low, jnp.concatenate([high, rest], axis=1))
    product = (product[:, : 2 * HEADS] + product[:, 2 * HEADS :]) * own
    summed = exact_dot(jnp.asarray(rows), product, ((0,), (0,)))
    summed = jnp.concatenate([summed, jnp.sum(both, axis=0, keepdims=True)], axis=0)
    grad_proj = exact_dot(summed, jnp.asarray(groups), ((1,), (1,)))
    grad_heads = exact_dot(both, weights["gate_columns"][0], ((1,), (1,)))
    return (grad_heads, grad_proj, grad_scale)


def layer_forward(hidden, fill, weights, span, pick):
    vector = weights["layer_vec"].astype(F32)
    in_low = hidden.astype(BF)
    qkv_proj = dot_nn(in_low, weights["w_qkv"])
    query_low = ((qkv_proj[:, :D] + vec_part(vector, 0)) * HEAD_DIM ** (-0.5)).astype(BF)
    key_low = qkv_proj[:, D : 2 * D].astype(BF)
    value_low = (qkv_proj[:, 2 * D :] + vec_part(vector, 1)).astype(BF)
    gate_vals, first, second = gate_forward(in_low, weights)
    gate_wide = jnp.pad(jnp.transpose(gate_vals), ((0, 16 - HEADS), (0, 0)))
    attended, lse, bias = attention_forward(
        query_low, key_low, value_low, gate_wide, span, fill, pick
    )
    attn_out = dot_nn(attended, weights["w_out"]) + vec_part(vector, 2)
    mid_rows, normed_one, inv_one = norm_forward(
        DEEP_ALPHA * hidden + attn_out, vec_part(vector, 3), vec_part(vector, 4)
    )
    mid_low = mid_rows.astype(BF)
    pre_act = dot_nn(mid_low, weights["w_up"]) + vector[8 * D :]
    act_low = gelu(pre_act).astype(BF)
    ffn_out = dot_nn(act_low, weights["w_down"]) + vec_part(vector, 5)
    final_rows, normed_two, inv_two = norm_forward(
        DEEP_ALPHA * mid_rows + ffn_out, vec_part(vector, 6), vec_part(vector, 7)
    )
    kept = (in_low, query_low, key_low, value_low, gate_wide, first, second, lse, attended, bias)
    kept += (mid_low, pre_act, act_low, normed_one, inv_one, normed_two, inv_two)
    return (final_rows, kept)


def layer_backward(upstream, kept, fill, weights, span, pick):
    in_low, query_low, key_low, value_low, gate_wide, first, second, lse, attended, bias = kept[:10]
    mid_low, pre_act, act_low, normed_one, inv_one, normed_two, inv_two = kept[10:]
    vector = weights["layer_vec"].astype(F32)
    grad_res_two, grad_gain_two, grad_shift_two = norm_backward(
        upstream, normed_two, inv_two, vec_part(vector, 6)
    )
    ffn_low = grad_res_two.astype(BF)
    grad_down = weight_grad(act_low, ffn_low, 768)
    grad_pre = dot_nt(ffn_low, weights["w_down"]) * gelu_grad(pre_act)
    pre_low = grad_pre.astype(BF)
    grad_up = weight_grad(mid_low, pre_low)
    grad_mid = DEEP_ALPHA * grad_res_two + dot_nt(pre_low, weights["w_up"])
    grad_res_one, grad_gain_one, grad_shift_one = norm_backward(
        grad_mid, normed_one, inv_one, vec_part(vector, 3)
    )
    out_low = grad_res_one.astype(BF)
    grad_out = weight_grad(attended, out_low)
    grad_att = dot_nt(out_low, weights["w_out"]).astype(BF)
    parts, part_sums, grad_gate, grad_span = attention_backward(
        query_low, key_low, value_low, grad_att, gate_wide, span, fill, lse, pick, bias
    )
    grad_heads, grad_gate_proj, grad_gate_scale = gate_backward(
        jnp.transpose(grad_gate[:HEADS]), first, second, in_low, weights
    )
    proj_low = jnp.concatenate([parts[0], parts[1], parts[2]], axis=1)
    grad_qkv = weight_grad(in_low, proj_low)
    grad_hidden = DEEP_ALPHA * grad_res_one + dot_nt(proj_low, weights["w_qkv"]) + grad_heads
    grad_vec = jnp.concatenate(
        [
            part_sums[0],
            part_sums[1],
            jnp.sum(grad_res_one, axis=0),
            grad_gain_one,
            grad_shift_one,
            jnp.sum(grad_res_two, axis=0),
            grad_gain_two,
            grad_shift_two,
            jnp.sum(grad_pre, axis=0),
        ]
    )
    grad_map = {
        "w_qkv": grad_qkv,
        "w_out": grad_out,
        "w_up": grad_up,
        "w_down": grad_down,
        "layer_vec": grad_vec,
        "gate_proj": grad_gate_proj,
        "gate_scale": grad_gate_scale,
    }
    return (grad_hidden, grad_map, grad_span)


def head_pass(hidden, w_head, codebook, codes, target_codes):
    row_low = hidden.astype(BF)
    projected = dot_nn(row_low, w_head)
    inv_len = lax.rsqrt(jnp.sum(projected * projected, axis=-1, keepdims=True) + UNIT_EPSILON)
    unit_rows = projected * inv_len
    live_rows = (target_codes >= 0).astype(F32)[:, None]
    logits = LOGIT_SCALE * dot_nt(unit_rows.astype(BF), codebook)
    hits = (target_codes[:, None] == codes).astype(F32)
    top = jnp.max(logits, axis=1, keepdims=True)
    log_total = top + jnp.log(jnp.sum(jnp.exp(logits - top), axis=1, keepdims=True))
    picked = jnp.sum(logits * hits, axis=1, keepdims=True)
    loss_local = jnp.sum((log_total - picked) * live_rows)
    grad_logits = ((jnp.exp(logits - log_total) - hits) * live_rows * LOGIT_SCALE).astype(BF)
    grad_unit = dot_nn(grad_logits, codebook)
    grad_proj = (
        grad_unit - unit_rows * jnp.sum(unit_rows * grad_unit, axis=-1, keepdims=True)
    ) * inv_len
    proj_low = grad_proj.astype(BF)
    grad_head = weight_grad(row_low, proj_low)
    grad_rows = dot_nt(proj_low, w_head)
    return (loss_local, grad_rows, grad_head)


def local(
    patches,
    lengths,
    patch_masks,
    targets,
    codebook,
    params,
    first_moment,
    second_moment,
    step_count,
):
    dp_count = lax.axis_size("dp")
    code_count = lax.axis_size("code")
    code_index = lax.axis_index("code")
    shard_len = params.shape[0]
    shard_rows = shard_len // 128
    dp_index = lax.axis_index("dp")
    geometry = Geometry(dp_count, code_count, shard_rows)
    own_offset = lax.rem((dp_index * code_count + code_index) * shard_rows + geometry.phase, TILE)
    own_window = lax.dynamic_update_slice(
        jnp.zeros((geometry.window, 128), F32), params.reshape(shard_rows, 128), (own_offset, 0)
    ).astype(BF)
    windows = lax.all_gather(own_window, ("dp", "code"), axis=0, tiled=False)
    where = starts()

    def values(seg_name):
        extent = dict(layout())[seg_name]
        begin, amount = where[seg_name], math.prod(extent)
        low, high = begin // 128, -(-(begin + amount) // 128)
        found = geometry.exact(windows, low, high).reshape(-1)
        return found[begin - low * 128 : begin - low * 128 + amount].reshape(extent)

    w_patch = values("w_patch")
    glob_vec = values("glob_vec").astype(F32)
    gate_proj = values("gate_proj")
    gate_scale = values("gate_scale")
    rel_table = values("rel_table")
    w_head = values("w_head")
    layer_vec = values("layer_vec")
    conv_weight = unpack_conv(geometry, windows, code_index)
    weights = []
    for index in range(LAYERS):
        mats = unpack(
            geometry,
            windows,
            [
                (geometry.place("w_qkv", index), D, 3 * D // 128, 128),
                (geometry.place("w_out", index), D, D // 128, 384),
                (geometry.place("w_up", index), D, FF // 128, 128),
                (geometry.place("w_down", index), FF, D // 128, 512),
            ],
        )
        weights.append(
            dict(zip(("w_qkv", "w_out", "w_up", "w_down"), mats))
            | {
                "layer_vec": layer_vec[index],
                "gate_columns": gate_columns(gate_proj[index]),
                "gate_scale": gate_scale[index],
            }
        )

    places = jnp.arange(ROWS, dtype=jnp.int32)
    mask_row = jnp.pad(patch_masks[0], (0, ROWS - LONG))
    live_slot = places < jnp.minimum(lengths[0], LONG)
    visible = live_slot & (mask_row == 0)
    rank = jnp.cumsum(visible.astype(jnp.int32)) - 1
    pick = (
        visible[None, :] & (rank[None, :] == jnp.arange(SEEN, dtype=jnp.int32)[:, None])
    )
    pick_low = pick.astype(BF)
    near = jnp.sum(pick_low.reshape(SEEN, ROWS // BLOCK, BLOCK), axis=1)
    hop = jnp.sum(pick.astype(F32).reshape(SEEN, ROWS // BLOCK, BLOCK), axis=2)
    pick_seen = (pick_low, near, jnp.pad(hop, ((0, 0), (0, BLOCK - ROWS // BLOCK))))
    pick_full = pick.astype(F32)
    seen_valid = jnp.arange(SEEN, dtype=jnp.int32) < lengths[0] // 4
    seen_fill = jnp.broadcast_to(jnp.where(seen_valid, 0.0, MASK_FILL)[:, None], (SEEN, BLOCK))
    live_fill = jnp.broadcast_to(jnp.where(live_slot, 0.0, MASK_FILL)[:, None], (ROWS, BLOCK))
    live_float = live_slot.astype(F32)[:, None]
    span_table = span_onehot()
    span = dot_tn(
        jnp.pad(rel_table, ((0, 0), (0, 16 - HEADS))), jnp.asarray(span_table.T, BF)
    )

    all_codes = jnp.concatenate(blocks_of_code(codebook), axis=0)
    code_places = (
        code_index - jnp.arange(code_count, dtype=jnp.int32) + code_count
    ) % code_count * codebook.shape[0]
    code_names = (
        code_places[:, None] + jnp.arange(codebook.shape[0], dtype=jnp.int32)[None, :]
    ).reshape(1, -1)
    patch_rows = jnp.pad(patches[0], ((0, ROWS - LONG), (0, 0)))
    embedded = dot_nn(patch_rows, w_patch)
    normed_rows, normed_zero, inv_zero = norm_forward(embedded, glob_vec[0], glob_vec[1])
    start_rows = normed_rows * live_float
    conv_in = start_rows.astype(BF)
    width = D // code_count
    own_cols = code_index * width
    own_in = lax.dynamic_slice_in_dim(conv_in, own_cols, width, 1)
    half = KERNEL // 2
    conv_own = conv_call(conv_forward_kernel, own_in[:LONG], conv_weight, half, False)
    seen_own = lax.dot_general(
        pick_full, conv_own, (((1,), (0,)), ((), ())), precision=HIGHEST
    )
    seen_raw = side_by_side(seen_own, code_index)
    seen_pre = seen_raw + glob_vec[2]
    seen_start = lax.dot_general(
        pick_full, start_rows, (((1,), (0,)), ((), ())), precision=HIGHEST
    )
    seen_rows = seen_start + gelu(seen_pre)
    encoded, kept_first = layer_forward(seen_rows, seen_fill, weights[0], span, pick_seen)
    placed = lax.dot_general(
        pick_full, encoded, (((0,), (0,)), ((), ())), precision=HIGHEST
    )
    hidden = jnp.where(visible[:, None], placed, glob_vec[3])
    final, kept_second = layer_forward(hidden, live_fill, weights[1], span, None)
    target_codes = jnp.where(mask_row == 1, jnp.pad(targets[0], (0, ROWS - LONG)), -1)
    loss_local, upstream, grad_head = head_pass(final, w_head, all_codes, code_names, target_codes)

    upstream, map_second, span_second = layer_backward(
        upstream, kept_second, live_fill, weights[1], span, None
    )
    grad_mask_emb = jnp.sum(jnp.where(visible[:, None], 0.0, upstream), axis=0)
    grad_encoded = lax.dot_general(
        pick_full, upstream, (((1,), (0,)), ((), ())), precision=HIGHEST
    )
    grad_seen, map_first, span_first = layer_backward(
        grad_encoded, kept_first, seen_fill, weights[0], span, pick_seen
    )
    grad_seen = grad_seen * seen_valid[:, None].astype(F32)
    grad_conv_seen = grad_seen * gelu_grad(seen_pre)
    grad_conv = dot_tn(pick_low, grad_conv_seen.astype(BF)).astype(BF)
    grad_full = lax.dot_general(
        pick_full, grad_seen, (((0,), (0,)), ((), ())), precision=HIGHEST
    )
    own_grad = lax.dynamic_slice_in_dim(grad_conv, own_cols, width, 1)
    grad_in_own = conv_call(conv_input_kernel, own_grad[:LONG], conv_weight, half - 1, True)
    grad_conv_in = side_by_side(grad_in_own.astype(BF), code_index)
    grad_kernel, chunks = conv_weight_grad(conv_in[:LONG], grad_conv, geometry, code_index)
    grad_start = (grad_full + grad_conv_in.astype(F32)) * live_float
    grad_embedded, grad_gain_zero, grad_shift_zero = norm_backward(
        grad_start, normed_zero, inv_zero, glob_vec[0]
    )
    grad_patch = dot_tn(patch_rows, grad_embedded.astype(BF))
    grad_glob = jnp.stack(
        [grad_gain_zero, grad_shift_zero, jnp.sum(grad_conv_seen, axis=0), grad_mask_emb]
    )
    grad_rel = lax.dot_general(
        jnp.asarray(span_table),
        (span_first + span_second)[:HEADS],
        (((0,), (1,)), ((), ())),
        precision=HIGHEST,
    )
    both = (map_first, map_second)
    front = jnp.concatenate([grad_patch.reshape(-1, 128), grad_glob.reshape(-1, 128)], axis=0)
    front = jnp.pad(front, ((geometry.phase, 0), (0, 0))).astype(BF)
    sources = [front, grad_kernel]
    common = [(0, front.shape[0], 0, 0)]
    for seg_name in ("w_qkv", "w_out", "w_up", "w_down"):
        for index, layer_map in enumerate(both):
            flat = layer_map[seg_name]
            common.append((geometry.place(seg_name, index), flat.shape[0], len(sources), 0))
            sources.append(flat)
    tail_place = geometry.place("layer_vec")
    vec_rows = jnp.concatenate(
        [layer_map["layer_vec"].reshape(-1, 128) for layer_map in both], axis=0
    )
    small = [layer_map[seg_name] for seg_name in ("gate_proj", "gate_scale") for layer_map in both]
    small = jnp.concatenate([part.reshape(-1) for part in small + [grad_rel]])
    lead = small.shape[0] % 128
    small_rows = jnp.pad(small, (0, -small.shape[0] % 128)).reshape(-1, 128)
    head_rows = jnp.pad(grad_head.astype(F32), ((1, 1), (0, 0)))
    head_rows = jnp.concatenate(
        [head_rows[:-1, 128 - lead :], head_rows[1:, : 128 - lead]], axis=1
    )
    whole = small.shape[0] // 128
    tail = jnp.concatenate(
        [vec_rows, small_rows[:whole], small_rows[whole:] + head_rows[:1], head_rows[1:]], axis=0
    ).astype(BF)
    tail_rows = geometry.begins[-1] + geometry.window - tail_place
    tail = jnp.pad(tail, ((0, tail_rows - tail.shape[0]), (0, 0)))
    common.append((tail_place, tail_rows, len(sources), 0))
    sources.append(tail)
    tap_rows = WIDTH * D // 128
    spans = [
        common
        + [
            (geometry.place("conv_w") + tap * tap_rows, CHUNK * tap_rows, 1, n * CHUNK * tap_rows)
            for n, tap in enumerate(chunks[code])
        ]
        for code in range(code_count)
    ]
    own_part = pack(geometry, code_index, sources, spans)
    reduced = lax.psum_scatter(own_part, "dp", scatter_dimension=0, tiled=False).astype(F32)
    reduced = lax.dynamic_slice(reduced, (own_offset, 0), (shard_rows, 128)).reshape(shard_len)
    leader = (code_index == 0).astype(F32)
    count_local = jnp.sum((target_codes >= 0).astype(F32))
    early = jnp.concatenate(
        [
            (grad_rel * leader).reshape(-1, 128),
            jnp.full((1, 128), loss_local * leader),
            jnp.full((1, 128), count_local * leader),
        ]
    )
    early = sum_over(sum_over(jnp.pad(early, ((0, -early.shape[0] % 8), (0, 0))), "dp"), "code")
    squares_all = sum_over(sum_over(jnp.full((8, 128), jnp.sum(reduced * reduced)), "dp"), "code")
    squares_all = squares_all[0, 0]
    rel_rows = BUCKETS * HEADS // 128
    rel_all = early[:rel_rows].reshape(BUCKETS, HEADS)
    loss_all, count_all = early[rel_rows, 0], early[rel_rows + 1, 0]
    grad_norm = jnp.sqrt(squares_all) / count_all
    clip_factor = jnp.minimum(1.0, CLIP_NORM / grad_norm)
    clipped = reduced / count_all * clip_factor
    rel_grad = rel_all / count_all * clip_factor
    step_value = step_count[0].astype(F32)
    new_first = BETA_ONE * first_moment + (1.0 - BETA_ONE) * clipped
    new_second = BETA_TWO * second_moment + (1.0 - BETA_TWO) * clipped * clipped
    first_hat = new_first / (1.0 - BETA_ONE**step_value)
    second_hat = new_second / (1.0 - BETA_TWO**step_value)
    new_params = params - LEARN_RATE * (
        first_hat / (jnp.sqrt(second_hat) + ADAM_EPSILON) + WEIGHT_DECAY * params
    )
    return (
        new_params,
        new_first,
        new_second,
        new_params.astype(BF),
        loss_all / count_all,
        grad_norm,
        rel_grad,
    )


def solution(mesh):
    placed = (
        P("dp", None, None),
        P("dp"),
        P("dp", None),
        P("dp", None),
        P("code", None),
        P(("dp", "code")),
        P(("dp", "code")),
        P(("dp", "code")),
        P(),
    )
    return jax.shard_map(
        local,
        mesh=mesh,
        in_specs=placed,
        out_specs=(
            P(("dp", "code")),
            P(("dp", "code")),
            P(("dp", "code")),
            P(("dp", "code")),
            P(),
            P(),
            P(),
        ),
        check_vma=False,
    )
```

```python
import functools
import math

import jax
import jax.numpy as jnp
import numpy as np
from jax import lax
from jax.experimental import pallas as pl
from jax.experimental.pallas import tpu as pltpu
from jax.sharding import PartitionSpec as P

D = 768
HEADS = 12
HEAD_DIM = 64
FF = 3072
PATCH_IN = 256
PROJ = 256
KERNEL = 128
GROUPS = 16
WIDTH = D // GROUPS
BUCKETS = 320
MAX_DIST = 800
LAYERS = 2
LONG = 496
VISIBLE = 124
ROWS = 512
SEEN = 128
SPAN = 1024

NORM_EPSILON = 1e-05
UNIT_EPSILON = 1e-06
DEEP_ALPHA = 2.2133638394006434
LOGIT_SCALE = 25.0
CLIP_NORM = 0.005
LEARN_RATE = 0.02
BETA_ONE = 0.9
BETA_TWO = 0.999
ADAM_EPSILON = 1e-10
WEIGHT_DECAY = 0.01
MASK_FILL = -1000000000.0
HIGHEST = lax.Precision.HIGHEST
BF = jnp.bfloat16
F32 = jnp.float32
VMEM_LIMIT = 56 << 20


def layout():
    return [
        ("w_patch", (PATCH_IN, D)),
        ("glob_vec", (4, D)),
        ("conv_w", (KERNEL, WIDTH, D)),
        ("w_qkv", (LAYERS, D, 3 * D)),
        ("w_out", (LAYERS, D, D)),
        ("w_up", (LAYERS, D, FF)),
        ("w_down", (LAYERS, FF, D)),
        ("layer_vec", (LAYERS, 8 * D + FF)),
        ("gate_proj", (LAYERS, HEAD_DIM + 1, 8)),
        ("gate_scale", (LAYERS, HEADS)),
        ("rel_table", (BUCKETS, HEADS)),
        ("w_head", (D, PROJ)),
    ]


def starts():
    where = {}
    offset = 0
    for seg_name, extent in layout():
        where[seg_name] = offset
        offset += math.prod(extent)
    return where


TILE = 16


class Geometry:
    def __init__(self, dp_count, code_count, shard_rows):
        self.dp_count, self.code_count, self.shard_rows = dp_count, code_count, shard_rows
        self.shards = dp_count * code_count
        self.phase = -(starts()["conv_w"] // 128) % TILE
        self.window = -(-(shard_rows + TILE - 1) // TILE) * TILE
        self.begins = [(shard_rows * s + self.phase) // TILE * TILE for s in range(self.shards)]
        self.offsets = [(shard_rows * s + self.phase) % TILE for s in range(self.shards)]

    def place(self, seg_name, index=0):
        extent = dict(layout())[seg_name]
        amount = math.prod(extent[1:]) if index else 0
        return (starts()[seg_name] + index * amount) // 128 + self.phase

    def pieces(self, low, high):
        main, edges = [], []
        row = low
        while row < high:
            shard = max(s for s in range(self.shards) if self.begins[s] <= row)
            begin = self.begins[shard]
            if row == begin and shard > 0 and self.offsets[shard]:
                main.append((shard - 1, row - self.begins[shard - 1], row - low, TILE))
                edges.append((shard, row - low))
                row += TILE
                continue
            stop = self.begins[shard + 1] if shard + 1 < self.shards else high
            count = min(stop, high) - row
            main.append((shard, row - begin, row - low, count))
            row += count
        merged = []
        for item in main:
            last = merged[-1] if merged else None
            if last and last[0] == item[0] and last[1] + last[3] == item[1]:
                merged[-1] = last[:3] + (last[3] + item[3],)
            else:
                merged.append(item)
        return merged, edges

    def exact(self, windows, low, high):
        parts = []
        row = low
        while row < high:
            shard = row // self.shard_rows
            stop = min(high, (shard + 1) * self.shard_rows)
            begin = self.offsets[shard] + row - shard * self.shard_rows
            parts.append(windows[shard, begin : begin + stop - row])
            row = stop
        return parts[0] if len(parts) == 1 else jnp.concatenate(parts, axis=0)


def bucket_onehot():
    offsets = np.arange(-(LONG - 1), LONG)
    half_count = BUCKETS // 2
    exact_count = half_count // 2
    distance = np.abs(offsets)
    scaled = (
        np.log(np.maximum(distance, 1) / exact_count)
        / np.log(MAX_DIST / exact_count)
        * (half_count - exact_count)
    )
    larger = np.minimum(exact_count + np.maximum(scaled, 0.0).astype(np.int64), half_count - 1)
    bucket = (offsets > 0) * half_count + np.where(distance < exact_count, distance, larger)
    return (bucket[:, None] == np.arange(BUCKETS)[None, :]).astype(np.float32)


def span_onehot():
    shift = SPAN // 2 - (LONG - 1)
    table = np.zeros((SPAN, BUCKETS), np.float32)
    table[shift : shift + 2 * LONG - 1] = bucket_onehot()[::-1]
    return table


def params_of(grid_rank=1):
    return pltpu.CompilerParams(
        dimension_semantics=("arbitrary",) * grid_rank, vmem_limit_bytes=VMEM_LIMIT
    )


def dot_nn(left, right):
    return lax.dot_general(left, right, (((1,), (0,)), ((), ())), preferred_element_type=F32)


def dot_nt(left, right):
    return lax.dot_general(left, right, (((1,), (1,)), ((), ())), preferred_element_type=F32)


def dot_tn(left, right):
    return lax.dot_general(left, right, (((0,), (0,)), ((), ())), preferred_element_type=F32)


TAPS = 16


def lane_masks(width):
    group = np.arange(width)[None, :] // WIDTH
    return (group == np.arange(width // WIDTH)[:, None]).astype(np.float32)


def shifted_taps(source_ref, target_ref, count):
    width = source_ref.shape[1]
    for tap in range(TAPS):
        target_ref[:, tap * width : (tap + 1) * width] = source_ref[tap : tap + count, :].astype(BF)


def conv_forward_kernel(in_ref, weight_ref, mask_ref, out_ref, taps_ref, block_ref):
    step = pl.program_id(0)
    width = weight_ref.shape[1]

    @pl.when(step == 0)
    def _():
        shifted_taps(in_ref, taps_ref, taps_ref.shape[0])
        block_ref[...] = jnp.zeros_like(block_ref)

    for tap in range(TAPS):
        piece = weight_ref[tap * WIDTH : (tap + 1) * WIDTH, :]
        for group in range(width // WIDTH):
            low = tap * width + group * WIDTH
            block_ref[low : low + WIDTH, :] = piece * mask_ref[group : group + 1, :]
    begin = pl.multiple_of(step * TAPS, TAPS)
    term = dot_nn(taps_ref[pl.ds(begin, ROWS), :], block_ref[...])

    @pl.when(step == 0)
    def _():
        out_ref[...] = term

    @pl.when(step > 0)
    def _():
        out_ref[...] += term


def conv_input_kernel(in_ref, weight_ref, mask_ref, out_ref, taps_ref, block_ref):
    step = pl.program_id(0)
    width = weight_ref.shape[1]

    @pl.when(step == 0)
    def _():
        shifted_taps(in_ref, taps_ref, taps_ref.shape[0])
        block_ref[...] = jnp.zeros_like(block_ref)

    for tap in range(TAPS):
        piece = weight_ref[tap * WIDTH : (tap + 1) * WIDTH, :]
        low = (TAPS - 1 - tap) * width
        for group in range(width // WIDTH):
            block_ref[group * WIDTH : (group + 1) * WIDTH, low : low + width] = (
                piece * mask_ref[group : group + 1, :]
            )
    begin = pl.multiple_of((pl.num_programs(0) - 1 - step) * TAPS, TAPS)
    term = dot_nt(taps_ref[pl.ds(begin, ROWS), :], block_ref[...])

    @pl.when(step == 0)
    def _():
        out_ref[...] = term

    @pl.when(step > 0)
    def _():
        out_ref[...] += term


def conv_call(kernel, conv_in, weight, front, nt):
    width = weight.shape[1]
    steps = KERNEL // TAPS
    count = ROWS + KERNEL - TAPS
    padded = jnp.pad(
        conv_in.astype(F32),
        ((front, count + TAPS - front - conv_in.shape[0]), (0, 0)),
    )
    block = (width, TAPS * width) if nt else (TAPS * width, width)
    return pl.pallas_call(
        kernel,
        grid=(steps,),
        in_specs=[
            pl.BlockSpec(padded.shape, lambda i: (0, 0)),
            pl.BlockSpec((TAPS * WIDTH, width), lambda i: (i, 0)),
            pl.BlockSpec((width // WIDTH, width), lambda i: (0, 0)),
        ],
        out_specs=pl.BlockSpec((ROWS, width), lambda i: (0, 0)),
        out_shape=jax.ShapeDtypeStruct((ROWS, width), F32),
        scratch_shapes=[pltpu.VMEM((count, TAPS * width), BF), pltpu.VMEM(block, BF)],
        compiler_params=params_of(),
    )(padded, weight, jnp.asarray(lane_masks(width), BF))


CHUNK = 6


def conv_weight_kernel(tap_ref, in_ref, grad_ref, mask_ref, out_ref, taps_ref, turn_ref):
    parts = in_ref.shape[0]
    begin = tap_ref[pl.program_id(0)]
    strips = D // 128
    rows = CHUNK * WIDTH
    for part in range(parts):
        turned = pltpu.roll(in_ref[part], in_ref.shape[2] - begin, 1)
        for tap in range(CHUNK):
            taps_ref[part, tap * PART : (tap + 1) * PART, :] = turned[:, tap : tap + ROWS].astype(
                BF
            )
    sums = []
    for part in range(parts):
        term = dot_nn(taps_ref[part], grad_ref[part])
        pieces = []
        for tap in range(CHUNK):
            total = None
            for group in range(mask_ref.shape[0]):
                low = tap * PART + group * WIDTH
                piece = term[low : low + WIDTH, :] * mask_ref[group : group + 1, :]
                total = piece if total is None else total + piece
            pieces.append(total)
        sums.append(jnp.concatenate(pieces, axis=0))
    for strip in range(strips):
        part, low = divmod(strip * 128, PART)
        columns = sums[part][:, low : min(low + 128, PART)]
        if low + 128 > PART:
            columns = jnp.concatenate([columns, sums[part + 1][:, : low + 128 - PART]], axis=1)
        turn_ref[pl.ds(strip, rows, stride=strips), :] = columns
    out_ref[...] = turn_ref[...].astype(BF)


PART = 4 * WIDTH


def owned_chunks(geometry, base, unit, count, chunk, step, slots):
    tables = []
    for code in range(geometry.code_count):
        found = []
        for slot in slots:
            begin = geometry.begins[slot * geometry.code_count + code] - base
            low = max(begin // unit, 0) // step * step
            high = min(-(-(begin + geometry.window) // unit), count)
            while low < high:
                found.append(min(low, count - chunk))
                low += chunk
        tables.append(list(dict.fromkeys(found)))
    most = max([1] + [len(table) for table in tables])
    return [(table or [0]) + (table or [0])[-1:] * (most - max(len(table), 1)) for table in tables]


def chunk_spans(chunks, base, unit, chunk, source):
    return [
        [(base + low * unit, chunk * unit, source, n * chunk * unit) for n, low in enumerate(table)]
        for table in chunks
    ]


def chunk_table(chunks, code_index):
    return lax.dynamic_index_in_dim(jnp.asarray(chunks, jnp.int32), code_index, 0, False)


def conv_weight_inputs(conv_in, grad_low):
    parts = D // PART
    front = KERNEL // 2
    padded = jnp.pad(
        jnp.transpose(conv_in).astype(F32),
        ((0, 0), (front, ROWS + KERNEL - front - conv_in.shape[0])),
    ).reshape(parts, PART, ROWS + KERNEL)
    return padded, jnp.transpose(grad_low.reshape(ROWS, parts, PART), (1, 0, 2))


def conv_weight_grad(padded, grads, geometry, code_index, slots):
    parts = D // PART
    masks = jnp.asarray(lane_masks(PART), F32)
    base, unit = geometry.place("conv_w"), WIDTH * D // 128
    chunks = owned_chunks(geometry, base, unit, KERNEL, CHUNK, 1, slots)
    table = chunk_table(chunks, code_index)
    rows = CHUNK * unit
    out = pl.pallas_call(
        conv_weight_kernel,
        grid_spec=pltpu.PrefetchScalarGridSpec(
            num_scalar_prefetch=1,
            grid=(len(chunks[0]),),
            in_specs=[
                pl.BlockSpec(padded.shape, lambda i, t: (0, 0, 0)),
                pl.BlockSpec(grads.shape, lambda i, t: (0, 0, 0)),
                pl.BlockSpec(masks.shape, lambda i, t: (0, 0)),
            ],
            out_specs=pl.BlockSpec((rows, 128), lambda i, t: (i, 0)),
            scratch_shapes=[
                pltpu.VMEM((parts, CHUNK * PART, ROWS), BF),
                pltpu.VMEM((rows, 128), F32),
            ],
        ),
        out_shape=jax.ShapeDtypeStruct((len(chunks[0]) * rows, 128), BF),
        compiler_params=params_of(),
    )(table, padded, grads, masks)
    return out, (chunks, base, unit, CHUNK)


BLOCK = 128


def half_mask(side):
    lane = lax.broadcasted_iota(jnp.int32, (1, BLOCK), 1)
    return jnp.where(lane // HEAD_DIM == side, 1.0, 0.0).astype(BF)


def toeplitz(span_ref, head):
    row = jnp.broadcast_to(span_ref[pl.ds(head, 1), :], (BLOCK, SPAN))
    return pltpu.roll(row, 0, 1, stride=1, stride_axis=0)


def hop_columns(hop):
    return [hop[:, index : index + 1] for index in range(ROWS // BLOCK)]


def seen_biases(turned, pick, near, hop):
    moved = [dot_nn(near, item.astype(BF)) for item in turned]
    columns = [jnp.broadcast_to(column, (SEEN, ROWS)) for column in hop_columns(hop)]
    tables = []
    for item in moved:
        table = None
        for index, column in enumerate(columns):
            low = index * BLOCK
            part = column * item[:, ROWS - low : SPAN - low]
            table = part if table is None else table + part
        tables.append(table.astype(BF))
    return [dot_nt(table, pick) for table in tables]


def wide(column, length):
    return jnp.concatenate([column] * (length // BLOCK), axis=1)


def attention_forward_kernel(
    q_ref, k_ref, v_ref, gate_ref, span_ref, fill_ref, out_ref, lse_ref, score_ref, turn_ref
):
    step = pl.program_id(0)
    length = q_ref.shape[0]
    values = jnp.transpose(v_ref[...])
    sides = range(2)
    turned = [toeplitz(span_ref, step * 2 + side) for side in sides]
    for side in sides:
        score_ref[side] = dot_nt(k_ref[...] * half_mask(side), q_ref[...])
    tops = []
    for side in sides:
        gate = gate_ref[pl.ds(step * 2 + side, 1), :]
        top = None
        for low in range(0, length, BLOCK):
            rows = slice(low, low + BLOCK)
            bias = turned[side][:, ROWS - low : SPAN - low]
            scores = score_ref[side, rows, :] + gate * bias + wide(fill_ref[rows, :], length)
            score_ref[side, rows, :] = scores
            most = jnp.max(scores, axis=0, keepdims=True)
            top = most if top is None else jnp.maximum(top, most)
        tops.append(top)
    totals = []
    for side in sides:
        total = None
        for low in range(0, length, BLOCK):
            rows = slice(low, low + BLOCK)
            weights = jnp.exp(score_ref[side, rows, :] - tops[side])
            part = jnp.sum(weights, axis=0, keepdims=True)
            total = part if total is None else total + part
            turn_ref[side, rows, :] = weights.astype(BF)
        totals.append(total)
    mixed = []
    for side in sides:
        lse_ref[pl.ds(step * 2 + side, 1), :] = tops[side] + jnp.log(totals[side])
        part = dot_nn(values[side * HEAD_DIM : (side + 1) * HEAD_DIM, :], turn_ref[side])
        mixed.append(part * (1.0 / totals[side]))
    out_ref[...] = jnp.transpose(jnp.concatenate(mixed, axis=0)).astype(BF)


SEEN_HEADS = 12


def seen_forward_kernel(
    q_ref, k_ref, v_ref, gate_ref, span_ref, fill_ref, pick_ref, near_ref, hop_ref,
    out_ref, lse_ref, bias_ref,
):
    heads = range(SEEN_HEADS)
    base = pl.program_id(0) * SEEN_HEADS
    pick, near, hop = pick_ref[...], near_ref[...], hop_ref[...]
    pairs = range(SEEN_HEADS // 2)
    query = [q_ref[:, pair * BLOCK : (pair + 1) * BLOCK] for pair in pairs]
    keyv = [k_ref[:, pair * BLOCK : (pair + 1) * BLOCK] for pair in pairs]
    values = [jnp.transpose(v_ref[:, pair * BLOCK : (pair + 1) * BLOCK]) for pair in pairs]
    turned = [toeplitz(span_ref, base + head) for head in heads]
    bias = seen_biases(turned, pick, near, hop)
    scores = [dot_nt(keyv[head // 2] * half_mask(head % 2), query[head // 2]) for head in heads]
    for head in heads:
        bias_ref[head * BLOCK : (head + 1) * BLOCK, :] = bias[head].astype(BF)
    scores = [
        scores[head] + gate_ref[pl.ds(base + head, 1), :] * bias[head] + fill_ref[...]
        for head in heads
    ]
    tops = [jnp.max(item, axis=0, keepdims=True) for item in scores]
    weights = [jnp.exp(scores[head] - tops[head]) for head in heads]
    totals = [jnp.sum(item, axis=0, keepdims=True) for item in weights]
    mixed = []
    for head in heads:
        lse_ref[pl.ds(base + head, 1), :] = tops[head] + jnp.log(totals[head])
        low = (head % 2) * HEAD_DIM
        part = dot_nn(values[head // 2][low : low + HEAD_DIM, :], weights[head].astype(BF))
        mixed.append(part * (1.0 / totals[head]))
    for pair in pairs:
        both = jnp.concatenate(mixed[2 * pair : 2 * pair + 2], axis=0)
        out_ref[:, pair * BLOCK : (pair + 1) * BLOCK] = jnp.transpose(both).astype(BF)


def pair_spec(length):
    return pl.BlockSpec((length, 2 * HEAD_DIM), lambda i: (0, i))


def whole_spec(shape):
    return pl.BlockSpec(shape, lambda i: (0,) * len(shape))


def attention_forward(query, keyv, value, gate, span, fill, pick):
    length = query.shape[0]
    args = [query, keyv, value, gate, span, fill] + list(pick or ())
    shapes = [
        jax.ShapeDtypeStruct((length, D), BF),
        jax.ShapeDtypeStruct((16, length), F32),
    ]
    if pick is None:
        found = pl.pallas_call(
            attention_forward_kernel,
            grid=(HEADS // 2,),
            in_specs=[pair_spec(length)] * 3 + [whole_spec(a.shape) for a in args[3:]],
            out_specs=[pair_spec(length), whole_spec((16, length))],
            out_shape=shapes,
            scratch_shapes=[
                pltpu.VMEM((2, length, length), F32),
                pltpu.VMEM((2, length, length), BF),
            ],
            compiler_params=params_of(),
        )(*args)
        return found[0], found[1], None
    columns = pl.BlockSpec((length, SEEN_HEADS * HEAD_DIM), lambda i: (0, i))
    return pl.pallas_call(
        seen_forward_kernel,
        grid=(HEADS // SEEN_HEADS,),
        in_specs=[columns] * 3 + [whole_spec(a.shape) for a in args[3:]],
        out_specs=[
            columns,
            whole_spec((16, length)),
            pl.BlockSpec((SEEN_HEADS * BLOCK, BLOCK), lambda i: (i, 0)),
        ],
        out_shape=shapes + [jax.ShapeDtypeStruct((HEADS * BLOCK, BLOCK), BF)],
        compiler_params=params_of(),
    )(*args)


def diagonal_sums(turn):
    half = BLOCK // 2
    while half:
        turn = turn[:half, :] + pltpu.roll(turn[half:, :], SPAN - half, 1)
        half //= 2
    return turn


def attention_backward_kernel(
    q_ref, k_ref, v_ref, up_ref, gate_ref, span_ref, fill_ref, lse_ref,
    dq_ref, dk_ref, dv_ref, sum_ref, dgate_ref, dspan_ref,
    prob_ref, grad_ref, turn_ref, low_ref, diag_ref,
):
    step = pl.program_id(0)
    length = q_ref.shape[0]
    sides = range(2)

    @pl.when(step == 0)
    def _():
        dspan_ref[...] = jnp.zeros_like(dspan_ref)
        dgate_ref[...] = jnp.zeros_like(dgate_ref)

    keys = jnp.transpose(k_ref[...])
    turned = [toeplitz(span_ref, step * 2 + side) for side in sides]
    for side in sides:
        prob_ref[side] = dot_nt(k_ref[...] * half_mask(side), q_ref[...])
        grad_ref[side] = dot_nt(v_ref[...] * half_mask(side), up_ref[...])
        diag_ref[side] = jnp.zeros_like(diag_ref[side])
    shared = []
    for side in sides:
        gate = gate_ref[pl.ds(step * 2 + side, 1), :]
        lse = lse_ref[pl.ds(step * 2 + side, 1), :]
        total = None
        for low in range(0, length, BLOCK):
            rows = slice(low, low + BLOCK)
            bias = turned[side][:, ROWS - low : SPAN - low]
            scores = prob_ref[side, rows, :] + gate * bias + wide(fill_ref[rows, :], length)
            probs = jnp.exp(scores - lse)
            prob_ref[side, rows, :] = probs
            low_ref[side, rows, :] = probs.astype(BF)
            part = jnp.sum(probs * grad_ref[side, rows, :], axis=0, keepdims=True)
            total = part if total is None else total + part
        shared.append(total)
    val_total = sum(dot_nn(low_ref[side], up_ref[...] * half_mask(side)) for side in sides)
    for side in sides:
        gate = gate_ref[pl.ds(step * 2 + side, 1), :]
        dgate = None
        for low in range(0, length, BLOCK):
            rows = slice(low, low + BLOCK)
            bias = turned[side][:, ROWS - low : SPAN - low]
            grad_scores = prob_ref[side, rows, :] * (grad_ref[side, rows, :] - shared[side])
            turn_ref[side, rows, :] = grad_scores.astype(BF)
            part = jnp.sum(grad_scores * bias, axis=0, keepdims=True)
            dgate = part if dgate is None else dgate + part
            diag_ref[side, :, ROWS - low : SPAN - low] += grad_scores * gate
        dgate_ref[pl.ds(step * 2 + side, 1), :] = dgate
    key_total = sum(dot_nn(turn_ref[side], q_ref[...] * half_mask(side)) for side in sides)
    halves = [
        dot_nn(keys[side * HEAD_DIM : (side + 1) * HEAD_DIM, :], turn_ref[side]) for side in sides
    ]
    for side in sides:
        dspan_ref[pl.ds(step * 2 + side, 1), :] = diagonal_sums(diag_ref[side])
    grad_query = jnp.transpose(jnp.concatenate(halves, axis=0)) * HEAD_DIM ** (-0.5)
    dq_ref[...] = grad_query.astype(BF)
    dk_ref[...] = key_total.astype(BF)
    dv_ref[...] = val_total.astype(BF)
    sum_ref[0:1, :] = jnp.sum(grad_query, axis=0, keepdims=True)
    sum_ref[1:2, :] = jnp.sum(val_total, axis=0, keepdims=True)


def split_low(value):
    high = value.astype(BF)
    return high, (value - high.astype(F32)).astype(BF)


def seen_backward_kernel(
    q_ref, k_ref, v_ref, up_ref, gate_ref, fill_ref, lse_ref, pick_ref, hop_ref, flip_ref,
    bias_ref, dq_ref, dk_ref, dv_ref, sum_ref, dgate_ref, dspan_ref, diag_ref,
):
    heads, pairs = range(SEEN_HEADS), range(SEEN_HEADS // 2)
    base = pl.program_id(0) * SEEN_HEADS

    @pl.when(base == 0)
    def _():
        dspan_ref[...] = jnp.zeros_like(dspan_ref)
        dgate_ref[...] = jnp.zeros_like(dgate_ref)

    def pair_of(ref):
        return [ref[:, pair * BLOCK : (pair + 1) * BLOCK] for pair in pairs]

    query, keyv, value, upstream = (pair_of(ref) for ref in (q_ref, k_ref, v_ref, up_ref))
    keys = [jnp.transpose(item) for item in keyv]
    gate = [gate_ref[pl.ds(base + head, 1), :] for head in heads]
    bias = [bias_ref[head * BLOCK : (head + 1) * BLOCK, :].astype(F32) for head in heads]
    scores = [dot_nt(keyv[head // 2] * half_mask(head % 2), query[head // 2]) for head in heads]
    grads = [dot_nt(value[head // 2] * half_mask(head % 2), upstream[head // 2]) for head in heads]
    probs = [
        jnp.exp(
            scores[head]
            + gate[head] * bias[head]
            + fill_ref[...]
            - lse_ref[pl.ds(base + head, 1), :]
        )
        for head in heads
    ]
    shared = [jnp.sum(probs[head] * grads[head], axis=0, keepdims=True) for head in heads]
    moves = [probs[head] * (grads[head] - shared[head]) for head in heads]
    val_terms = [
        dot_nn(probs[head].astype(BF), upstream[head // 2] * half_mask(head % 2)) for head in heads
    ]
    low = [item.astype(BF) for item in moves]
    key_terms = [dot_nn(low[head], query[head // 2] * half_mask(head % 2)) for head in heads]
    halves = [
        dot_nn(keys[head // 2][(head % 2) * HEAD_DIM : (head % 2 + 1) * HEAD_DIM, :], low[head])
        for head in heads
    ]
    for head in heads:
        dgate_ref[pl.ds(base + head, 1), :] = jnp.sum(
            moves[head] * bias[head], axis=0, keepdims=True
        )
    pieces = [jnp.concatenate(split_low(moves[head] * gate[head]), axis=0) for head in heads]
    placed = [dot_nn(piece, pick_ref[...]) for piece in pieces]
    columns = [jnp.broadcast_to(column, (SEEN, ROWS)) for column in hop_columns(hop_ref[...])]
    for head in heads:
        both = placed[head][:BLOCK, :] + placed[head][BLOCK:, :]
        diag_ref[head] = jnp.zeros_like(diag_ref[head])
        for index, column in enumerate(columns):
            begin = ROWS - index * BLOCK
            diag_ref[head, :, begin : begin + ROWS] += column * both
    turns = [
        dot_nn(flip_ref[...], jnp.concatenate(split_low(diag_ref[head]), axis=0)) for head in heads
    ]
    for head in heads:
        dspan_ref[pl.ds(base + head, 1), :] = diagonal_sums(turns[head])
    for pair in pairs:
        cols = slice(pair * BLOCK, (pair + 1) * BLOCK)
        grad_query = jnp.transpose(jnp.concatenate(halves[2 * pair : 2 * pair + 2], axis=0))
        grad_query = grad_query * HEAD_DIM ** (-0.5)
        val_total = val_terms[2 * pair] + val_terms[2 * pair + 1]
        dq_ref[:, cols] = grad_query.astype(BF)
        dk_ref[:, cols] = (key_terms[2 * pair] + key_terms[2 * pair + 1]).astype(BF)
        dv_ref[:, cols] = val_total.astype(BF)
        sum_ref[0:1, cols] = jnp.sum(grad_query, axis=0, keepdims=True)
        sum_ref[1:2, cols] = jnp.sum(val_total, axis=0, keepdims=True)


def attention_backward(query, keyv, value, upstream, gate, span, fill, lse, pick, bias):
    length = query.shape[0]
    heads = 2 if pick is None else SEEN_HEADS
    columns = pl.BlockSpec((length, heads * HEAD_DIM), lambda i: (0, i))
    shapes = [
        jax.ShapeDtypeStruct((length, D), BF),
        jax.ShapeDtypeStruct((length, D), BF),
        jax.ShapeDtypeStruct((length, D), BF),
        jax.ShapeDtypeStruct((8, D), F32),
        jax.ShapeDtypeStruct((16, length), F32),
        jax.ShapeDtypeStruct((16, SPAN), F32),
    ]
    out_specs = [
        columns,
        columns,
        columns,
        pl.BlockSpec((8, heads * HEAD_DIM), lambda i: (0, i)),
        whole_spec((16, length)),
        whole_spec((16, SPAN)),
    ]
    if pick is None:
        args = [query, keyv, value, upstream, gate, span, fill, lse]
        kernel, more = attention_backward_kernel, []
        scratch = [
            pltpu.VMEM((2, length, length), F32),
            pltpu.VMEM((2, length, length), F32),
            pltpu.VMEM((2, length, length), BF),
            pltpu.VMEM((2, length, length), BF),
            pltpu.VMEM((2, BLOCK, SPAN), F32),
        ]
    else:
        turned = jnp.transpose(pick[1])
        flip = jnp.concatenate([turned, turned], axis=1)
        args = [query, keyv, value, upstream, gate, fill, lse, pick[0], pick[2], flip, bias]
        kernel = seen_backward_kernel
        more = [pl.BlockSpec((heads * BLOCK, BLOCK), lambda i: (i, 0))]
        scratch = [pltpu.VMEM((heads, BLOCK, SPAN), F32)]
    return pl.pallas_call(
        kernel,
        grid=(HEADS // heads,),
        in_specs=[columns] * 4 + [whole_spec(a.shape) for a in args[4 : len(args) - len(more)]] + more,
        out_specs=out_specs,
        out_shape=shapes,
        scratch_shapes=scratch,
        compiler_params=params_of(),
    )(*args)


def weight_grad_kernel(table_ref, left_ref, right_ref, out_ref, turn_ref):
    rows = left_ref.shape[1]
    strips = right_ref.shape[1] // 128
    grad = dot_tn(left_ref[...], right_ref[...])
    for strip in range(strips):
        turn_ref[pl.ds(strip, rows, stride=strips), :] = grad[:, strip * 128 : (strip + 1) * 128]
    out_ref[...] = turn_ref[...].astype(BF)


def weight_grad(left, right, geometry, code_index, base, rows):
    length, depth = left.shape
    strips = right.shape[1] // 128
    slots = range(geometry.dp_count)
    chunks = owned_chunks(geometry, base, strips, depth, rows, rows, slots)
    out = pl.pallas_call(
        weight_grad_kernel,
        grid_spec=pltpu.PrefetchScalarGridSpec(
            num_scalar_prefetch=1,
            grid=(len(chunks[0]),),
            in_specs=[
                pl.BlockSpec((length, rows), lambda i, t: (0, t[i])),
                pl.BlockSpec(right.shape, lambda i, t: (0, 0)),
            ],
            out_specs=pl.BlockSpec((rows * strips, 128), lambda i, t: (i, 0)),
            scratch_shapes=[pltpu.VMEM((rows * strips, 128), F32)],
        ),
        out_shape=jax.ShapeDtypeStruct((len(chunks[0]) * rows * strips, 128), BF),
        compiler_params=params_of(),
    )(chunk_table(chunks, code_index) // rows, left, right)
    return out, (chunks, base, strips, rows)


def unpack_jobs(geometry, specs):
    jobs = []
    for target, (base, depth, strips, rows) in enumerate(specs):
        for low in range(0, depth, rows):
            begin = base + low * strips
            jobs.append((target, low, rows, strips) + geometry.pieces(begin, begin + rows * strips))
    return jobs


def stream_jobs(jobs, source_ref, buffer_ref, edge_ref, sems, work):
    def copies(number):
        main, edges = jobs[number][4:6]
        slot = number % 2
        found = []
        for shard, begin, low, count in main:
            found.append(
                (source_ref.at[shard, pl.ds(begin, count)], buffer_ref.at[slot, pl.ds(low, count)])
            )
        for place, (shard, _) in enumerate(edges):
            found.append((source_ref.at[shard, pl.ds(0, TILE)], edge_ref.at[slot, place]))
        return [
            pltpu.make_async_copy(source, target, sems.at[slot, index])
            for index, (source, target) in enumerate(found)
        ]

    for copy in copies(0):
        copy.start()
    for number, job in enumerate(jobs):
        if number + 1 < len(jobs):
            for copy in copies(number + 1):
                copy.start()
        for copy in copies(number):
            copy.wait()
        slot = number % 2
        for place, (_, low) in enumerate(job[5]):
            buffer_ref[slot, low : low + TILE, :] += edge_ref[slot, place]
        work(number, job, slot)


def unpack_kernel(*refs, jobs, stages):
    source_ref = refs[0]
    targets = refs[1 : 1 + len(stages)]
    buffer_ref, edge_ref, turn_ref, sems, out_sems = refs[1 + len(stages) : 6 + len(stages)]
    stage_refs = refs[6 + len(stages) :]
    pending = {}

    def work(number, job, slot):
        target, low, rows, strips = job[:4]
        stage_ref, key = stage_refs[stages[target]], (stages[target], slot)
        if key in pending:
            pending.pop(key).wait()
        turn_ref[: rows * strips, :] = buffer_ref[slot, : rows * strips, :].astype(F32)
        for strip in range(strips):
            stage_ref[slot, :rows, strip * 128 : (strip + 1) * 128] = turn_ref[
                pl.ds(strip, rows, stride=strips), :
            ].astype(BF)
        copy = pltpu.make_async_copy(
            stage_ref.at[slot, pl.ds(0, rows)],
            targets[target].at[pl.ds(low, rows)],
            out_sems.at[stages[target], slot],
        )
        copy.start()
        pending[key] = copy

    stream_jobs(jobs, source_ref, buffer_ref, edge_ref, sems, work)
    for copy in pending.values():
        copy.wait()


def unpack(geometry, windows, specs):
    jobs = unpack_jobs(geometry, specs)
    kinds = sorted({spec[2] for spec in specs})
    stages = [kinds.index(spec[2]) for spec in specs]
    most = max(job[2] * job[3] for job in jobs)
    copies = max(len(job[4]) + len(job[5]) for job in jobs)
    edges = max([1] + [len(job[5]) for job in jobs])
    return pl.pallas_call(
        functools.partial(unpack_kernel, jobs=jobs, stages=stages),
        in_specs=[pl.BlockSpec(memory_space=pl.ANY)],
        out_specs=[pl.BlockSpec(memory_space=pl.ANY)] * len(specs),
        out_shape=[jax.ShapeDtypeStruct((s[1], s[2] * 128), BF) for s in specs],
        scratch_shapes=[
            pltpu.VMEM((2, most, 128), BF),
            pltpu.VMEM((2, edges, TILE, 128), BF),
            pltpu.VMEM((most, 128), F32),
            pltpu.SemaphoreType.DMA((2, copies)),
            pltpu.SemaphoreType.DMA((len(kinds), 2)),
        ]
        + [
            pltpu.VMEM((2, max(s[3] for s in specs if s[2] == kind), kind * 128), BF)
            for kind in kinds
        ],
        compiler_params=pltpu.CompilerParams(vmem_limit_bytes=VMEM_LIMIT),
    )(windows)


def unpack_conv_kernel(
    code_ref, source_ref, target_ref, buffer_ref, edge_ref, turn_ref, stage_ref, sems, out_sems, *,
    jobs, width
):
    first = code_ref[0] * width
    strip = first // 128
    strips = D // 128
    lead = first - strip * 128
    pending = {}

    def work(number, job, slot):
        low, rows = job[1], job[2]
        if slot in pending:
            pending.pop(slot).wait()
        turn_ref[...] = buffer_ref[slot].astype(F32)
        one = turn_ref[pl.ds(strip, rows, stride=strips), :]
        two = turn_ref[pl.ds(jnp.minimum(strip + 1, strips - 1), rows, stride=strips), :]
        pair = pltpu.roll(jnp.concatenate([one, two], axis=1), lax.rem(256 - lead, 256), 1)
        stage_ref[slot] = pair[:, :width].astype(BF)
        copy = pltpu.make_async_copy(
            stage_ref.at[slot], target_ref.at[pl.ds(low, rows)], out_sems.at[slot]
        )
        copy.start()
        pending[slot] = copy

    stream_jobs(jobs, source_ref, buffer_ref, edge_ref, sems, work)
    for copy in pending.values():
        copy.wait()


def unpack_conv(geometry, windows, code_index, rows=768):
    width = D // geometry.code_count
    depth = KERNEL * WIDTH
    jobs = unpack_jobs(geometry, [(geometry.place("conv_w"), depth, D // 128, rows)])
    copies = max(len(job[4]) + len(job[5]) for job in jobs)
    edges = max([1] + [len(job[5]) for job in jobs])
    return pl.pallas_call(
        functools.partial(unpack_conv_kernel, jobs=jobs, width=width),
        in_specs=[
            pl.BlockSpec(memory_space=pltpu.SMEM),
            pl.BlockSpec(memory_space=pl.ANY),
        ],
        out_specs=pl.BlockSpec(memory_space=pl.ANY),
        out_shape=jax.ShapeDtypeStruct((depth, width), BF),
        scratch_shapes=[
            pltpu.VMEM((2, rows * D // 128, 128), BF),
            pltpu.VMEM((2, edges, TILE, 128), BF),
            pltpu.VMEM((rows * D // 128, 128), F32),
            pltpu.VMEM((2, rows, width), BF),
            pltpu.SemaphoreType.DMA((2, copies)),
            pltpu.SemaphoreType.DMA((2,)),
        ],
        compiler_params=pltpu.CompilerParams(vmem_limit_bytes=VMEM_LIMIT),
    )(jnp.full((1,), code_index, jnp.int32), windows)


def pack_kernel(code_ref, *refs, plans, empty):
    sources, out_ref, sems = refs[:-2], refs[-2], refs[-1]
    for slot in range(empty):
        out_ref[slot] = jnp.zeros_like(out_ref[slot])
    for code, plan in enumerate(plans):

        @pl.when(code_ref[0] == code)
        def _():
            copies = [
                pltpu.make_async_copy(
                    sources[source].at[pl.ds(begin, count)],
                    out_ref.at[slot, pl.ds(low, count)],
                    sems.at[index],
                )
                for index, (source, begin, slot, low, count) in enumerate(plan)
            ]
            for copy in copies:
                copy.start()
            for copy in copies:
                copy.wait()


def pack_plans(geometry, spans, slots):
    plans = []
    for code in range(geometry.code_count):
        plan = []
        for slot in slots:
            begin = geometry.begins[slot * geometry.code_count + code]
            stop = begin + geometry.window
            row = begin
            while row < stop:
                place, rows, source, inner = next(
                    item for item in spans[code] if item[0] <= row < item[0] + item[1]
                )
                count = min(stop, place + rows) - row
                plan.append((source, inner + row - place, slot, row - begin, count))
                row += count
        plans.append(plan)
    return plans


def pack(geometry, code_index, sources, spans, low, high):
    plans = pack_plans(geometry, spans, range(low, high))
    return pl.pallas_call(
        functools.partial(pack_kernel, plans=plans, empty=low),
        in_specs=[pl.BlockSpec(memory_space=pltpu.SMEM)]
        + [pl.BlockSpec(memory_space=pl.ANY)] * len(sources),
        out_specs=pl.BlockSpec(memory_space=pltpu.VMEM),
        out_shape=jax.ShapeDtypeStruct((high, geometry.window, 128), BF),
        scratch_shapes=[pltpu.SemaphoreType.DMA((max(len(plan) for plan in plans),))],
        compiler_params=pltpu.CompilerParams(vmem_limit_bytes=VMEM_LIMIT),
    )(jnp.full((1,), code_index, jnp.int32), *sources)


def front_slots(geometry):
    stop = geometry.place("w_qkv")
    count = sum(
        geometry.begins[slot * geometry.code_count + geometry.code_count - 1] + geometry.window
        <= stop
        for slot in range(geometry.dp_count)
    )
    if geometry.dp_count & (geometry.dp_count - 1) or not count:
        return 0
    return 1 << (count.bit_length() - 1)


def add_low(left, right):
    return (left.astype(F32) + right.astype(F32)).astype(BF)


def reduce_front(held, dp_count, dp_index):
    count = held.shape[0]
    bit = count // 2
    while bit:
        mine = dp_index // bit % 2
        keep = lax.dynamic_slice_in_dim(held, mine * bit, bit, 0)
        give = lax.dynamic_slice_in_dim(held, (1 - mine) * bit, bit, 0)
        held = add_low(keep, lax.ppermute(give, "dp", [(i, i ^ bit) for i in range(dp_count)]))
        bit //= 2
    bits = []
    while count < dp_count:
        bits.append(count)
        count *= 2
    middle = held.shape[1] // (2 * TILE) * TILE
    halves = [held[0, :middle], held[0, middle:]]
    for number in range(len(bits)):
        for side, bit in enumerate((bits[number], bits[-1 - number])):
            moved = lax.ppermute(
                halves[side], "dp", [(i, i - bit) for i in range(dp_count) if i & bit]
            )
            halves[side] = add_low(halves[side], moved)
    return jnp.concatenate(halves, axis=0)


def blocks_of_code(block):
    count = lax.axis_size("code")
    return [block] + [
        lax.ppermute(block, "code", [(i, (i + step) % count) for i in range(count)])
        for step in range(1, count)
    ]


def side_kernel(code_ref, *refs):
    blocks, out_ref = refs[:-1], refs[-1]
    count, width = len(blocks), blocks[0].shape[1]
    for code in range(count):

        @pl.when(code_ref[0] == code)
        def _():
            for source in range(count):
                out_ref[:, source * width : (source + 1) * width] = blocks[
                    (code - source) % count
                ][...]


def side_by_side(block, code_index):
    blocks = blocks_of_code(block)
    rows, width = block.shape
    return pl.pallas_call(
        side_kernel,
        in_specs=[pl.BlockSpec(memory_space=pltpu.SMEM)]
        + [pl.BlockSpec(memory_space=pltpu.VMEM)] * len(blocks),
        out_specs=pl.BlockSpec(memory_space=pltpu.VMEM),
        out_shape=jax.ShapeDtypeStruct((rows, width * len(blocks)), block.dtype),
    )(jnp.full((1,), code_index, jnp.int32), *blocks)


def sum_over(value, axis):
    count = lax.axis_size(axis)
    if count & (count - 1):
        return lax.psum(value, axis)
    bit = 1
    while bit < count:
        value = value + lax.ppermute(value, axis, [(i, i ^ bit) for i in range(count)])
        bit *= 2
    return value


def sum_over_all(value):
    count = lax.axis_size("dp") * lax.axis_size("code")
    sent = jnp.broadcast_to(value[None], (count,) + value.shape)
    return jnp.sum(lax.all_to_all(sent, ("dp", "code"), 0, 0), axis=0)


def norm_forward(before, norm_gain, norm_shift):
    centred = before - jnp.mean(before, axis=-1, keepdims=True)
    inv_std = lax.rsqrt(jnp.mean(centred * centred, axis=-1, keepdims=True) + NORM_EPSILON)
    normed = centred * inv_std
    return (normed * norm_gain + norm_shift, normed, inv_std)


def norm_backward(upstream, normed, inv_std, norm_gain):
    scaled = upstream * norm_gain
    centred_grad = (
        scaled
        - jnp.mean(scaled, axis=-1, keepdims=True)
        - normed * jnp.mean(scaled * normed, axis=-1, keepdims=True)
    )
    return (
        centred_grad * inv_std,
        jnp.sum(upstream * normed, axis=0),
        jnp.sum(upstream, axis=0),
    )


def gelu(pre_act):
    return 0.5 * pre_act * (1.0 + lax.erf(pre_act * 0.7071067811865476))


def gelu_grad(pre_act):
    return (
        0.5 * (1.0 + lax.erf(pre_act * 0.7071067811865476))
        + pre_act * jnp.exp(-0.5 * pre_act * pre_act) * 0.3989422804014327
    )


def vec_part(vector, slot_index):
    return vector[slot_index * D : (slot_index + 1) * D]


def gate_maps():
    rows = (np.arange(D)[:, None] % HEAD_DIM == np.arange(HEAD_DIM)[None, :]).astype(np.float32)
    groups = np.arange(8)[:, None] // 4 == np.arange(2 * HEADS)[None, :] // HEADS
    own = np.arange(D)[:, None] // HEAD_DIM == np.arange(2 * HEADS)[None, :] % HEADS
    return rows, groups.astype(np.float32), own.astype(np.float32)


def exact_dot(left, right, dims=((1,), (0,))):
    return lax.dot_general(left, right, (dims, ((), ())), precision=HIGHEST)


def gate_columns(gate_weight):
    rows, groups, own = gate_maps()
    wide = gate_weight.astype(F32)
    sums = exact_dot(wide, jnp.asarray(groups))
    return exact_dot(jnp.asarray(rows), sums[:HEAD_DIM]) * own, sums[HEAD_DIM:]


def gate_forward(in_low, weights):
    columns, bias = weights["gate_columns"]
    high = columns.astype(BF)
    rest = (columns - high.astype(F32)).astype(BF)
    logit = dot_nn(in_low, jnp.concatenate([high, rest], axis=1))
    logit = logit[:, : 2 * HEADS] + logit[:, 2 * HEADS :] + bias
    pair = jax.nn.sigmoid(logit)
    first, second = pair[:, :HEADS], pair[:, HEADS:]
    gate_vals = first * (second * weights["gate_scale"].astype(F32) - 1.0) + 2.0
    return (gate_vals, first, second)


def gate_backward(grad_gate, first, second, in_low, weights):
    scale_vec = weights["gate_scale"].astype(F32)
    grad_scale = jnp.sum(grad_gate * first * second, axis=0)
    grad_one = grad_gate * (second * scale_vec - 1.0) * first * (1.0 - first)
    grad_two = grad_gate * first * scale_vec * second * (1.0 - second)
    both = jnp.concatenate([grad_one, grad_two], axis=1)
    rows, groups, own = gate_maps()
    high = both.astype(BF)
    rest = (both - high.astype(F32)).astype(BF)
    product = dot_tn(in_low, jnp.concatenate([high, rest], axis=1))
    product = (product[:, : 2 * HEADS] + product[:, 2 * HEADS :]) * own
    summed = exact_dot(jnp.asarray(rows), product, ((0,), (0,)))
    summed = jnp.concatenate([summed, jnp.sum(both, axis=0, keepdims=True)], axis=0)
    grad_proj = exact_dot(summed, jnp.asarray(groups), ((1,), (1,)))
    grad_heads = exact_dot(both, weights["gate_columns"][0], ((1,), (1,)))
    return (grad_heads, grad_proj, grad_scale)


def layer_forward(hidden, fill, weights, span, pick):
    vector = weights["layer_vec"].astype(F32)
    in_low = hidden.astype(BF)
    qkv_proj = dot_nn(in_low, weights["w_qkv"])
    query_low = ((qkv_proj[:, :D] + vec_part(vector, 0)) * HEAD_DIM ** (-0.5)).astype(BF)
    key_low = qkv_proj[:, D : 2 * D].astype(BF)
    value_low = (qkv_proj[:, 2 * D :] + vec_part(vector, 1)).astype(BF)
    gate_vals, first, second = gate_forward(in_low, weights)
    gate_wide = jnp.pad(jnp.transpose(gate_vals), ((0, 16 - HEADS), (0, 0)))
    attended, lse, bias = attention_forward(
        query_low, key_low, value_low, gate_wide, span, fill, pick
    )
    attn_out = dot_nn(attended, weights["w_out"]) + vec_part(vector, 2)
    mid_rows, normed_one, inv_one = norm_forward(
        DEEP_ALPHA * hidden + attn_out, vec_part(vector, 3), vec_part(vector, 4)
    )
    mid_low = mid_rows.astype(BF)
    pre_act = dot_nn(mid_low, weights["w_up"]) + vector[8 * D :]
    act_low = gelu(pre_act).astype(BF)
    ffn_out = dot_nn(act_low, weights["w_down"]) + vec_part(vector, 5)
    final_rows, normed_two, inv_two = norm_forward(
        DEEP_ALPHA * mid_rows + ffn_out, vec_part(vector, 6), vec_part(vector, 7)
    )
    kept = (in_low, query_low, key_low, value_low, gate_wide, first, second, lse, attended, bias)
    kept += (mid_low, pre_act, act_low, normed_one, inv_one, normed_two, inv_two)
    return (final_rows, kept)


def layer_backward(upstream, kept, fill, weights, span, pick, grad_of):
    in_low, query_low, key_low, value_low, gate_wide, first, second, lse, attended, bias = kept[:10]
    mid_low, pre_act, act_low, normed_one, inv_one, normed_two, inv_two = kept[10:]
    vector = weights["layer_vec"].astype(F32)
    grad_res_two, grad_gain_two, grad_shift_two = norm_backward(
        upstream, normed_two, inv_two, vec_part(vector, 6)
    )
    ffn_low = grad_res_two.astype(BF)
    grad_down = grad_of("w_down", act_low, ffn_low, 512)
    grad_pre = dot_nt(ffn_low, weights["w_down"]) * gelu_grad(pre_act)
    pre_low = grad_pre.astype(BF)
    grad_up = grad_of("w_up", mid_low, pre_low, 256)
    grad_mid = DEEP_ALPHA * grad_res_two + dot_nt(pre_low, weights["w_up"])
    grad_res_one, grad_gain_one, grad_shift_one = norm_backward(
        grad_mid, normed_one, inv_one, vec_part(vector, 3)
    )
    out_low = grad_res_one.astype(BF)
    grad_out = grad_of("w_out", attended, out_low, 384)
    grad_att = dot_nt(out_low, weights["w_out"]).astype(BF)
    grad_q, grad_k, grad_v, part_sums, grad_gate, grad_span = attention_backward(
        query_low, key_low, value_low, grad_att, gate_wide, span, fill, lse, pick, bias
    )
    grad_heads, grad_gate_proj, grad_gate_scale = gate_backward(
        jnp.transpose(grad_gate[:HEADS]), first, second, in_low, weights
    )
    proj_low = jnp.concatenate([grad_q, grad_k, grad_v], axis=1)
    grad_qkv = grad_of("w_qkv", in_low, proj_low, 256)
    grad_hidden = DEEP_ALPHA * grad_res_one + dot_nt(proj_low, weights["w_qkv"]) + grad_heads
    grad_vec = jnp.concatenate(
        [
            part_sums[0],
            part_sums[1],
            jnp.sum(grad_res_one, axis=0),
            grad_gain_one,
            grad_shift_one,
            jnp.sum(grad_res_two, axis=0),
            grad_gain_two,
            grad_shift_two,
            jnp.sum(grad_pre, axis=0),
        ]
    )
    grad_map = {
        "w_qkv": grad_qkv,
        "w_out": grad_out,
        "w_up": grad_up,
        "w_down": grad_down,
        "layer_vec": grad_vec,
        "gate_proj": grad_gate_proj,
        "gate_scale": grad_gate_scale,
    }
    return (grad_hidden, grad_map, grad_span)


def head_kernel(
    in_ref, weight_ref, code_ref, name_ref, target_ref, loss_ref, rows_ref, flat_ref, low_ref
):
    weight, codebook, names = weight_ref[...], code_ref[...], name_ref[0:1, :]
    loss = jnp.zeros((1, 1), F32)
    for low in range(0, in_ref.shape[0], BLOCK):
        rows = slice(low, low + BLOCK)
        projected = dot_nn(in_ref[rows, :], weight)
        inv_len = lax.rsqrt(jnp.sum(projected * projected, axis=1, keepdims=True) + UNIT_EPSILON)
        unit_rows = projected * inv_len
        logits = LOGIT_SCALE * dot_nt(unit_rows.astype(BF), codebook)
        target = target_ref[rows, 0:1]
        live = jnp.where(target >= 0, 1.0, 0.0)
        hits = jnp.where(names == target, 1.0, 0.0)
        top = jnp.max(logits, axis=1, keepdims=True)
        weights = jnp.exp(logits - top)
        total = jnp.sum(weights, axis=1, keepdims=True)
        picked = jnp.sum(logits * hits, axis=1, keepdims=True)
        loss += jnp.sum((top + jnp.log(total) - picked) * live, axis=0, keepdims=True)
        grad_logits = (weights * (1.0 / total) - hits) * (live * LOGIT_SCALE)
        grad_unit = dot_nn(grad_logits.astype(BF), codebook)
        grad_proj = (
            grad_unit - unit_rows * jnp.sum(unit_rows * grad_unit, axis=1, keepdims=True)
        ) * inv_len
        proj_low = grad_proj.astype(BF)
        low_ref[rows, :] = proj_low
        rows_ref[rows, :] = dot_nt(proj_low, weight)
    loss_ref[...] = jnp.broadcast_to(loss, loss_ref.shape)
    grad = dot_tn(in_ref[...], low_ref[...])
    strips = PROJ // 128
    for strip in range(strips):
        flat_ref[pl.ds(strip, D, stride=strips), :] = grad[:, strip * 128 : (strip + 1) * 128]


def head_pass(hidden, w_head, codebook, codes, target_codes):
    targets = jnp.broadcast_to(target_codes[:, None], (ROWS, 128))
    names = jnp.broadcast_to(codes, (8, codes.shape[1]))
    loss, grad_rows, grad_head = pl.pallas_call(
        head_kernel,
        out_shape=[
            jax.ShapeDtypeStruct((8, 128), F32),
            jax.ShapeDtypeStruct((ROWS, D), F32),
            jax.ShapeDtypeStruct((D * PROJ // 128, 128), F32),
        ],
        scratch_shapes=[pltpu.VMEM((ROWS, PROJ), BF)],
        compiler_params=pltpu.CompilerParams(vmem_limit_bytes=VMEM_LIMIT),
    )(hidden.astype(BF), w_head, codebook, names, targets)
    return (loss[0, 0], grad_rows, grad_head)


def local(
    patches,
    lengths,
    patch_masks,
    targets,
    codebook,
    params,
    first_moment,
    second_moment,
    step_count,
):
    dp_count = lax.axis_size("dp")
    code_count = lax.axis_size("code")
    code_index = lax.axis_index("code")
    shard_len = params.shape[0]
    shard_rows = shard_len // 128
    dp_index = lax.axis_index("dp")
    geometry = Geometry(dp_count, code_count, shard_rows)
    own_offset = lax.rem((dp_index * code_count + code_index) * shard_rows + geometry.phase, TILE)
    own_window = lax.dynamic_update_slice(
        jnp.zeros((geometry.window, 128), F32), params.reshape(shard_rows, 128), (own_offset, 0)
    ).astype(BF)
    windows = lax.all_gather(own_window, ("dp", "code"), axis=0, tiled=False)
    where = starts()

    def values(seg_name):
        extent = dict(layout())[seg_name]
        begin, amount = where[seg_name], math.prod(extent)
        low, high = begin // 128, -(-(begin + amount) // 128)
        found = geometry.exact(windows, low, high).reshape(-1)
        return found[begin - low * 128 : begin - low * 128 + amount].reshape(extent)

    w_patch = values("w_patch")
    glob_vec = values("glob_vec").astype(F32)
    gate_proj = values("gate_proj")
    gate_scale = values("gate_scale")
    rel_table = values("rel_table")
    w_head = values("w_head")
    layer_vec = values("layer_vec")
    conv_weight = unpack_conv(geometry, windows, code_index)
    weights = []
    for index in range(LAYERS):
        mats = unpack(
            geometry,
            windows,
            [
                (geometry.place("w_qkv", index), D, 3 * D // 128, 128),
                (geometry.place("w_out", index), D, D // 128, 384),
                (geometry.place("w_up", index), D, FF // 128, 128),
                (geometry.place("w_down", index), FF, D // 128, 512),
            ],
        )
        weights.append(
            dict(zip(("w_qkv", "w_out", "w_up", "w_down"), mats))
            | {
                "layer_vec": layer_vec[index],
                "gate_columns": gate_columns(gate_proj[index]),
                "gate_scale": gate_scale[index],
            }
        )

    places = jnp.arange(ROWS, dtype=jnp.int32)
    mask_row = jnp.pad(patch_masks[0], (0, ROWS - LONG))
    live_slot = places < jnp.minimum(lengths[0], LONG)
    visible = live_slot & (mask_row == 0)
    rank = jnp.cumsum(visible.astype(jnp.int32)) - 1
    pick = (
        visible[None, :] & (rank[None, :] == jnp.arange(SEEN, dtype=jnp.int32)[:, None])
    )
    pick_low = pick.astype(BF)
    near = jnp.sum(pick_low.reshape(SEEN, ROWS // BLOCK, BLOCK), axis=1)
    hop = jnp.sum(pick.astype(F32).reshape(SEEN, ROWS // BLOCK, BLOCK), axis=2)
    pick_seen = (pick_low, near, jnp.pad(hop, ((0, 0), (0, BLOCK - ROWS // BLOCK))))
    pick_full = pick.astype(F32)
    seen_valid = jnp.arange(SEEN, dtype=jnp.int32) < lengths[0] // 4
    seen_fill = jnp.broadcast_to(jnp.where(seen_valid, 0.0, MASK_FILL)[:, None], (SEEN, BLOCK))
    live_fill = jnp.broadcast_to(jnp.where(live_slot, 0.0, MASK_FILL)[:, None], (ROWS, BLOCK))
    live_float = live_slot.astype(F32)[:, None]
    span_table = span_onehot()
    span = dot_tn(
        jnp.pad(rel_table, ((0, 0), (0, 16 - HEADS))), jnp.asarray(span_table.T, BF)
    )

    all_codes = jnp.concatenate(blocks_of_code(codebook), axis=0)
    code_places = (
        code_index - jnp.arange(code_count, dtype=jnp.int32) + code_count
    ) % code_count * codebook.shape[0]
    code_names = (
        code_places[:, None] + jnp.arange(codebook.shape[0], dtype=jnp.int32)[None, :]
    ).reshape(1, -1)
    patch_rows = jnp.pad(patches[0], ((0, ROWS - LONG), (0, 0)))
    embedded = dot_nn(patch_rows, w_patch)
    normed_rows, normed_zero, inv_zero = norm_forward(embedded, glob_vec[0], glob_vec[1])
    start_rows = normed_rows * live_float
    conv_in = start_rows.astype(BF)
    width = D // code_count
    own_cols = code_index * width
    own_in = lax.dynamic_slice_in_dim(conv_in, own_cols, width, 1)
    half = KERNEL // 2
    conv_own = conv_call(conv_forward_kernel, own_in[:LONG], conv_weight, half, False)
    seen_own = lax.dot_general(
        pick_full, conv_own, (((1,), (0,)), ((), ())), precision=HIGHEST
    )
    seen_raw = side_by_side(seen_own, code_index)
    seen_pre = seen_raw + glob_vec[2]
    seen_start = lax.dot_general(
        pick_full, start_rows, (((1,), (0,)), ((), ())), precision=HIGHEST
    )
    seen_rows = seen_start + gelu(seen_pre)
    encoded, kept_first = layer_forward(seen_rows, seen_fill, weights[0], span, pick_seen)
    placed = lax.dot_general(
        pick_full, encoded, (((0,), (0,)), ((), ())), precision=HIGHEST
    )
    hidden = jnp.where(visible[:, None], placed, glob_vec[3])
    final, kept_second = layer_forward(hidden, live_fill, weights[1], span, None)
    target_codes = jnp.where(mask_row == 1, jnp.pad(targets[0], (0, ROWS - LONG)), -1)
    loss_local, upstream, grad_head = head_pass(final, w_head, all_codes, code_names, target_codes)

    def grad_maker(index):
        return lambda seg_name, left, right, rows: weight_grad(
            left, right, geometry, code_index, geometry.place(seg_name, index), rows
        )

    upstream, map_second, span_second = layer_backward(
        upstream, kept_second, live_fill, weights[1], span, None, grad_maker(1)
    )
    grad_mask_emb = jnp.sum(jnp.where(visible[:, None], 0.0, upstream), axis=0)
    grad_encoded = lax.dot_general(
        pick_full, upstream, (((1,), (0,)), ((), ())), precision=HIGHEST
    )
    grad_seen, map_first, span_first = layer_backward(
        grad_encoded, kept_first, seen_fill, weights[0], span, pick_seen, grad_maker(0)
    )
    grad_seen = grad_seen * seen_valid[:, None].astype(F32)
    grad_conv_seen = grad_seen * gelu_grad(seen_pre)
    grad_conv = dot_tn(pick_low, grad_conv_seen.astype(BF)).astype(BF)
    grad_full = lax.dot_general(
        pick_full, grad_seen, (((0,), (0,)), ((), ())), precision=HIGHEST
    )
    own_grad = lax.dynamic_slice_in_dim(grad_conv, own_cols, width, 1)
    grad_in_own = conv_call(conv_input_kernel, own_grad[:LONG], conv_weight, half - 1, True)
    grad_conv_in = side_by_side(grad_in_own.astype(BF), code_index)
    split = front_slots(geometry)
    padded, grads = conv_weight_inputs(conv_in[:LONG], grad_conv)
    rest_grad = conv_weight_grad(padded, grads, geometry, code_index, range(split, dp_count))
    grad_start = (grad_full + grad_conv_in.astype(F32)) * live_float
    grad_embedded, grad_gain_zero, grad_shift_zero = norm_backward(
        grad_start, normed_zero, inv_zero, glob_vec[0]
    )
    grad_patch = dot_tn(patch_rows, grad_embedded.astype(BF))
    grad_glob = jnp.stack(
        [grad_gain_zero, grad_shift_zero, jnp.sum(grad_conv_seen, axis=0), grad_mask_emb]
    )
    grad_rel = lax.dot_general(
        jnp.asarray(span_table),
        (span_first + span_second)[:HEADS],
        (((0,), (1,)), ((), ())),
        precision=HIGHEST,
    )
    leader = (code_index == 0).astype(F32)
    count_local = jnp.sum((target_codes >= 0).astype(F32))
    early = jnp.concatenate(
        [
            (grad_rel * leader).reshape(-1, 128),
            jnp.full((1, 128), loss_local * leader),
            jnp.full((1, 128), count_local * leader),
        ]
    )
    early = sum_over(sum_over(jnp.pad(early, ((0, -early.shape[0] % 8), (0, 0))), "dp"), "code")
    both = (map_first, map_second)
    sources, spans = [], [[] for _ in range(code_count)]

    def add_source(found):
        array, (chunks, base, unit, chunk) = found
        for code, items in enumerate(chunk_spans(chunks, base, unit, chunk, len(sources))):
            spans[code] += items
        sources.append(array)

    for seg_name in ("w_qkv", "w_out", "w_up", "w_down"):
        for layer_map in both:
            add_source(layer_map[seg_name])
    add_source(rest_grad)
    tail_place = geometry.place("layer_vec")
    vec_rows = jnp.concatenate(
        [layer_map["layer_vec"].reshape(-1, 128) for layer_map in both], axis=0
    )
    small = [layer_map[seg_name] for seg_name in ("gate_proj", "gate_scale") for layer_map in both]
    small = jnp.concatenate([part.reshape(-1) for part in small + [grad_rel]])
    lead = small.shape[0] % 128
    small_rows = jnp.pad(small, (0, -small.shape[0] % 128)).reshape(-1, 128)
    head_rows = jnp.pad(grad_head, ((1, 1), (0, 0)))
    head_rows = jnp.concatenate(
        [head_rows[:-1, 128 - lead :], head_rows[1:, : 128 - lead]], axis=1
    )
    whole = small.shape[0] // 128
    tail = jnp.concatenate(
        [vec_rows, small_rows[:whole], small_rows[whole:] + head_rows[:1], head_rows[1:]], axis=0
    ).astype(BF)
    tail_rows = geometry.begins[-1] + geometry.window - tail_place
    tail = jnp.pad(tail, ((0, tail_rows - tail.shape[0]), (0, 0)))
    for items in spans:
        items.append((tail_place, tail_rows, len(sources), 0))
    sources.append(tail)
    front = jnp.concatenate([grad_patch.reshape(-1, 128), grad_glob.reshape(-1, 128)], axis=0)
    front = jnp.pad(front, ((geometry.phase, 0), (0, 0))).astype(BF)
    if split:
        own_part = pack(geometry, code_index, sources, spans, split, dp_count)
        reduced = lax.psum_scatter(own_part, "dp", scatter_dimension=0, tiled=False)
        sources, spans = [], [[] for _ in range(code_count)]
        add_source(conv_weight_grad(padded, grads, geometry, code_index, range(split)))
    for items in spans:
        items.append((0, front.shape[0], len(sources), 0))
    front, early = lax.optimization_barrier((front, early))
    sources.append(front)
    last_part = pack(geometry, code_index, sources, spans, 0, split or dp_count)
    if split:
        first = reduce_front(last_part, dp_count, dp_index)
        reduced = jnp.where(dp_index < split, first, reduced)
    else:
        reduced = lax.psum_scatter(last_part, "dp", scatter_dimension=0, tiled=False)
    reduced = lax.dynamic_slice(reduced.astype(F32), (own_offset, 0), (shard_rows, 128))
    reduced = reduced.reshape(shard_len)
    squares_all = sum_over_all(jnp.full((8, 128), jnp.sum(reduced * reduced)))
    squares_all = squares_all[0, 0]
    rel_rows = BUCKETS * HEADS // 128
    rel_all = early[:rel_rows].reshape(BUCKETS, HEADS)
    loss_all, count_all = early[rel_rows, 0], early[rel_rows + 1, 0]
    grad_norm = jnp.sqrt(squares_all) / count_all
    clip_factor = jnp.minimum(1.0, CLIP_NORM / grad_norm)
    clipped = reduced / count_all * clip_factor
    rel_grad = rel_all / count_all * clip_factor
    step_value = step_count[0].astype(F32)
    new_first = BETA_ONE * first_moment + (1.0 - BETA_ONE) * clipped
    new_second = BETA_TWO * second_moment + (1.0 - BETA_TWO) * clipped * clipped
    first_hat = new_first / (1.0 - BETA_ONE**step_value)
    second_hat = new_second / (1.0 - BETA_TWO**step_value)
    new_params = params - LEARN_RATE * (
        first_hat / (jnp.sqrt(second_hat) + ADAM_EPSILON) + WEIGHT_DECAY * params
    )
    return (
        new_params,
        new_first,
        new_second,
        new_params.astype(BF),
        loss_all / count_all,
        grad_norm,
        rel_grad,
    )


def solution(mesh):
    placed = (
        P("dp", None, None),
        P("dp"),
        P("dp", None),
        P("dp", None),
        P("code", None),
        P(("dp", "code")),
        P(("dp", "code")),
        P(("dp", "code")),
        P(),
    )
    return jax.shard_map(
        local,
        mesh=mesh,
        in_specs=placed,
        out_specs=(
            P(("dp", "code")),
            P(("dp", "code")),
            P(("dp", "code")),
            P(("dp", "code")),
            P(),
            P(),
            P(),
        ),
        check_vma=False,
    )
```

```python
import functools
import math

import jax
import jax.numpy as jnp
import numpy as np
from jax import lax
from jax.experimental import pallas as pl
from jax.experimental.pallas import tpu as pltpu
from jax.sharding import PartitionSpec as P

D = 768
HEADS = 12
HEAD_DIM = 64
FF = 3072
PATCH_IN = 256
PROJ = 256
KERNEL = 128
GROUPS = 16
WIDTH = D // GROUPS
BUCKETS = 320
MAX_DIST = 800
LAYERS = 2
LONG = 496
VISIBLE = 124
ROWS = 512
SEEN = 128
SPAN = 1024

NORM_EPSILON = 1e-05
UNIT_EPSILON = 1e-06
DEEP_ALPHA = 2.2133638394006434
LOGIT_SCALE = 25.0
CLIP_NORM = 0.005
LEARN_RATE = 0.02
BETA_ONE = 0.9
BETA_TWO = 0.999
ADAM_EPSILON = 1e-10
WEIGHT_DECAY = 0.01
MASK_FILL = -1000000000.0
HIGHEST = lax.Precision.HIGHEST
BF = jnp.bfloat16
F32 = jnp.float32
VMEM_LIMIT = 56 << 20


def layout():
    return [
        ("w_patch", (PATCH_IN, D)),
        ("glob_vec", (4, D)),
        ("conv_w", (KERNEL, WIDTH, D)),
        ("w_qkv", (LAYERS, D, 3 * D)),
        ("w_out", (LAYERS, D, D)),
        ("w_up", (LAYERS, D, FF)),
        ("w_down", (LAYERS, FF, D)),
        ("layer_vec", (LAYERS, 8 * D + FF)),
        ("gate_proj", (LAYERS, HEAD_DIM + 1, 8)),
        ("gate_scale", (LAYERS, HEADS)),
        ("rel_table", (BUCKETS, HEADS)),
        ("w_head", (D, PROJ)),
    ]


def starts():
    where = {}
    offset = 0
    for seg_name, extent in layout():
        where[seg_name] = offset
        offset += math.prod(extent)
    return where


TILE = 16


class Geometry:
    def __init__(self, dp_count, code_count, shard_rows):
        self.dp_count, self.code_count, self.shard_rows = dp_count, code_count, shard_rows
        self.shards = dp_count * code_count
        self.phase = -(starts()["conv_w"] // 128) % TILE
        self.window = -(-(shard_rows + TILE - 1) // TILE) * TILE
        self.begins = [(shard_rows * s + self.phase) // TILE * TILE for s in range(self.shards)]
        self.offsets = [(shard_rows * s + self.phase) % TILE for s in range(self.shards)]

    def place(self, seg_name, index=0):
        extent = dict(layout())[seg_name]
        amount = math.prod(extent[1:]) if index else 0
        return (starts()[seg_name] + index * amount) // 128 + self.phase

    def pieces(self, low, high):
        main, edges = [], []
        row = low
        while row < high:
            shard = max(s for s in range(self.shards) if self.begins[s] <= row)
            begin = self.begins[shard]
            if row == begin and shard > 0 and self.offsets[shard]:
                main.append((shard - 1, row - self.begins[shard - 1], row - low, TILE))
                edges.append((shard, row - low))
                row += TILE
                continue
            stop = self.begins[shard + 1] if shard + 1 < self.shards else high
            count = min(stop, high) - row
            main.append((shard, row - begin, row - low, count))
            row += count
        merged = []
        for item in main:
            last = merged[-1] if merged else None
            if last and last[0] == item[0] and last[1] + last[3] == item[1]:
                merged[-1] = last[:3] + (last[3] + item[3],)
            else:
                merged.append(item)
        return merged, edges


def bucket_onehot():
    offsets = np.arange(-(LONG - 1), LONG)
    half_count = BUCKETS // 2
    exact_count = half_count // 2
    distance = np.abs(offsets)
    scaled = (
        np.log(np.maximum(distance, 1) / exact_count)
        / np.log(MAX_DIST / exact_count)
        * (half_count - exact_count)
    )
    larger = np.minimum(exact_count + np.maximum(scaled, 0.0).astype(np.int64), half_count - 1)
    bucket = (offsets > 0) * half_count + np.where(distance < exact_count, distance, larger)
    return (bucket[:, None] == np.arange(BUCKETS)[None, :]).astype(np.float32)


def span_onehot():
    shift = SPAN // 2 - (LONG - 1)
    table = np.zeros((SPAN, BUCKETS), np.float32)
    table[shift : shift + 2 * LONG - 1] = bucket_onehot()[::-1]
    return table


def params_of(grid_rank=1):
    return pltpu.CompilerParams(
        dimension_semantics=("arbitrary",) * grid_rank, vmem_limit_bytes=VMEM_LIMIT
    )


def dot_nn(left, right):
    return lax.dot_general(left, right, (((1,), (0,)), ((), ())), preferred_element_type=F32)


def dot_nt(left, right):
    return lax.dot_general(left, right, (((1,), (1,)), ((), ())), preferred_element_type=F32)


def dot_tn(left, right):
    return lax.dot_general(left, right, (((0,), (0,)), ((), ())), preferred_element_type=F32)


TAPS = 16


def lane_masks(width):
    group = np.arange(width)[None, :] // WIDTH
    return (group == np.arange(width // WIDTH)[:, None]).astype(np.float32)


def shifted_taps(source_ref, target_ref, count):
    width = source_ref.shape[1]
    for tap in range(TAPS):
        target_ref[:, tap * width : (tap + 1) * width] = source_ref[tap : tap + count, :].astype(BF)


def conv_forward_kernel(in_ref, weight_ref, mask_ref, out_ref, taps_ref, block_ref):
    step = pl.program_id(0)
    width = weight_ref.shape[1]

    @pl.when(step == 0)
    def _():
        shifted_taps(in_ref, taps_ref, taps_ref.shape[0])
        block_ref[...] = jnp.zeros_like(block_ref)

    for tap in range(TAPS):
        piece = weight_ref[tap * WIDTH : (tap + 1) * WIDTH, :]
        for group in range(width // WIDTH):
            low = tap * width + group * WIDTH
            block_ref[low : low + WIDTH, :] = piece * mask_ref[group : group + 1, :]
    begin = pl.multiple_of(step * TAPS, TAPS)
    term = dot_nn(taps_ref[pl.ds(begin, ROWS), :], block_ref[...])

    @pl.when(step == 0)
    def _():
        out_ref[...] = term

    @pl.when(step > 0)
    def _():
        out_ref[...] += term


def conv_input_kernel(in_ref, weight_ref, mask_ref, out_ref, taps_ref, block_ref):
    step = pl.program_id(0)
    width = weight_ref.shape[1]

    @pl.when(step == 0)
    def _():
        shifted_taps(in_ref, taps_ref, taps_ref.shape[0])
        block_ref[...] = jnp.zeros_like(block_ref)

    for tap in range(TAPS):
        piece = weight_ref[tap * WIDTH : (tap + 1) * WIDTH, :]
        low = (TAPS - 1 - tap) * width
        for group in range(width // WIDTH):
            block_ref[group * WIDTH : (group + 1) * WIDTH, low : low + width] = (
                piece * mask_ref[group : group + 1, :]
            )
    begin = pl.multiple_of((pl.num_programs(0) - 1 - step) * TAPS, TAPS)
    term = dot_nt(taps_ref[pl.ds(begin, ROWS), :], block_ref[...])

    @pl.when(step == 0)
    def _():
        out_ref[...] = term

    @pl.when(step > 0)
    def _():
        out_ref[...] += term


def conv_call(kernel, conv_in, weight, front, nt):
    width = weight.shape[1]
    steps = KERNEL // TAPS
    count = ROWS + KERNEL - TAPS
    padded = jnp.pad(
        conv_in.astype(F32),
        ((front, count + TAPS - front - conv_in.shape[0]), (0, 0)),
    )
    block = (width, TAPS * width) if nt else (TAPS * width, width)
    return pl.pallas_call(
        kernel,
        grid=(steps,),
        in_specs=[
            pl.BlockSpec(padded.shape, lambda i: (0, 0)),
            pl.BlockSpec((TAPS * WIDTH, width), lambda i: (i, 0)),
            pl.BlockSpec((width // WIDTH, width), lambda i: (0, 0)),
        ],
        out_specs=pl.BlockSpec((ROWS, width), lambda i: (0, 0)),
        out_shape=jax.ShapeDtypeStruct((ROWS, width), F32),
        scratch_shapes=[pltpu.VMEM((count, TAPS * width), BF), pltpu.VMEM(block, BF)],
        compiler_params=params_of(),
    )(padded, weight, jnp.asarray(lane_masks(width), BF))


CHUNK = 6


def conv_weight_kernel(tap_ref, in_ref, grad_ref, mask_ref, out_ref, taps_ref, turn_ref):
    parts = in_ref.shape[0]
    begin = tap_ref[pl.program_id(0)]
    strips = D // 128
    rows = CHUNK * WIDTH
    for part in range(parts):
        turned = pltpu.roll(in_ref[part], in_ref.shape[2] - begin, 1)
        for tap in range(CHUNK):
            taps_ref[part, tap * PART : (tap + 1) * PART, :] = turned[:, tap : tap + ROWS].astype(
                BF
            )
    sums = []
    for part in range(parts):
        term = dot_nn(taps_ref[part], grad_ref[part])
        pieces = []
        for tap in range(CHUNK):
            total = None
            for group in range(mask_ref.shape[0]):
                low = tap * PART + group * WIDTH
                piece = term[low : low + WIDTH, :] * mask_ref[group : group + 1, :]
                total = piece if total is None else total + piece
            pieces.append(total)
        sums.append(jnp.concatenate(pieces, axis=0))
    for strip in range(strips):
        part, low = divmod(strip * 128, PART)
        columns = sums[part][:, low : min(low + 128, PART)]
        if low + 128 > PART:
            columns = jnp.concatenate([columns, sums[part + 1][:, : low + 128 - PART]], axis=1)
        turn_ref[pl.ds(strip, rows, stride=strips), :] = columns
    out_ref[...] = turn_ref[...].astype(BF)


PART = 4 * WIDTH


def owned_chunks(geometry, base, unit, count, chunk, step, slots):
    tables = []
    for code in range(geometry.code_count):
        found = []
        for slot in slots:
            begin = geometry.begins[slot * geometry.code_count + code] - base
            low = max(begin // unit, 0) // step * step
            high = min(-(-(begin + geometry.window) // unit), count)
            while low < high:
                found.append(min(low, count - chunk))
                low += chunk
        tables.append(list(dict.fromkeys(found)))
    most = max([1] + [len(table) for table in tables])
    return [(table or [0]) + (table or [0])[-1:] * (most - max(len(table), 1)) for table in tables]


def chunk_spans(chunks, base, unit, chunk, source):
    return [
        [(base + low * unit, chunk * unit, source, n * chunk * unit) for n, low in enumerate(table)]
        for table in chunks
    ]


def chunk_table(chunks, code_index):
    return lax.dynamic_index_in_dim(jnp.asarray(chunks, jnp.int32), code_index, 0, False)


def conv_weight_inputs(conv_in, grad_low):
    parts = D // PART
    front = KERNEL // 2
    padded = jnp.pad(
        jnp.transpose(conv_in).astype(F32),
        ((0, 0), (front, ROWS + KERNEL - front - conv_in.shape[0])),
    ).reshape(parts, PART, ROWS + KERNEL)
    return padded, jnp.transpose(grad_low.reshape(ROWS, parts, PART), (1, 0, 2))


def conv_weight_grad(padded, grads, geometry, code_index, slots):
    parts = D // PART
    masks = jnp.asarray(lane_masks(PART), F32)
    base, unit = geometry.place("conv_w"), WIDTH * D // 128
    chunks = owned_chunks(geometry, base, unit, KERNEL, CHUNK, 1, slots)
    table = chunk_table(chunks, code_index)
    rows = CHUNK * unit
    out = pl.pallas_call(
        conv_weight_kernel,
        grid_spec=pltpu.PrefetchScalarGridSpec(
            num_scalar_prefetch=1,
            grid=(len(chunks[0]),),
            in_specs=[
                pl.BlockSpec(padded.shape, lambda i, t: (0, 0, 0)),
                pl.BlockSpec(grads.shape, lambda i, t: (0, 0, 0)),
                pl.BlockSpec(masks.shape, lambda i, t: (0, 0)),
            ],
            out_specs=pl.BlockSpec((rows, 128), lambda i, t: (i, 0)),
            scratch_shapes=[
                pltpu.VMEM((parts, CHUNK * PART, ROWS), BF),
                pltpu.VMEM((rows, 128), F32),
            ],
        ),
        out_shape=jax.ShapeDtypeStruct((len(chunks[0]) * rows, 128), BF),
        compiler_params=params_of(),
    )(table, padded, grads, masks)
    return out, (chunks, base, unit, CHUNK)


BLOCK = 128


def half_mask(side):
    lane = lax.broadcasted_iota(jnp.int32, (1, BLOCK), 1)
    return jnp.where(lane // HEAD_DIM == side, 1.0, 0.0).astype(BF)


def toeplitz(span_ref, head):
    row = jnp.broadcast_to(span_ref[pl.ds(head, 1), :], (BLOCK, SPAN))
    return pltpu.roll(row, 0, 1, stride=1, stride_axis=0)


def hop_columns(hop):
    return [hop[:, index : index + 1] for index in range(ROWS // BLOCK)]


def seen_biases(turned, pick, near, hop):
    moved = [dot_nn(near, item.astype(BF)) for item in turned]
    columns = [jnp.broadcast_to(column, (SEEN, ROWS)) for column in hop_columns(hop)]
    tables = []
    for item in moved:
        table = None
        for index, column in enumerate(columns):
            low = index * BLOCK
            part = column * item[:, ROWS - low : SPAN - low]
            table = part if table is None else table + part
        tables.append(table.astype(BF))
    return [dot_nt(table, pick) for table in tables]


def wide(column, length):
    return jnp.concatenate([column] * (length // BLOCK), axis=1)


def attention_forward_kernel(
    q_ref, k_ref, v_ref, gate_ref, span_ref, fill_ref, out_ref, lse_ref, score_ref, turn_ref
):
    step = pl.program_id(0)
    length = q_ref.shape[0]
    values = jnp.transpose(v_ref[...])
    sides = range(2)
    turned = [toeplitz(span_ref, step * 2 + side) for side in sides]
    for side in sides:
        score_ref[side] = dot_nt(k_ref[...] * half_mask(side), q_ref[...])
    tops = []
    for side in sides:
        gate = gate_ref[pl.ds(step * 2 + side, 1), :]
        top = None
        for low in range(0, length, BLOCK):
            rows = slice(low, low + BLOCK)
            bias = turned[side][:, ROWS - low : SPAN - low]
            scores = score_ref[side, rows, :] + gate * bias + wide(fill_ref[rows, :], length)
            score_ref[side, rows, :] = scores
            most = jnp.max(scores, axis=0, keepdims=True)
            top = most if top is None else jnp.maximum(top, most)
        tops.append(top)
    totals = []
    for side in sides:
        total = None
        for low in range(0, length, BLOCK):
            rows = slice(low, low + BLOCK)
            weights = jnp.exp(score_ref[side, rows, :] - tops[side])
            part = jnp.sum(weights, axis=0, keepdims=True)
            total = part if total is None else total + part
            turn_ref[side, rows, :] = weights.astype(BF)
        totals.append(total)
    mixed = []
    for side in sides:
        lse_ref[pl.ds(step * 2 + side, 1), :] = tops[side] + jnp.log(totals[side])
        part = dot_nn(values[side * HEAD_DIM : (side + 1) * HEAD_DIM, :], turn_ref[side])
        mixed.append(part * (1.0 / totals[side]))
    out_ref[...] = jnp.transpose(jnp.concatenate(mixed, axis=0)).astype(BF)


SEEN_HEADS = 12


def seen_forward_kernel(
    q_ref, k_ref, v_ref, gate_ref, span_ref, fill_ref, pick_ref, near_ref, hop_ref,
    out_ref, lse_ref, bias_ref,
):
    heads = range(SEEN_HEADS)
    base = pl.program_id(0) * SEEN_HEADS
    pick, near, hop = pick_ref[...], near_ref[...], hop_ref[...]
    pairs = range(SEEN_HEADS // 2)
    query = [q_ref[:, pair * BLOCK : (pair + 1) * BLOCK] for pair in pairs]
    keyv = [k_ref[:, pair * BLOCK : (pair + 1) * BLOCK] for pair in pairs]
    values = [jnp.transpose(v_ref[:, pair * BLOCK : (pair + 1) * BLOCK]) for pair in pairs]
    turned = [toeplitz(span_ref, base + head) for head in heads]
    bias = seen_biases(turned, pick, near, hop)
    scores = [dot_nt(keyv[head // 2] * half_mask(head % 2), query[head // 2]) for head in heads]
    for head in heads:
        bias_ref[head * BLOCK : (head + 1) * BLOCK, :] = bias[head].astype(BF)
    scores = [
        scores[head] + gate_ref[pl.ds(base + head, 1), :] * bias[head] + fill_ref[...]
        for head in heads
    ]
    tops = [jnp.max(item, axis=0, keepdims=True) for item in scores]
    weights = [jnp.exp(scores[head] - tops[head]) for head in heads]
    totals = [jnp.sum(item, axis=0, keepdims=True) for item in weights]
    mixed = []
    for head in heads:
        lse_ref[pl.ds(base + head, 1), :] = tops[head] + jnp.log(totals[head])
        low = (head % 2) * HEAD_DIM
        part = dot_nn(values[head // 2][low : low + HEAD_DIM, :], weights[head].astype(BF))
        mixed.append(part * (1.0 / totals[head]))
    for pair in pairs:
        both = jnp.concatenate(mixed[2 * pair : 2 * pair + 2], axis=0)
        out_ref[:, pair * BLOCK : (pair + 1) * BLOCK] = jnp.transpose(both).astype(BF)


def head_specs(length, heads):
    count = HEADS // heads
    return [
        pl.BlockSpec((length, heads * HEAD_DIM), lambda i, part=part: (0, part * count + i))
        for part in range(3)
    ]


def whole_spec(shape):
    return pl.BlockSpec(shape, lambda i: (0,) * len(shape))


def attention_forward(qkv, gate, span, fill, pick):
    length = qkv.shape[0]
    heads = 2 if pick is None else SEEN_HEADS
    specs = head_specs(length, heads)
    args = [qkv, qkv, qkv, gate, span, fill] + list(pick or ())
    shapes = [
        jax.ShapeDtypeStruct((length, D), BF),
        jax.ShapeDtypeStruct((16, length), F32),
    ]
    out_specs = [specs[0], whole_spec((16, length))]
    scratch = []
    if pick is None:
        kernel = attention_forward_kernel
        scratch = [pltpu.VMEM((2, length, length), F32), pltpu.VMEM((2, length, length), BF)]
    else:
        kernel = seen_forward_kernel
        out_specs.append(pl.BlockSpec((SEEN_HEADS * BLOCK, BLOCK), lambda i: (i, 0)))
        shapes.append(jax.ShapeDtypeStruct((HEADS * BLOCK, BLOCK), BF))
    found = pl.pallas_call(
        kernel,
        grid=(HEADS // heads,),
        in_specs=specs + [whole_spec(a.shape) for a in args[3:]],
        out_specs=out_specs,
        out_shape=shapes,
        scratch_shapes=scratch,
        compiler_params=params_of(),
    )(*args)
    return found[0], found[1], None if pick is None else found[2]


def diagonal_sums(turn):
    half = BLOCK // 2
    while half:
        turn = turn[:half, :] + pltpu.roll(turn[half:, :], SPAN - half, 1)
        half //= 2
    return turn


def attention_backward_kernel(
    q_ref, k_ref, v_ref, up_ref, gate_ref, span_ref, fill_ref, lse_ref,
    out_ref, sum_ref, dgate_ref, dspan_ref, prob_ref, grad_ref, turn_ref, low_ref, diag_ref,
):
    step = pl.program_id(0)
    length = q_ref.shape[0]
    sides = range(2)

    @pl.when(step == 0)
    def _():
        dspan_ref[...] = jnp.zeros_like(dspan_ref)
        dgate_ref[...] = jnp.zeros_like(dgate_ref)

    keys = jnp.transpose(k_ref[...])
    turned = [toeplitz(span_ref, step * 2 + side) for side in sides]
    for side in sides:
        prob_ref[side] = dot_nt(k_ref[...] * half_mask(side), q_ref[...])
        grad_ref[side] = dot_nt(v_ref[...] * half_mask(side), up_ref[...])
        diag_ref[side] = jnp.zeros_like(diag_ref[side])
    shared = []
    for side in sides:
        gate = gate_ref[pl.ds(step * 2 + side, 1), :]
        lse = lse_ref[pl.ds(step * 2 + side, 1), :]
        total = None
        for low in range(0, length, BLOCK):
            rows = slice(low, low + BLOCK)
            bias = turned[side][:, ROWS - low : SPAN - low]
            scores = prob_ref[side, rows, :] + gate * bias + wide(fill_ref[rows, :], length)
            probs = jnp.exp(scores - lse)
            prob_ref[side, rows, :] = probs
            low_ref[side, rows, :] = probs.astype(BF)
            part = jnp.sum(probs * grad_ref[side, rows, :], axis=0, keepdims=True)
            total = part if total is None else total + part
        shared.append(total)
    val_total = sum(dot_nn(low_ref[side], up_ref[...] * half_mask(side)) for side in sides)
    for side in sides:
        gate = gate_ref[pl.ds(step * 2 + side, 1), :]
        dgate = None
        for low in range(0, length, BLOCK):
            rows = slice(low, low + BLOCK)
            bias = turned[side][:, ROWS - low : SPAN - low]
            grad_scores = prob_ref[side, rows, :] * (grad_ref[side, rows, :] - shared[side])
            turn_ref[side, rows, :] = grad_scores.astype(BF)
            part = jnp.sum(grad_scores * bias, axis=0, keepdims=True)
            dgate = part if dgate is None else dgate + part
            diag_ref[side, :, ROWS - low : SPAN - low] += grad_scores * gate
        dgate_ref[pl.ds(step * 2 + side, 1), :] = dgate
    key_total = sum(dot_nn(turn_ref[side], q_ref[...] * half_mask(side)) for side in sides)
    halves = [
        dot_nn(keys[side * HEAD_DIM : (side + 1) * HEAD_DIM, :], turn_ref[side]) for side in sides
    ]
    for side in sides:
        dspan_ref[pl.ds(step * 2 + side, 1), :] = diagonal_sums(diag_ref[side])
    grad_query = jnp.transpose(jnp.concatenate(halves, axis=0)) * HEAD_DIM ** (-0.5)
    for part, value in enumerate((grad_query, key_total, val_total)):
        begin = pl.multiple_of(part * D + step * BLOCK, BLOCK)
        out_ref[:, pl.ds(begin, BLOCK)] = value.astype(BF)
    sum_ref[0:1, :] = jnp.sum(grad_query, axis=0, keepdims=True)
    sum_ref[1:2, :] = jnp.sum(val_total, axis=0, keepdims=True)


def split_low(value):
    high = value.astype(BF)
    return high, (value - high.astype(F32)).astype(BF)


def seen_backward_kernel(
    q_ref, k_ref, v_ref, up_ref, gate_ref, fill_ref, lse_ref, pick_ref, hop_ref, flip_ref,
    bias_ref, out_ref, sum_ref, dgate_ref, dspan_ref, diag_ref,
):
    heads, pairs = range(SEEN_HEADS), range(SEEN_HEADS // 2)
    base = pl.program_id(0) * SEEN_HEADS

    @pl.when(base == 0)
    def _():
        dspan_ref[...] = jnp.zeros_like(dspan_ref)
        dgate_ref[...] = jnp.zeros_like(dgate_ref)

    def pair_of(ref):
        return [ref[:, pair * BLOCK : (pair + 1) * BLOCK] for pair in pairs]

    query, keyv, value, upstream = (pair_of(ref) for ref in (q_ref, k_ref, v_ref, up_ref))
    keys = [jnp.transpose(item) for item in keyv]
    gate = [gate_ref[pl.ds(base + head, 1), :] for head in heads]
    bias = [bias_ref[head * BLOCK : (head + 1) * BLOCK, :].astype(F32) for head in heads]
    scores = [dot_nt(keyv[head // 2] * half_mask(head % 2), query[head // 2]) for head in heads]
    grads = [dot_nt(value[head // 2] * half_mask(head % 2), upstream[head // 2]) for head in heads]
    probs = [
        jnp.exp(
            scores[head]
            + gate[head] * bias[head]
            + fill_ref[...]
            - lse_ref[pl.ds(base + head, 1), :]
        )
        for head in heads
    ]
    shared = [jnp.sum(probs[head] * grads[head], axis=0, keepdims=True) for head in heads]
    moves = [probs[head] * (grads[head] - shared[head]) for head in heads]
    val_terms = [
        dot_nn(probs[head].astype(BF), upstream[head // 2] * half_mask(head % 2)) for head in heads
    ]
    low = [item.astype(BF) for item in moves]
    key_terms = [dot_nn(low[head], query[head // 2] * half_mask(head % 2)) for head in heads]
    halves = [
        dot_nn(keys[head // 2][(head % 2) * HEAD_DIM : (head % 2 + 1) * HEAD_DIM, :], low[head])
        for head in heads
    ]
    for head in heads:
        dgate_ref[pl.ds(base + head, 1), :] = jnp.sum(
            moves[head] * bias[head], axis=0, keepdims=True
        )
    pieces = [jnp.concatenate(split_low(moves[head] * gate[head]), axis=0) for head in heads]
    placed = [dot_nn(piece, pick_ref[...]) for piece in pieces]
    columns = [jnp.broadcast_to(column, (SEEN, ROWS)) for column in hop_columns(hop_ref[...])]
    for head in heads:
        both = placed[head][:BLOCK, :] + placed[head][BLOCK:, :]
        diag_ref[head] = jnp.zeros_like(diag_ref[head])
        for index, column in enumerate(columns):
            begin = ROWS - index * BLOCK
            diag_ref[head, :, begin : begin + ROWS] += column * both
    turns = [
        dot_nn(flip_ref[...], jnp.concatenate(split_low(diag_ref[head]), axis=0)) for head in heads
    ]
    for head in heads:
        dspan_ref[pl.ds(base + head, 1), :] = diagonal_sums(turns[head])
    for pair in pairs:
        cols = slice(pair * BLOCK, (pair + 1) * BLOCK)
        grad_query = jnp.transpose(jnp.concatenate(halves[2 * pair : 2 * pair + 2], axis=0))
        grad_query = grad_query * HEAD_DIM ** (-0.5)
        val_total = val_terms[2 * pair] + val_terms[2 * pair + 1]
        key_total = key_terms[2 * pair] + key_terms[2 * pair + 1]
        for part, value in enumerate((grad_query, key_total, val_total)):
            begin = pl.multiple_of(part * D + base * HEAD_DIM + pair * BLOCK, BLOCK)
            out_ref[:, pl.ds(begin, BLOCK)] = value.astype(BF)
        sum_ref[0:1, cols] = jnp.sum(grad_query, axis=0, keepdims=True)
        sum_ref[1:2, cols] = jnp.sum(val_total, axis=0, keepdims=True)


def attention_backward(qkv, upstream, gate, span, fill, lse, pick, bias):
    length = qkv.shape[0]
    heads = 2 if pick is None else SEEN_HEADS
    specs = head_specs(length, heads)
    shapes = [
        jax.ShapeDtypeStruct((length, 3 * D), BF),
        jax.ShapeDtypeStruct((8, D), F32),
        jax.ShapeDtypeStruct((16, length), F32),
        jax.ShapeDtypeStruct((16, SPAN), F32),
    ]
    out_specs = [
        whole_spec((length, 3 * D)),
        pl.BlockSpec((8, heads * HEAD_DIM), lambda i: (0, i)),
        whole_spec((16, length)),
        whole_spec((16, SPAN)),
    ]
    if pick is None:
        args = [qkv, qkv, qkv, upstream, gate, span, fill, lse]
        kernel, more = attention_backward_kernel, []
        scratch = [
            pltpu.VMEM((2, length, length), F32),
            pltpu.VMEM((2, length, length), F32),
            pltpu.VMEM((2, length, length), BF),
            pltpu.VMEM((2, length, length), BF),
            pltpu.VMEM((2, BLOCK, SPAN), F32),
        ]
    else:
        turned = jnp.transpose(pick[1])
        flip = jnp.concatenate([turned, turned], axis=1)
        args = [qkv, qkv, qkv, upstream, gate, fill, lse, pick[0], pick[2], flip, bias]
        kernel = seen_backward_kernel
        more = [pl.BlockSpec((heads * BLOCK, BLOCK), lambda i: (i, 0))]
        scratch = [pltpu.VMEM((heads, BLOCK, SPAN), F32)]
    return pl.pallas_call(
        kernel,
        grid=(HEADS // heads,),
        in_specs=specs
        + [specs[0]]
        + [whole_spec(a.shape) for a in args[4 : len(args) - len(more)]]
        + more,
        out_specs=out_specs,
        out_shape=shapes,
        scratch_shapes=scratch,
        compiler_params=params_of(),
    )(*args)


def weight_grad_kernel(table_ref, left_ref, right_ref, out_ref, turn_ref):
    rows = left_ref.shape[1]
    strips = right_ref.shape[1] // 128
    grad = dot_tn(left_ref[...], right_ref[...])
    for strip in range(strips):
        turn_ref[pl.ds(strip, rows, stride=strips), :] = grad[:, strip * 128 : (strip + 1) * 128]
    out_ref[...] = turn_ref[...].astype(BF)


def weight_grad(left, right, geometry, code_index, base, rows):
    length, depth = left.shape
    strips = right.shape[1] // 128
    slots = range(geometry.dp_count)
    chunks = owned_chunks(geometry, base, strips, depth, rows, rows, slots)
    out = pl.pallas_call(
        weight_grad_kernel,
        grid_spec=pltpu.PrefetchScalarGridSpec(
            num_scalar_prefetch=1,
            grid=(len(chunks[0]),),
            in_specs=[
                pl.BlockSpec((length, rows), lambda i, t: (0, t[i])),
                pl.BlockSpec(right.shape, lambda i, t: (0, 0)),
            ],
            out_specs=pl.BlockSpec((rows * strips, 128), lambda i, t: (i, 0)),
            scratch_shapes=[pltpu.VMEM((rows * strips, 128), F32)],
        ),
        out_shape=jax.ShapeDtypeStruct((len(chunks[0]) * rows * strips, 128), BF),
        compiler_params=params_of(),
    )(chunk_table(chunks, code_index) // rows, left, right)
    return out, (chunks, base, strips, rows)


def unpack_jobs(geometry, specs):
    jobs = []
    for target, (base, depth, strips, rows) in enumerate(specs):
        for low in range(0, depth, rows):
            begin = base + low * strips
            jobs.append((target, low, rows, strips) + geometry.pieces(begin, begin + rows * strips))
    return jobs


DEPTH = 4


def stream_jobs(jobs, source_ref, buffer_ref, edge_ref, sems, work):
    def copies(number):
        main, edges = jobs[number][4:6]
        slot = number % DEPTH
        found = []
        for shard, begin, low, count in main:
            found.append(
                (source_ref.at[shard, pl.ds(begin, count)], buffer_ref.at[slot, pl.ds(low, count)])
            )
        for place, (shard, _) in enumerate(edges):
            found.append((source_ref.at[shard, pl.ds(0, TILE)], edge_ref.at[slot, place]))
        return [
            pltpu.make_async_copy(source, target, sems.at[slot, index])
            for index, (source, target) in enumerate(found)
        ]

    for number in range(min(DEPTH - 1, len(jobs))):
        for copy in copies(number):
            copy.start()
    for number, job in enumerate(jobs):
        if number + DEPTH - 1 < len(jobs):
            for copy in copies(number + DEPTH - 1):
                copy.start()
        for copy in copies(number):
            copy.wait()
        slot = number % DEPTH
        for place, (_, low) in enumerate(job[5]):
            buffer_ref[slot, low : low + TILE, :] += edge_ref[slot, place]
        work(number, job, slot)


def unpack_kernel(*refs, jobs, stages):
    source_ref = refs[0]
    targets = refs[1 : 1 + len(stages)]
    buffer_ref, edge_ref, turn_ref, sems, out_sems = refs[1 + len(stages) : 6 + len(stages)]
    stage_refs = refs[6 + len(stages) :]
    pending = {}

    def work(number, job, slot):
        target, low, rows, strips = job[:4]
        stage_ref, key = stage_refs[stages[target]], (stages[target], slot)
        if key in pending:
            pending.pop(key).wait()
        turn_ref[: rows * strips, :] = buffer_ref[slot, : rows * strips, :].astype(F32)
        for strip in range(strips):
            stage_ref[slot, :rows, strip * 128 : (strip + 1) * 128] = turn_ref[
                pl.ds(strip, rows, stride=strips), :
            ].astype(BF)
        copy = pltpu.make_async_copy(
            stage_ref.at[slot, pl.ds(0, rows)],
            targets[target].at[pl.ds(low, rows)],
            out_sems.at[stages[target], slot],
        )
        copy.start()
        pending[key] = copy

    stream_jobs(jobs, source_ref, buffer_ref, edge_ref, sems, work)
    for copy in pending.values():
        copy.wait()


def unpack(geometry, windows, specs):
    jobs = unpack_jobs(geometry, specs)
    kinds = sorted({spec[2] for spec in specs})
    stages = [kinds.index(spec[2]) for spec in specs]
    most = max(job[2] * job[3] for job in jobs)
    copies = max(len(job[4]) + len(job[5]) for job in jobs)
    edges = max([1] + [len(job[5]) for job in jobs])
    return pl.pallas_call(
        functools.partial(unpack_kernel, jobs=jobs, stages=stages),
        in_specs=[pl.BlockSpec(memory_space=pl.ANY)],
        out_specs=[pl.BlockSpec(memory_space=pl.ANY)] * len(specs),
        out_shape=[jax.ShapeDtypeStruct((s[1], s[2] * 128), BF) for s in specs],
        scratch_shapes=[
            pltpu.VMEM((DEPTH, most, 128), BF),
            pltpu.VMEM((DEPTH, edges, TILE, 128), BF),
            pltpu.VMEM((most, 128), F32),
            pltpu.SemaphoreType.DMA((DEPTH, copies)),
            pltpu.SemaphoreType.DMA((len(kinds), DEPTH)),
        ]
        + [
            pltpu.VMEM((DEPTH, max(s[3] for s in specs if s[2] == kind), kind * 128), BF)
            for kind in kinds
        ],
        compiler_params=pltpu.CompilerParams(vmem_limit_bytes=VMEM_LIMIT),
    )(windows)


def unpack_conv_kernel(
    code_ref, source_ref, target_ref, buffer_ref, edge_ref, turn_ref, stage_ref, sems, out_sems, *,
    jobs, width
):
    first = code_ref[0] * width
    strip = first // 128
    strips = D // 128
    lead = first - strip * 128
    pending = {}

    def work(number, job, slot):
        low, rows = job[1], job[2]
        if slot in pending:
            pending.pop(slot).wait()
        turn_ref[...] = buffer_ref[slot].astype(F32)
        one = turn_ref[pl.ds(strip, rows, stride=strips), :]
        two = turn_ref[pl.ds(jnp.minimum(strip + 1, strips - 1), rows, stride=strips), :]
        pair = pltpu.roll(jnp.concatenate([one, two], axis=1), lax.rem(256 - lead, 256), 1)
        stage_ref[slot] = pair[:, :width].astype(BF)
        copy = pltpu.make_async_copy(
            stage_ref.at[slot], target_ref.at[pl.ds(low, rows)], out_sems.at[slot]
        )
        copy.start()
        pending[slot] = copy

    stream_jobs(jobs, source_ref, buffer_ref, edge_ref, sems, work)
    for copy in pending.values():
        copy.wait()


def unpack_conv(geometry, windows, code_index, rows=768):
    width = D // geometry.code_count
    depth = KERNEL * WIDTH
    jobs = unpack_jobs(geometry, [(geometry.place("conv_w"), depth, D // 128, rows)])
    copies = max(len(job[4]) + len(job[5]) for job in jobs)
    edges = max([1] + [len(job[5]) for job in jobs])
    return pl.pallas_call(
        functools.partial(unpack_conv_kernel, jobs=jobs, width=width),
        in_specs=[
            pl.BlockSpec(memory_space=pltpu.SMEM),
            pl.BlockSpec(memory_space=pl.ANY),
        ],
        out_specs=pl.BlockSpec(memory_space=pl.ANY),
        out_shape=jax.ShapeDtypeStruct((depth, width), BF),
        scratch_shapes=[
            pltpu.VMEM((DEPTH, rows * D // 128, 128), BF),
            pltpu.VMEM((DEPTH, edges, TILE, 128), BF),
            pltpu.VMEM((rows * D // 128, 128), F32),
            pltpu.VMEM((DEPTH, rows, width), BF),
            pltpu.SemaphoreType.DMA((DEPTH, copies)),
            pltpu.SemaphoreType.DMA((DEPTH,)),
        ],
        compiler_params=pltpu.CompilerParams(vmem_limit_bytes=VMEM_LIMIT),
    )(jnp.full((1,), code_index, jnp.int32), windows)


def small_kernel(
    source_ref, patch_ref, glob_ref, vec_ref, up_ref, rest_ref, head_ref,
    buffer_ref, edge_ref, turn_ref, head_turn_ref, sems, *, jobs, phase, lead, whole
):
    strips = D // 128

    def columns(target_ref, begin, count, kind):
        for strip in range(strips):
            target_ref[:, strip * 128 : (strip + 1) * 128] = turn_ref[
                pl.ds(begin + strip, count, stride=strips), :
            ].astype(kind)

    def work(number, job, slot):
        turn_ref[: job[2], :] = buffer_ref[slot, : job[2], :].astype(F32)
        if number == 0:
            columns(patch_ref, phase, PATCH_IN, BF)
            columns(glob_ref, phase + PATCH_IN * strips, 4, F32)
            return
        count = vec_ref.shape[0]
        columns(vec_ref, 0, count, F32)
        wide = FF // 128
        for layer in range(LAYERS):
            begin = (layer + 1) * (count // LAYERS) * strips - wide
            for strip in range(wide):
                up_ref[layer : layer + 1, strip * 128 : (strip + 1) * 128] = turn_ref[
                    begin + strip : begin + strip + 1, :
                ]
        begin = count * strips
        rest_ref[...] = turn_ref[begin : begin + rest_ref.shape[0], :]
        begin += whole
        rows = head_turn_ref.shape[0]
        turned = turn_ref[begin : begin + rows, :]
        if lead:
            lane = lax.broadcasted_iota(jnp.int32, (1, 128), 1)
            turned = jnp.where(
                lane < 128 - lead,
                pltpu.roll(turned, 128 - lead, 1),
                pltpu.roll(turn_ref[begin + 1 : begin + 1 + rows, :], 128 - lead, 1),
            )
        head_turn_ref[...] = turned
        for strip in range(PROJ // 128):
            head_ref[:, strip * 128 : (strip + 1) * 128] = head_turn_ref[
                pl.ds(strip, D, stride=PROJ // 128), :
            ].astype(BF)

    stream_jobs(jobs, source_ref, buffer_ref, edge_ref, sems, work)


def unpack_small(geometry, windows):
    where = starts()
    tail = geometry.place("layer_vec")
    regions = [(0, geometry.place("conv_w")), (tail, geometry.begins[-1] + geometry.window)]
    jobs = [
        (0, 0, high - low, 1) + geometry.pieces(low, high) for low, high in regions
    ]
    most = max(job[2] for job in jobs)
    copies = max(len(job[4]) + len(job[5]) for job in jobs)
    edges = max([1] + [len(job[5]) for job in jobs])
    slots = LAYERS * (8 + FF // D)
    offset = where["w_head"] - where["gate_proj"]
    rest = -(-(-(-offset // 128)) // 8) * 8
    return pl.pallas_call(
        functools.partial(
            small_kernel, jobs=jobs, phase=geometry.phase, lead=offset % 128, whole=offset // 128
        ),
        in_specs=[pl.BlockSpec(memory_space=pl.ANY)],
        out_shape=[
            jax.ShapeDtypeStruct((PATCH_IN, D), BF),
            jax.ShapeDtypeStruct((4, D), F32),
            jax.ShapeDtypeStruct((slots, D), F32),
            jax.ShapeDtypeStruct((LAYERS, FF), F32),
            jax.ShapeDtypeStruct((rest, 128), F32),
            jax.ShapeDtypeStruct((D, PROJ), BF),
        ],
        scratch_shapes=[
            pltpu.VMEM((DEPTH, most, 128), BF),
            pltpu.VMEM((DEPTH, edges, TILE, 128), BF),
            pltpu.VMEM((most, 128), F32),
            pltpu.VMEM((D * PROJ // 128, 128), F32),
            pltpu.SemaphoreType.DMA((DEPTH, copies)),
        ],
        compiler_params=pltpu.CompilerParams(vmem_limit_bytes=VMEM_LIMIT),
    )(windows)


def pack_kernel(code_ref, *refs, plans, empty):
    sources, out_ref, sems = refs[:-2], refs[-2], refs[-1]
    for slot in range(empty):
        out_ref[slot] = jnp.zeros_like(out_ref[slot])
    for code, plan in enumerate(plans):

        @pl.when(code_ref[0] == code)
        def _():
            copies = [
                pltpu.make_async_copy(
                    sources[source].at[pl.ds(begin, count)],
                    out_ref.at[slot, pl.ds(low, count)],
                    sems.at[index],
                )
                for index, (source, begin, slot, low, count) in enumerate(plan)
            ]
            for copy in copies:
                copy.start()
            for copy in copies:
                copy.wait()


def pack_plans(geometry, spans, slots):
    plans = []
    for code in range(geometry.code_count):
        plan = []
        for slot in slots:
            begin = geometry.begins[slot * geometry.code_count + code]
            stop = begin + geometry.window
            row = begin
            while row < stop:
                place, rows, source, inner = next(
                    item for item in spans[code] if item[0] <= row < item[0] + item[1]
                )
                count = min(stop, place + rows) - row
                plan.append((source, inner + row - place, slot, row - begin, count))
                row += count
        plans.append(plan)
    return plans


def pack(geometry, code_index, sources, spans, low, high):
    plans = pack_plans(geometry, spans, range(low, high))
    return pl.pallas_call(
        functools.partial(pack_kernel, plans=plans, empty=low),
        in_specs=[pl.BlockSpec(memory_space=pltpu.SMEM)]
        + [pl.BlockSpec(memory_space=pl.ANY)] * len(sources),
        out_specs=pl.BlockSpec(memory_space=pltpu.VMEM),
        out_shape=jax.ShapeDtypeStruct((high, geometry.window, 128), BF),
        scratch_shapes=[pltpu.SemaphoreType.DMA((max(len(plan) for plan in plans),))],
        compiler_params=pltpu.CompilerParams(vmem_limit_bytes=VMEM_LIMIT),
    )(jnp.full((1,), code_index, jnp.int32), *sources)


def front_slots(geometry):
    stop = geometry.place("w_qkv")
    count = sum(
        geometry.begins[slot * geometry.code_count + geometry.code_count - 1] + geometry.window
        <= stop
        for slot in range(geometry.dp_count)
    )
    if geometry.dp_count & (geometry.dp_count - 1) or not count:
        return 0
    return 1 << (count.bit_length() - 1)


def add_low(left, right):
    return (left.astype(F32) + right.astype(F32)).astype(BF)


def reduce_front(held, dp_count, dp_index):
    count = held.shape[0]
    bit = count // 2
    while bit:
        mine = dp_index // bit % 2
        keep = lax.dynamic_slice_in_dim(held, mine * bit, bit, 0)
        give = lax.dynamic_slice_in_dim(held, (1 - mine) * bit, bit, 0)
        held = add_low(keep, lax.ppermute(give, "dp", [(i, i ^ bit) for i in range(dp_count)]))
        bit //= 2
    bits = []
    while count < dp_count:
        bits.append(count)
        count *= 2
    middle = held.shape[1] // (2 * TILE) * TILE
    halves = [held[0, :middle], held[0, middle:]]
    for number in range(len(bits)):
        for side, bit in enumerate((bits[number], bits[-1 - number])):
            moved = lax.ppermute(
                halves[side], "dp", [(i, i - bit) for i in range(dp_count) if i & bit]
            )
            halves[side] = add_low(halves[side], moved)
    return jnp.concatenate(halves, axis=0)


def tail_kernel(*refs, lead, whole):
    vectors = refs[:-4]
    small_ref, head_ref, out_ref, turn_ref = refs[-4:]
    begin = 0
    for vector_ref in vectors:
        if len(vector_ref.shape) == 2:
            for row in range(2):
                for low in range(0, D, 128):
                    turn_ref[begin : begin + 1, :] = vector_ref[row : row + 1, low : low + 128]
                    begin += 1
        else:
            for low in range(0, vector_ref.shape[0], 128):
                turn_ref[begin : begin + 1, :] = vector_ref[low : low + 128].reshape(1, 128)
                begin += 1
    turn_ref[begin:, :] = jnp.zeros((turn_ref.shape[0] - begin, 128), F32)
    turn_ref[begin : begin + small_ref.shape[0], :] = small_ref[...]
    begin += whole
    rows = head_ref.shape[0]
    turned = pltpu.roll(head_ref[...], lead, 1) if lead else head_ref[...]
    lane = lax.broadcasted_iota(jnp.int32, (1, 128), 1)
    turn_ref[begin : begin + rows, :] += jnp.where(lane >= lead, turned, 0.0)
    turn_ref[begin + 1 : begin + 1 + rows, :] += jnp.where(lane < lead, turned, 0.0)
    out_ref[...] = turn_ref[...].astype(BF)


def tail_grad(vectors, small, grad_head, rows):
    lead, whole = small.shape[0] % 128, small.shape[0] // 128
    small = jnp.pad(small, (0, -small.shape[0] % 128)).reshape(-1, 128)
    return pl.pallas_call(
        functools.partial(tail_kernel, lead=lead, whole=whole),
        out_shape=jax.ShapeDtypeStruct((rows, 128), BF),
        scratch_shapes=[pltpu.VMEM((rows, 128), F32)],
        compiler_params=pltpu.CompilerParams(vmem_limit_bytes=VMEM_LIMIT),
    )(*vectors, small, grad_head)


def blocks_of_code(block):
    count = lax.axis_size("code")
    return [block] + [
        lax.ppermute(block, "code", [(i, (i + step) % count) for i in range(count)])
        for step in range(1, count)
    ]


def side_kernel(code_ref, *refs):
    blocks, out_ref = refs[:-1], refs[-1]
    count, width = len(blocks), blocks[0].shape[1]
    for code in range(count):

        @pl.when(code_ref[0] == code)
        def _():
            for source in range(count):
                out_ref[:, source * width : (source + 1) * width] = blocks[
                    (code - source) % count
                ][...]


def side_by_side(block, code_index):
    blocks = blocks_of_code(block)
    rows, width = block.shape
    return pl.pallas_call(
        side_kernel,
        in_specs=[pl.BlockSpec(memory_space=pltpu.SMEM)]
        + [pl.BlockSpec(memory_space=pltpu.VMEM)] * len(blocks),
        out_specs=pl.BlockSpec(memory_space=pltpu.VMEM),
        out_shape=jax.ShapeDtypeStruct((rows, width * len(blocks)), block.dtype),
    )(jnp.full((1,), code_index, jnp.int32), *blocks)


def sum_over(value, axis):
    count = lax.axis_size(axis)
    if count & (count - 1):
        return lax.psum(value, axis)
    bit = 1
    while bit < count:
        value = value + lax.ppermute(value, axis, [(i, i ^ bit) for i in range(count)])
        bit *= 2
    return value


def sum_over_all(value):
    count = lax.axis_size("dp") * lax.axis_size("code")
    sent = jnp.broadcast_to(value[None], (count,) + value.shape)
    return jnp.sum(lax.all_to_all(sent, ("dp", "code"), 0, 0), axis=0)


def norm_forward(before, norm_gain, norm_shift):
    centred = before - jnp.mean(before, axis=-1, keepdims=True)
    inv_std = lax.rsqrt(jnp.mean(centred * centred, axis=-1, keepdims=True) + NORM_EPSILON)
    normed = centred * inv_std
    return (normed * norm_gain + norm_shift, normed, inv_std)


def norm_backward(upstream, normed, inv_std, norm_gain):
    scaled = upstream * norm_gain
    centred_grad = (
        scaled
        - jnp.mean(scaled, axis=-1, keepdims=True)
        - normed * jnp.mean(scaled * normed, axis=-1, keepdims=True)
    )
    return (
        centred_grad * inv_std,
        jnp.sum(upstream * normed, axis=0),
        jnp.sum(upstream, axis=0),
    )


def gelu(pre_act):
    return 0.5 * pre_act * (1.0 + lax.erf(pre_act * 0.7071067811865476))


def gelu_grad(pre_act):
    return (
        0.5 * (1.0 + lax.erf(pre_act * 0.7071067811865476))
        + pre_act * jnp.exp(-0.5 * pre_act * pre_act) * 0.3989422804014327
    )


def vec_part(vector, slot_index):
    return vector[slot_index : slot_index + 1]


def gate_maps():
    rows = (np.arange(D)[:, None] % HEAD_DIM == np.arange(HEAD_DIM)[None, :]).astype(np.float32)
    groups = np.arange(8)[:, None] // 4 == np.arange(2 * HEADS)[None, :] // HEADS
    own = np.arange(D)[:, None] // HEAD_DIM == np.arange(2 * HEADS)[None, :] % HEADS
    return rows, groups.astype(np.float32), own.astype(np.float32)


def exact_dot(left, right, dims=((1,), (0,))):
    return lax.dot_general(left, right, (dims, ((), ())), precision=HIGHEST)


def gate_columns(gate_weight):
    rows, groups, own = gate_maps()
    wide = gate_weight.astype(F32)
    sums = exact_dot(wide, jnp.asarray(groups))
    return exact_dot(jnp.asarray(rows), sums[:HEAD_DIM]) * own, sums[HEAD_DIM:]


def gate_forward(in_low, weights):
    columns, bias = weights["gate_columns"]
    high = columns.astype(BF)
    rest = (columns - high.astype(F32)).astype(BF)
    logit = dot_nn(in_low, jnp.concatenate([high, rest], axis=1))
    logit = logit[:, : 2 * HEADS] + logit[:, 2 * HEADS :] + bias
    pair = jax.nn.sigmoid(logit)
    first, second = pair[:, :HEADS], pair[:, HEADS:]
    gate_vals = first * (second * weights["gate_scale"].astype(F32) - 1.0) + 2.0
    return (gate_vals, first, second)


def gate_backward(grad_gate, first, second, in_low, weights):
    scale_vec = weights["gate_scale"].astype(F32)
    grad_scale = jnp.sum(grad_gate * first * second, axis=0)
    grad_one = grad_gate * (second * scale_vec - 1.0) * first * (1.0 - first)
    grad_two = grad_gate * first * scale_vec * second * (1.0 - second)
    both = jnp.concatenate([grad_one, grad_two], axis=1)
    rows, groups, own = gate_maps()
    high = both.astype(BF)
    rest = (both - high.astype(F32)).astype(BF)
    product = dot_tn(in_low, jnp.concatenate([high, rest], axis=1))
    product = (product[:, : 2 * HEADS] + product[:, 2 * HEADS :]) * own
    summed = exact_dot(jnp.asarray(rows), product, ((0,), (0,)))
    summed = jnp.concatenate([summed, jnp.sum(both, axis=0, keepdims=True)], axis=0)
    grad_proj = exact_dot(summed, jnp.asarray(groups), ((1,), (1,)))
    columns_high, columns_rest = split_low(weights["gate_columns"][0])
    grad_heads = dot_nt(
        jnp.concatenate([high, rest, high], axis=1),
        jnp.concatenate([columns_high, columns_high, columns_rest], axis=1),
    )
    return (grad_heads, grad_proj, grad_scale)


def layer_forward(hidden, fill, weights, span, pick):
    vector = weights["layer_vec"]
    in_low = hidden.astype(BF)
    shift = jnp.concatenate(
        [vec_part(vector, 0), jnp.zeros((1, D), F32), vec_part(vector, 1)], axis=1
    )
    scale = np.ones((1, 3 * D), np.float32)
    scale[:, :D] = HEAD_DIM ** (-0.5)
    qkv_low = ((dot_nn(in_low, weights["w_qkv"]) + shift) * scale).astype(BF)
    gate_vals, first, second = gate_forward(in_low, weights)
    gate_wide = jnp.pad(jnp.transpose(gate_vals), ((0, 16 - HEADS), (0, 0)))
    attended, lse, bias = attention_forward(qkv_low, gate_wide, span, fill, pick)
    attn_out = dot_nn(attended, weights["w_out"]) + vec_part(vector, 2)
    mid_rows, normed_one, inv_one = norm_forward(
        DEEP_ALPHA * hidden + attn_out, vec_part(vector, 3), vec_part(vector, 4)
    )
    mid_low = mid_rows.astype(BF)
    pre_act = dot_nn(mid_low, weights["w_up"]) + weights["up_bias"]
    act_low = gelu(pre_act).astype(BF)
    ffn_out = dot_nn(act_low, weights["w_down"]) + vec_part(vector, 5)
    final_rows, normed_two, inv_two = norm_forward(
        DEEP_ALPHA * mid_rows + ffn_out, vec_part(vector, 6), vec_part(vector, 7)
    )
    kept = (in_low, qkv_low, gate_wide, first, second, lse, attended, bias)
    kept += (mid_low, pre_act, act_low, normed_one, inv_one, normed_two, inv_two)
    return (final_rows, kept)


def layer_backward(upstream, kept, fill, weights, span, pick, grad_of):
    in_low, qkv_low, gate_wide, first, second, lse, attended, bias = kept[:8]
    mid_low, pre_act, act_low, normed_one, inv_one, normed_two, inv_two = kept[8:]
    vector = weights["layer_vec"]
    grad_res_two, grad_gain_two, grad_shift_two = norm_backward(
        upstream, normed_two, inv_two, vec_part(vector, 6)
    )
    ffn_low = grad_res_two.astype(BF)
    grad_down = grad_of("w_down", act_low, ffn_low, 512)
    grad_pre = dot_nt(ffn_low, weights["w_down"]) * gelu_grad(pre_act)
    pre_low = grad_pre.astype(BF)
    grad_up = grad_of("w_up", mid_low, pre_low, 256)
    grad_mid = DEEP_ALPHA * grad_res_two + dot_nt(pre_low, weights["w_up"])
    grad_res_one, grad_gain_one, grad_shift_one = norm_backward(
        grad_mid, normed_one, inv_one, vec_part(vector, 3)
    )
    out_low = grad_res_one.astype(BF)
    grad_out = grad_of("w_out", attended, out_low, 384)
    grad_att = dot_nt(out_low, weights["w_out"]).astype(BF)
    proj_low, part_sums, grad_gate, grad_span = attention_backward(
        qkv_low, grad_att, gate_wide, span, fill, lse, pick, bias
    )
    grad_heads, grad_gate_proj, grad_gate_scale = gate_backward(
        jnp.transpose(grad_gate[:HEADS]), first, second, in_low, weights
    )
    grad_qkv = grad_of("w_qkv", in_low, proj_low, 256)
    grad_hidden = DEEP_ALPHA * grad_res_one + dot_nt(proj_low, weights["w_qkv"]) + grad_heads
    grad_vec = [
        part_sums,
        jnp.sum(grad_res_one, axis=0),
        grad_gain_one,
        grad_shift_one,
        jnp.sum(grad_res_two, axis=0),
        grad_gain_two,
        grad_shift_two,
        jnp.sum(grad_pre, axis=0),
    ]
    grad_map = {
        "w_qkv": grad_qkv,
        "w_out": grad_out,
        "w_up": grad_up,
        "w_down": grad_down,
        "layer_vec": grad_vec,
        "gate_proj": grad_gate_proj,
        "gate_scale": grad_gate_scale,
    }
    return (grad_hidden, grad_map, grad_span)


def head_kernel(
    in_ref, weight_ref, code_ref, name_ref, target_ref, loss_ref, rows_ref, flat_ref, low_ref
):
    weight, codebook, names = weight_ref[...], code_ref[...], name_ref[0:1, :]
    loss = jnp.zeros((1, 1), F32)
    for low in range(0, in_ref.shape[0], BLOCK):
        rows = slice(low, low + BLOCK)
        projected = dot_nn(in_ref[rows, :], weight)
        inv_len = lax.rsqrt(jnp.sum(projected * projected, axis=1, keepdims=True) + UNIT_EPSILON)
        unit_rows = projected * inv_len
        logits = LOGIT_SCALE * dot_nt(unit_rows.astype(BF), codebook)
        target = target_ref[rows, 0:1]
        live = jnp.where(target >= 0, 1.0, 0.0)
        hits = jnp.where(names == target, 1.0, 0.0)
        top = jnp.max(logits, axis=1, keepdims=True)
        weights = jnp.exp(logits - top)
        total = jnp.sum(weights, axis=1, keepdims=True)
        picked = jnp.sum(logits * hits, axis=1, keepdims=True)
        loss += jnp.sum((top + jnp.log(total) - picked) * live, axis=0, keepdims=True)
        grad_logits = (weights * (1.0 / total) - hits) * (live * LOGIT_SCALE)
        grad_unit = dot_nn(grad_logits.astype(BF), codebook)
        grad_proj = (
            grad_unit - unit_rows * jnp.sum(unit_rows * grad_unit, axis=1, keepdims=True)
        ) * inv_len
        proj_low = grad_proj.astype(BF)
        low_ref[rows, :] = proj_low
        rows_ref[rows, :] = dot_nt(proj_low, weight)
    loss_ref[...] = jnp.broadcast_to(loss, loss_ref.shape)
    grad = dot_tn(in_ref[...], low_ref[...])
    strips = PROJ // 128
    for strip in range(strips):
        flat_ref[pl.ds(strip, D, stride=strips), :] = grad[:, strip * 128 : (strip + 1) * 128]


def head_pass(hidden, w_head, codebook, codes, target_codes):
    targets = jnp.broadcast_to(target_codes[:, None], (ROWS, 128))
    names = jnp.broadcast_to(codes, (8, codes.shape[1]))
    loss, grad_rows, grad_head = pl.pallas_call(
        head_kernel,
        out_shape=[
            jax.ShapeDtypeStruct((8, 128), F32),
            jax.ShapeDtypeStruct((ROWS, D), F32),
            jax.ShapeDtypeStruct((D * PROJ // 128, 128), F32),
        ],
        scratch_shapes=[pltpu.VMEM((ROWS, PROJ), BF)],
        compiler_params=pltpu.CompilerParams(vmem_limit_bytes=VMEM_LIMIT),
    )(hidden.astype(BF), w_head, codebook, names, targets)
    return (loss[0, 0], grad_rows, grad_head)


def local(
    patches,
    lengths,
    patch_masks,
    targets,
    codebook,
    params,
    first_moment,
    second_moment,
    step_count,
):
    dp_count = lax.axis_size("dp")
    code_count = lax.axis_size("code")
    code_index = lax.axis_index("code")
    shard_len = params.shape[0]
    shard_rows = shard_len // 128
    dp_index = lax.axis_index("dp")
    geometry = Geometry(dp_count, code_count, shard_rows)
    own_offset = lax.rem((dp_index * code_count + code_index) * shard_rows + geometry.phase, TILE)
    own_window = lax.dynamic_update_slice(
        jnp.zeros((geometry.window, 128), F32), params.reshape(shard_rows, 128), (own_offset, 0)
    ).astype(BF)
    windows = lax.all_gather(own_window, ("dp", "code"), axis=0, tiled=False)
    where = starts()

    w_patch, glob_vec, vectors, up_bias, rest, w_head = unpack_small(geometry, windows)
    rest = rest.reshape(-1)

    def values(seg_name):
        extent = dict(layout())[seg_name]
        begin = where[seg_name] - where["gate_proj"]
        return rest[begin : begin + math.prod(extent)].reshape(extent)

    gate_proj = values("gate_proj")
    gate_scale = values("gate_scale")
    rel_table = values("rel_table").astype(BF)
    conv_weight = unpack_conv(geometry, windows, code_index)
    weights = []
    for index in range(LAYERS):
        mats = unpack(
            geometry,
            windows,
            [
                (geometry.place("w_qkv", index), D, 3 * D // 128, 128),
                (geometry.place("w_out", index), D, D // 128, 384),
                (geometry.place("w_up", index), D, FF // 128, 128),
                (geometry.place("w_down", index), FF, D // 128, 512),
            ],
        )
        weights.append(
            dict(zip(("w_qkv", "w_out", "w_up", "w_down"), mats))
            | {
                "layer_vec": vectors[index * (8 + FF // D) :],
                "up_bias": up_bias[index : index + 1],
                "gate_columns": gate_columns(gate_proj[index]),
                "gate_scale": gate_scale[index],
            }
        )

    places = jnp.arange(ROWS, dtype=jnp.int32)
    mask_row = jnp.pad(patch_masks[0], (0, ROWS - LONG))
    live_slot = places < jnp.minimum(lengths[0], LONG)
    visible = live_slot & (mask_row == 0)
    rank = jnp.cumsum(visible.astype(jnp.int32)) - 1
    pick = (
        visible[None, :] & (rank[None, :] == jnp.arange(SEEN, dtype=jnp.int32)[:, None])
    )
    pick_low = pick.astype(BF)
    near = jnp.sum(pick_low.reshape(SEEN, ROWS // BLOCK, BLOCK), axis=1)
    hop = jnp.sum(pick.astype(F32).reshape(SEEN, ROWS // BLOCK, BLOCK), axis=2)
    pick_seen = (pick_low, near, jnp.pad(hop, ((0, 0), (0, BLOCK - ROWS // BLOCK))))
    pick_full = pick.astype(F32)
    seen_valid = jnp.arange(SEEN, dtype=jnp.int32) < lengths[0] // 4
    seen_fill = jnp.broadcast_to(jnp.where(seen_valid, 0.0, MASK_FILL)[:, None], (SEEN, BLOCK))
    live_fill = jnp.broadcast_to(jnp.where(live_slot, 0.0, MASK_FILL)[:, None], (ROWS, BLOCK))
    live_float = live_slot.astype(F32)[:, None]
    span_table = span_onehot()
    span = dot_tn(
        jnp.pad(rel_table, ((0, 0), (0, 16 - HEADS))), jnp.asarray(span_table.T, BF)
    )

    all_codes = jnp.concatenate(blocks_of_code(codebook), axis=0)
    code_places = (
        code_index - jnp.arange(code_count, dtype=jnp.int32) + code_count
    ) % code_count * codebook.shape[0]
    code_names = (
        code_places[:, None] + jnp.arange(codebook.shape[0], dtype=jnp.int32)[None, :]
    ).reshape(1, -1)
    patch_rows = jnp.pad(patches[0], ((0, ROWS - LONG), (0, 0)))
    embedded = dot_nn(patch_rows, w_patch)
    normed_rows, normed_zero, inv_zero = norm_forward(embedded, glob_vec[0 : 1], glob_vec[1 : 2])
    start_rows = normed_rows * live_float
    conv_in = start_rows.astype(BF)
    width = D // code_count
    own_cols = code_index * width
    own_in = lax.dynamic_slice_in_dim(conv_in, own_cols, width, 1)
    half = KERNEL // 2
    conv_own = conv_call(conv_forward_kernel, own_in[:LONG], conv_weight, half, False)
    seen_own = lax.dot_general(
        pick_full, conv_own, (((1,), (0,)), ((), ())), precision=HIGHEST
    )
    seen_raw = side_by_side(seen_own, code_index)
    seen_pre = seen_raw + glob_vec[2 : 3]
    seen_start = lax.dot_general(
        pick_full, start_rows, (((1,), (0,)), ((), ())), precision=HIGHEST
    )
    seen_rows = seen_start + gelu(seen_pre)
    encoded, kept_first = layer_forward(seen_rows, seen_fill, weights[0], span, pick_seen)
    placed = lax.dot_general(
        pick_full, encoded, (((0,), (0,)), ((), ())), precision=HIGHEST
    )
    hidden = jnp.where(visible[:, None], placed, glob_vec[3 : 4])
    final, kept_second = layer_forward(hidden, live_fill, weights[1], span, None)
    target_codes = jnp.where(mask_row == 1, jnp.pad(targets[0], (0, ROWS - LONG)), -1)
    loss_local, upstream, grad_head = head_pass(final, w_head, all_codes, code_names, target_codes)

    def grad_maker(index):
        return lambda seg_name, left, right, rows: weight_grad(
            left, right, geometry, code_index, geometry.place(seg_name, index), rows
        )

    upstream, map_second, span_second = layer_backward(
        upstream, kept_second, live_fill, weights[1], span, None, grad_maker(1)
    )
    grad_mask_emb = jnp.sum(jnp.where(visible[:, None], 0.0, upstream), axis=0)
    grad_encoded = lax.dot_general(
        pick_full, upstream, (((1,), (0,)), ((), ())), precision=HIGHEST
    )
    grad_seen, map_first, span_first = layer_backward(
        grad_encoded, kept_first, seen_fill, weights[0], span, pick_seen, grad_maker(0)
    )
    grad_seen = grad_seen * seen_valid[:, None].astype(F32)
    grad_conv_seen = grad_seen * gelu_grad(seen_pre)
    grad_conv = dot_tn(pick_low, grad_conv_seen.astype(BF)).astype(BF)
    grad_full = lax.dot_general(
        pick_full, grad_seen, (((0,), (0,)), ((), ())), precision=HIGHEST
    )
    own_grad = lax.dynamic_slice_in_dim(grad_conv, own_cols, width, 1)
    grad_in_own = conv_call(conv_input_kernel, own_grad[:LONG], conv_weight, half - 1, True)
    grad_conv_in = side_by_side(grad_in_own.astype(BF), code_index)
    split = front_slots(geometry)
    padded, grads = conv_weight_inputs(conv_in[:LONG], grad_conv)
    rest_grad = conv_weight_grad(padded, grads, geometry, code_index, range(split, dp_count))
    grad_start = (grad_full + grad_conv_in.astype(F32)) * live_float
    grad_embedded, grad_gain_zero, grad_shift_zero = norm_backward(
        grad_start, normed_zero, inv_zero, glob_vec[0 : 1]
    )
    grad_patch = dot_tn(patch_rows, grad_embedded.astype(BF))
    grad_glob = jnp.stack(
        [grad_gain_zero, grad_shift_zero, jnp.sum(grad_conv_seen, axis=0), grad_mask_emb]
    )
    grad_rel = lax.dot_general(
        jnp.asarray(span_table),
        (span_first + span_second)[:HEADS],
        (((0,), (1,)), ((), ())),
        precision=HIGHEST,
    )
    leader = (code_index == 0).astype(F32)
    count_local = jnp.sum((target_codes >= 0).astype(F32))
    early = jnp.concatenate(
        [
            (grad_rel * leader).reshape(-1, 128),
            jnp.full((1, 128), loss_local * leader),
            jnp.full((1, 128), count_local * leader),
        ]
    )
    early = sum_over(sum_over(jnp.pad(early, ((0, -early.shape[0] % 8), (0, 0))), "dp"), "code")
    both = (map_first, map_second)
    sources, spans = [], [[] for _ in range(code_count)]

    def add_source(found):
        array, (chunks, base, unit, chunk) = found
        for code, items in enumerate(chunk_spans(chunks, base, unit, chunk, len(sources))):
            spans[code] += items
        sources.append(array)

    for seg_name in ("w_qkv", "w_out", "w_up", "w_down"):
        for layer_map in both:
            add_source(layer_map[seg_name])
    add_source(rest_grad)
    tail_place = geometry.place("layer_vec")
    vectors = [vector for layer_map in both for vector in layer_map["layer_vec"]]
    small = [layer_map[seg_name] for seg_name in ("gate_proj", "gate_scale") for layer_map in both]
    small = jnp.concatenate([part.reshape(-1) for part in small + [grad_rel]])
    tail_rows = geometry.begins[-1] + geometry.window - tail_place
    tail = tail_grad(vectors, small, grad_head, tail_rows)
    for items in spans:
        items.append((tail_place, tail_rows, len(sources), 0))
    sources.append(tail)
    front = jnp.concatenate([grad_patch.reshape(-1, 128), grad_glob.reshape(-1, 128)], axis=0)
    front = jnp.pad(front, ((geometry.phase, 0), (0, 0))).astype(BF)
    if split:
        own_part = pack(geometry, code_index, sources, spans, split, dp_count)
        reduced = lax.psum_scatter(own_part, "dp", scatter_dimension=0, tiled=False)
        sources, spans = [], [[] for _ in range(code_count)]
        add_source(conv_weight_grad(padded, grads, geometry, code_index, range(split)))
    for items in spans:
        items.append((0, front.shape[0], len(sources), 0))
    front, early = lax.optimization_barrier((front, early))
    sources.append(front)
    last_part = pack(geometry, code_index, sources, spans, 0, split or dp_count)
    if split:
        first = reduce_front(last_part, dp_count, dp_index)
        reduced = jnp.where(dp_index < split, first, reduced)
    else:
        reduced = lax.psum_scatter(last_part, "dp", scatter_dimension=0, tiled=False)
    reduced = lax.dynamic_slice(reduced.astype(F32), (own_offset, 0), (shard_rows, 128))
    reduced = reduced.reshape(shard_len)
    squares_all = sum_over_all(jnp.full((8, 128), jnp.sum(reduced * reduced)))
    squares_all = squares_all[0, 0]
    rel_rows = BUCKETS * HEADS // 128
    rel_all = early[:rel_rows].reshape(BUCKETS, HEADS)
    loss_all, count_all = early[rel_rows, 0], early[rel_rows + 1, 0]
    grad_norm = jnp.sqrt(squares_all) / count_all
    clip_factor = jnp.minimum(1.0, CLIP_NORM / grad_norm)
    clipped = reduced / count_all * clip_factor
    rel_grad = rel_all / count_all * clip_factor
    step_value = step_count[0].astype(F32)
    new_first = BETA_ONE * first_moment + (1.0 - BETA_ONE) * clipped
    new_second = BETA_TWO * second_moment + (1.0 - BETA_TWO) * clipped * clipped
    first_hat = new_first / (1.0 - BETA_ONE**step_value)
    second_hat = new_second / (1.0 - BETA_TWO**step_value)
    new_params = params - LEARN_RATE * (
        first_hat / (jnp.sqrt(second_hat) + ADAM_EPSILON) + WEIGHT_DECAY * params
    )
    return (
        new_params,
        new_first,
        new_second,
        new_params.astype(BF),
        loss_all / count_all,
        grad_norm,
        rel_grad,
    )


def solution(mesh):
    placed = (
        P("dp", None, None),
        P("dp"),
        P("dp", None),
        P("dp", None),
        P("code", None),
        P(("dp", "code")),
        P(("dp", "code")),
        P(("dp", "code")),
        P(),
    )
    return jax.shard_map(
        local,
        mesh=mesh,
        in_specs=placed,
        out_specs=(
            P(("dp", "code")),
            P(("dp", "code")),
            P(("dp", "code")),
            P(("dp", "code")),
            P(),
            P(),
            P(),
        ),
        check_vma=False,
    )
```

```python
import functools
import math

import jax
import jax.numpy as jnp
import numpy as np
from jax import lax
from jax.experimental import pallas as pl
from jax.experimental.pallas import tpu as pltpu
from jax.sharding import PartitionSpec as P

D = 768
HEADS = 12
HEAD_DIM = 64
FF = 3072
PATCH_IN = 256
PROJ = 256
KERNEL = 128
GROUPS = 16
WIDTH = D // GROUPS
BUCKETS = 320
MAX_DIST = 800
LAYERS = 2
LONG = 496
VISIBLE = 124
ROWS = 512
SEEN = 128
SPAN = 1024

NORM_EPSILON = 1e-05
UNIT_EPSILON = 1e-06
DEEP_ALPHA = 2.2133638394006434
LOGIT_SCALE = 25.0
CLIP_NORM = 0.005
LEARN_RATE = 0.02
BETA_ONE = 0.9
BETA_TWO = 0.999
ADAM_EPSILON = 1e-10
WEIGHT_DECAY = 0.01
MASK_FILL = -1000000000.0
HIGHEST = lax.Precision.HIGHEST
BF = jnp.bfloat16
F32 = jnp.float32
VMEM_LIMIT = 56 << 20


def layout():
    return [
        ("w_patch", (PATCH_IN, D)),
        ("glob_vec", (4, D)),
        ("conv_w", (KERNEL, WIDTH, D)),
        ("w_qkv", (LAYERS, D, 3 * D)),
        ("w_out", (LAYERS, D, D)),
        ("w_up", (LAYERS, D, FF)),
        ("w_down", (LAYERS, FF, D)),
        ("layer_vec", (LAYERS, 8 * D + FF)),
        ("gate_proj", (LAYERS, HEAD_DIM + 1, 8)),
        ("gate_scale", (LAYERS, HEADS)),
        ("rel_table", (BUCKETS, HEADS)),
        ("w_head", (D, PROJ)),
    ]


def starts():
    where = {}
    offset = 0
    for seg_name, extent in layout():
        where[seg_name] = offset
        offset += math.prod(extent)
    return where


TILE = 16


class Geometry:
    def __init__(self, dp_count, code_count, shard_rows):
        self.dp_count, self.code_count, self.shard_rows = dp_count, code_count, shard_rows
        self.shards = dp_count * code_count
        self.phase = -(starts()["conv_w"] // 128) % TILE
        self.window = -(-(shard_rows + TILE - 1) // TILE) * TILE
        self.begins = [(shard_rows * s + self.phase) // TILE * TILE for s in range(self.shards)]
        self.offsets = [(shard_rows * s + self.phase) % TILE for s in range(self.shards)]

    def place(self, seg_name, index=0):
        extent = dict(layout())[seg_name]
        amount = math.prod(extent[1:]) if index else 0
        return (starts()[seg_name] + index * amount) // 128 + self.phase

    def pieces(self, low, high):
        main, edges = [], []
        row = low
        while row < high:
            shard = max(s for s in range(self.shards) if self.begins[s] <= row)
            begin = self.begins[shard]
            if row == begin and shard > 0 and self.offsets[shard]:
                main.append((shard - 1, row - self.begins[shard - 1], row - low, TILE))
                edges.append((shard, row - low))
                row += TILE
                continue
            stop = self.begins[shard + 1] if shard + 1 < self.shards else high
            count = min(stop, high) - row
            main.append((shard, row - begin, row - low, count))
            row += count
        merged = []
        for item in main:
            last = merged[-1] if merged else None
            if last and last[0] == item[0] and last[1] + last[3] == item[1]:
                merged[-1] = last[:3] + (last[3] + item[3],)
            else:
                merged.append(item)
        return merged, edges


def bucket_onehot():
    offsets = np.arange(-(LONG - 1), LONG)
    half_count = BUCKETS // 2
    exact_count = half_count // 2
    distance = np.abs(offsets)
    scaled = (
        np.log(np.maximum(distance, 1) / exact_count)
        / np.log(MAX_DIST / exact_count)
        * (half_count - exact_count)
    )
    larger = np.minimum(exact_count + np.maximum(scaled, 0.0).astype(np.int64), half_count - 1)
    bucket = (offsets > 0) * half_count + np.where(distance < exact_count, distance, larger)
    return (bucket[:, None] == np.arange(BUCKETS)[None, :]).astype(np.float32)


def span_onehot():
    shift = SPAN // 2 - (LONG - 1)
    table = np.zeros((SPAN, BUCKETS), np.float32)
    table[shift : shift + 2 * LONG - 1] = bucket_onehot()[::-1]
    return table


def params_of(grid_rank=1):
    return pltpu.CompilerParams(
        dimension_semantics=("arbitrary",) * grid_rank, vmem_limit_bytes=VMEM_LIMIT
    )


def dot_nn(left, right):
    return lax.dot_general(left, right, (((1,), (0,)), ((), ())), preferred_element_type=F32)


def dot_nt(left, right):
    return lax.dot_general(left, right, (((1,), (1,)), ((), ())), preferred_element_type=F32)


def dot_tn(left, right):
    return lax.dot_general(left, right, (((0,), (0,)), ((), ())), preferred_element_type=F32)


TAPS = 16


def lane_masks(width):
    group = np.arange(width)[None, :] // WIDTH
    return (group == np.arange(width // WIDTH)[:, None]).astype(np.float32)


def shifted_taps(source_ref, target_ref, count):
    width = source_ref.shape[1]
    for tap in range(TAPS):
        target_ref[:, tap * width : (tap + 1) * width] = source_ref[tap : tap + count, :].astype(BF)


def conv_forward_kernel(in_ref, weight_ref, mask_ref, out_ref, taps_ref, block_ref):
    step = pl.program_id(0)
    width = weight_ref.shape[1]

    @pl.when(step == 0)
    def _():
        shifted_taps(in_ref, taps_ref, taps_ref.shape[0])
        block_ref[...] = jnp.zeros_like(block_ref)

    for tap in range(TAPS):
        piece = weight_ref[tap * WIDTH : (tap + 1) * WIDTH, :]
        for group in range(width // WIDTH):
            low = tap * width + group * WIDTH
            block_ref[low : low + WIDTH, :] = piece * mask_ref[group : group + 1, :]
    begin = pl.multiple_of(step * TAPS, TAPS)
    term = dot_nn(taps_ref[pl.ds(begin, ROWS), :], block_ref[...])

    @pl.when(step == 0)
    def _():
        out_ref[...] = term

    @pl.when(step > 0)
    def _():
        out_ref[...] += term


def conv_input_kernel(in_ref, weight_ref, mask_ref, out_ref, taps_ref, block_ref):
    step = pl.program_id(0)
    width = weight_ref.shape[1]

    @pl.when(step == 0)
    def _():
        shifted_taps(in_ref, taps_ref, taps_ref.shape[0])
        block_ref[...] = jnp.zeros_like(block_ref)

    for tap in range(TAPS):
        piece = weight_ref[tap * WIDTH : (tap + 1) * WIDTH, :]
        low = (TAPS - 1 - tap) * width
        for group in range(width // WIDTH):
            block_ref[group * WIDTH : (group + 1) * WIDTH, low : low + width] = (
                piece * mask_ref[group : group + 1, :]
            )
    begin = pl.multiple_of((pl.num_programs(0) - 1 - step) * TAPS, TAPS)
    term = dot_nt(taps_ref[pl.ds(begin, ROWS), :], block_ref[...])

    @pl.when(step == 0)
    def _():
        out_ref[...] = term

    @pl.when(step > 0)
    def _():
        out_ref[...] += term


def conv_call(kernel, conv_in, weight, front, nt):
    width = weight.shape[1]
    steps = KERNEL // TAPS
    count = ROWS + KERNEL - TAPS
    padded = jnp.pad(
        conv_in.astype(F32),
        ((front, count + TAPS - front - conv_in.shape[0]), (0, 0)),
    )
    block = (width, TAPS * width) if nt else (TAPS * width, width)
    return pl.pallas_call(
        kernel,
        grid=(steps,),
        in_specs=[
            pl.BlockSpec(padded.shape, lambda i: (0, 0)),
            pl.BlockSpec((TAPS * WIDTH, width), lambda i: (i, 0)),
            pl.BlockSpec((width // WIDTH, width), lambda i: (0, 0)),
        ],
        out_specs=pl.BlockSpec((ROWS, width), lambda i: (0, 0)),
        out_shape=jax.ShapeDtypeStruct((ROWS, width), F32),
        scratch_shapes=[pltpu.VMEM((count, TAPS * width), BF), pltpu.VMEM(block, BF)],
        compiler_params=params_of(),
    )(padded, weight, jnp.asarray(lane_masks(width), BF))


CHUNK = 6


def conv_weight_kernel(tap_ref, in_ref, grad_ref, mask_ref, out_ref, taps_ref, turn_ref, *, chunk):
    parts = in_ref.shape[0]
    begin = tap_ref[pl.program_id(0)]
    strips = D // 128
    rows = chunk * WIDTH
    for part in range(parts):
        turned = pltpu.roll(in_ref[part], in_ref.shape[2] - begin, 1)
        for tap in range(chunk):
            taps_ref[part, tap * PART : (tap + 1) * PART, :] = turned[:, tap : tap + ROWS].astype(
                BF
            )
    sums = []
    for part in range(parts):
        term = dot_nn(taps_ref[part], grad_ref[part])
        pieces = []
        for tap in range(chunk):
            total = None
            for group in range(mask_ref.shape[0]):
                low = tap * PART + group * WIDTH
                piece = term[low : low + WIDTH, :] * mask_ref[group : group + 1, :]
                total = piece if total is None else total + piece
            pieces.append(total)
        sums.append(jnp.concatenate(pieces, axis=0))
    for strip in range(strips):
        part, low = divmod(strip * 128, PART)
        columns = sums[part][:, low : min(low + 128, PART)]
        if low + 128 > PART:
            columns = jnp.concatenate([columns, sums[part + 1][:, : low + 128 - PART]], axis=1)
        turn_ref[pl.ds(strip, rows, stride=strips), :] = columns
    out_ref[...] = turn_ref[...].astype(BF)


PART = 4 * WIDTH


def owned_chunks(geometry, base, unit, count, chunk, step, slots):
    tables = []
    for code in range(geometry.code_count):
        found = []
        for slot in slots:
            begin = geometry.begins[slot * geometry.code_count + code] - base
            low = max(begin // unit, 0) // step * step
            high = min(-(-(begin + geometry.window) // unit), count)
            while low < high:
                found.append(min(low, count - chunk))
                low += chunk
        tables.append(list(dict.fromkeys(found)))
    most = max([1] + [len(table) for table in tables])
    return [(table or [0]) + (table or [0])[-1:] * (most - max(len(table), 1)) for table in tables]


def chunk_spans(chunks, base, unit, chunk, source):
    return [
        [(base + low * unit, chunk * unit, source, n * chunk * unit) for n, low in enumerate(table)]
        for table in chunks
    ]


def chunk_table(chunks, code_index):
    return lax.dynamic_index_in_dim(jnp.asarray(chunks, jnp.int32), code_index, 0, False)


def conv_weight_inputs(conv_in, grad_low):
    parts = D // PART
    front = KERNEL // 2
    padded = jnp.pad(
        jnp.transpose(conv_in).astype(F32),
        ((0, 0), (front, ROWS + KERNEL - front - conv_in.shape[0])),
    ).reshape(parts, PART, ROWS + KERNEL)
    return padded, jnp.transpose(grad_low.reshape(ROWS, parts, PART), (1, 0, 2))


def conv_weight_grad(padded, grads, geometry, code_index, slots, chunk=CHUNK):
    parts = D // PART
    masks = jnp.asarray(lane_masks(PART), F32)
    base, unit = geometry.place("conv_w"), WIDTH * D // 128
    chunks = owned_chunks(geometry, base, unit, KERNEL, chunk, 1, slots)
    table = chunk_table(chunks, code_index)
    rows = chunk * unit
    out = pl.pallas_call(
        functools.partial(conv_weight_kernel, chunk=chunk),
        grid_spec=pltpu.PrefetchScalarGridSpec(
            num_scalar_prefetch=1,
            grid=(len(chunks[0]),),
            in_specs=[
                pl.BlockSpec(padded.shape, lambda i, t: (0, 0, 0)),
                pl.BlockSpec(grads.shape, lambda i, t: (0, 0, 0)),
                pl.BlockSpec(masks.shape, lambda i, t: (0, 0)),
            ],
            out_specs=pl.BlockSpec((rows, 128), lambda i, t: (i, 0)),
            scratch_shapes=[
                pltpu.VMEM((parts, chunk * PART, ROWS), BF),
                pltpu.VMEM((rows, 128), F32),
            ],
        ),
        out_shape=jax.ShapeDtypeStruct((len(chunks[0]) * rows, 128), BF),
        compiler_params=params_of(),
    )(table, padded, grads, masks)
    return out, (chunks, base, unit, chunk)


BLOCK = 128


def half_mask(side):
    lane = lax.broadcasted_iota(jnp.int32, (1, BLOCK), 1)
    return jnp.where(lane // HEAD_DIM == side, 1.0, 0.0).astype(BF)


def toeplitz(span_ref, head):
    row = jnp.broadcast_to(span_ref[pl.ds(head, 1), :], (BLOCK, SPAN))
    return pltpu.roll(row, 0, 1, stride=1, stride_axis=0)


def hop_columns(hop):
    return [hop[:, index : index + 1] for index in range(ROWS // BLOCK)]


def seen_biases(turned, pick, near, hop):
    moved = [dot_nn(near, item.astype(BF)) for item in turned]
    columns = [jnp.broadcast_to(column, (SEEN, ROWS)) for column in hop_columns(hop)]
    tables = []
    for item in moved:
        table = None
        for index, column in enumerate(columns):
            low = index * BLOCK
            part = column * item[:, ROWS - low : SPAN - low]
            table = part if table is None else table + part
        tables.append(table.astype(BF))
    return [dot_nt(table, pick) for table in tables]


def wide(column, length):
    return jnp.concatenate([column] * (length // BLOCK), axis=1)


def attention_forward_kernel(
    q_ref, k_ref, v_ref, gate_ref, span_ref, fill_ref, out_ref, lse_ref, score_ref, turn_ref
):
    step = pl.program_id(0)
    length = q_ref.shape[0]
    values = jnp.transpose(v_ref[...])
    sides = range(2)
    turned = [toeplitz(span_ref, step * 2 + side) for side in sides]
    for side in sides:
        score_ref[side] = dot_nt(k_ref[...] * half_mask(side), q_ref[...])
    tops = []
    for side in sides:
        gate = gate_ref[pl.ds(step * 2 + side, 1), :]
        top = None
        for low in range(0, length, BLOCK):
            rows = slice(low, low + BLOCK)
            bias = turned[side][:, ROWS - low : SPAN - low]
            scores = score_ref[side, rows, :] + gate * bias + wide(fill_ref[rows, :], length)
            score_ref[side, rows, :] = scores
            most = jnp.max(scores, axis=0, keepdims=True)
            top = most if top is None else jnp.maximum(top, most)
        tops.append(top)
    totals = []
    for side in sides:
        total = None
        for low in range(0, length, BLOCK):
            rows = slice(low, low + BLOCK)
            weights = jnp.exp(score_ref[side, rows, :] - tops[side])
            part = jnp.sum(weights, axis=0, keepdims=True)
            total = part if total is None else total + part
            turn_ref[side, rows, :] = weights.astype(BF)
        totals.append(total)
    mixed = []
    for side in sides:
        lse_ref[pl.ds(step * 2 + side, 1), :] = tops[side] + jnp.log(totals[side])
        part = dot_nn(values[side * HEAD_DIM : (side + 1) * HEAD_DIM, :], turn_ref[side])
        mixed.append(part * (1.0 / totals[side]))
    out_ref[...] = jnp.transpose(jnp.concatenate(mixed, axis=0)).astype(BF)


SEEN_HEADS = 12


def seen_forward_kernel(
    q_ref, k_ref, v_ref, gate_ref, span_ref, fill_ref, pick_ref, near_ref, hop_ref,
    out_ref, lse_ref, bias_ref,
):
    heads = range(SEEN_HEADS)
    base = pl.program_id(0) * SEEN_HEADS
    pick, near, hop = pick_ref[...], near_ref[...], hop_ref[...]
    pairs = range(SEEN_HEADS // 2)
    query = [q_ref[:, pair * BLOCK : (pair + 1) * BLOCK] for pair in pairs]
    keyv = [k_ref[:, pair * BLOCK : (pair + 1) * BLOCK] for pair in pairs]
    values = [jnp.transpose(v_ref[:, pair * BLOCK : (pair + 1) * BLOCK]) for pair in pairs]
    turned = [toeplitz(span_ref, base + head) for head in heads]
    bias = seen_biases(turned, pick, near, hop)
    scores = [dot_nt(keyv[head // 2] * half_mask(head % 2), query[head // 2]) for head in heads]
    for head in heads:
        bias_ref[head * BLOCK : (head + 1) * BLOCK, :] = bias[head].astype(BF)
    scores = [
        scores[head] + gate_ref[pl.ds(base + head, 1), :] * bias[head] + fill_ref[...]
        for head in heads
    ]
    tops = [jnp.max(item, axis=0, keepdims=True) for item in scores]
    weights = [jnp.exp(scores[head] - tops[head]) for head in heads]
    totals = [jnp.sum(item, axis=0, keepdims=True) for item in weights]
    mixed = []
    for head in heads:
        lse_ref[pl.ds(base + head, 1), :] = tops[head] + jnp.log(totals[head])
        low = (head % 2) * HEAD_DIM
        part = dot_nn(values[head // 2][low : low + HEAD_DIM, :], weights[head].astype(BF))
        mixed.append(part * (1.0 / totals[head]))
    for pair in pairs:
        both = jnp.concatenate(mixed[2 * pair : 2 * pair + 2], axis=0)
        out_ref[:, pair * BLOCK : (pair + 1) * BLOCK] = jnp.transpose(both).astype(BF)


def head_specs(length, heads):
    count = HEADS // heads
    return [
        pl.BlockSpec((length, heads * HEAD_DIM), lambda i, part=part: (0, part * count + i))
        for part in range(3)
    ]


def whole_spec(shape):
    return pl.BlockSpec(shape, lambda i: (0,) * len(shape))


def attention_forward(qkv, gate, span, fill, pick):
    length = qkv.shape[0]
    heads = 2 if pick is None else SEEN_HEADS
    specs = head_specs(length, heads)
    args = [qkv, qkv, qkv, gate, span, fill] + list(pick[:3] if pick else ())
    shapes = [
        jax.ShapeDtypeStruct((length, D), BF),
        jax.ShapeDtypeStruct((16, length), F32),
    ]
    out_specs = [specs[0], whole_spec((16, length))]
    scratch = []
    if pick is None:
        kernel = attention_forward_kernel
        scratch = [pltpu.VMEM((2, length, length), F32), pltpu.VMEM((2, length, length), BF)]
    else:
        kernel = seen_forward_kernel
        out_specs.append(pl.BlockSpec((SEEN_HEADS * BLOCK, BLOCK), lambda i: (i, 0)))
        shapes.append(jax.ShapeDtypeStruct((HEADS * BLOCK, BLOCK), BF))
    found = pl.pallas_call(
        kernel,
        grid=(HEADS // heads,),
        in_specs=specs + [whole_spec(a.shape) for a in args[3:]],
        out_specs=out_specs,
        out_shape=shapes,
        scratch_shapes=scratch,
        compiler_params=params_of(),
    )(*args)
    return found[0], found[1], None if pick is None else found[2]


def diagonal_sums(turn):
    half = BLOCK // 2
    while half:
        turn = turn[:half, :] + pltpu.roll(turn[half:, :], SPAN - half, 1)
        half //= 2
    return turn


def attention_backward_kernel(
    q_ref, k_ref, v_ref, up_ref, gate_ref, span_ref, fill_ref, lse_ref,
    out_ref, sum_ref, dgate_ref, dspan_ref, prob_ref, grad_ref, turn_ref, low_ref, diag_ref,
):
    step = pl.program_id(0)
    length = q_ref.shape[0]
    sides = range(2)

    @pl.when(step == 0)
    def _():
        dspan_ref[...] = jnp.zeros_like(dspan_ref)
        dgate_ref[...] = jnp.zeros_like(dgate_ref)

    keys = jnp.transpose(k_ref[...])
    turned = [toeplitz(span_ref, step * 2 + side) for side in sides]
    for side in sides:
        prob_ref[side] = dot_nt(k_ref[...] * half_mask(side), q_ref[...])
        grad_ref[side] = dot_nt(v_ref[...] * half_mask(side), up_ref[...])
        diag_ref[side] = jnp.zeros_like(diag_ref[side])
    shared = []
    for side in sides:
        gate = gate_ref[pl.ds(step * 2 + side, 1), :]
        lse = lse_ref[pl.ds(step * 2 + side, 1), :]
        total = None
        for low in range(0, length, BLOCK):
            rows = slice(low, low + BLOCK)
            bias = turned[side][:, ROWS - low : SPAN - low]
            scores = prob_ref[side, rows, :] + gate * bias + wide(fill_ref[rows, :], length)
            probs = jnp.exp(scores - lse)
            prob_ref[side, rows, :] = probs
            low_ref[side, rows, :] = probs.astype(BF)
            part = jnp.sum(probs * grad_ref[side, rows, :], axis=0, keepdims=True)
            total = part if total is None else total + part
        shared.append(total)
    val_total = sum(dot_nn(low_ref[side], up_ref[...] * half_mask(side)) for side in sides)
    for side in sides:
        gate = gate_ref[pl.ds(step * 2 + side, 1), :]
        dgate = None
        for low in range(0, length, BLOCK):
            rows = slice(low, low + BLOCK)
            bias = turned[side][:, ROWS - low : SPAN - low]
            grad_scores = prob_ref[side, rows, :] * (grad_ref[side, rows, :] - shared[side])
            turn_ref[side, rows, :] = grad_scores.astype(BF)
            part = jnp.sum(grad_scores * bias, axis=0, keepdims=True)
            dgate = part if dgate is None else dgate + part
            diag_ref[side, :, ROWS - low : SPAN - low] += grad_scores * gate
        dgate_ref[pl.ds(step * 2 + side, 1), :] = dgate
    key_total = sum(dot_nn(turn_ref[side], q_ref[...] * half_mask(side)) for side in sides)
    halves = [
        dot_nn(keys[side * HEAD_DIM : (side + 1) * HEAD_DIM, :], turn_ref[side]) for side in sides
    ]
    for side in sides:
        dspan_ref[pl.ds(step * 2 + side, 1), :] = diagonal_sums(diag_ref[side])
    grad_query = jnp.transpose(jnp.concatenate(halves, axis=0)) * HEAD_DIM ** (-0.5)
    for part, value in enumerate((grad_query, key_total, val_total)):
        begin = pl.multiple_of(part * D + step * BLOCK, BLOCK)
        out_ref[:, pl.ds(begin, BLOCK)] = value.astype(BF)
    sum_ref[0:1, :] = jnp.sum(grad_query, axis=0, keepdims=True)
    sum_ref[1:2, :] = jnp.sum(val_total, axis=0, keepdims=True)


def split_low(value):
    high = value.astype(BF)
    return high, (value - high.astype(F32)).astype(BF)


def seen_backward_kernel(
    q_ref, k_ref, v_ref, up_ref, gate_ref, fill_ref, lse_ref, pick_ref, hop_ref, flip_ref,
    bias_ref, out_ref, sum_ref, dgate_ref, dspan_ref, diag_ref,
):
    heads, pairs = range(SEEN_HEADS), range(SEEN_HEADS // 2)
    base = pl.program_id(0) * SEEN_HEADS

    @pl.when(base == 0)
    def _():
        dspan_ref[...] = jnp.zeros_like(dspan_ref)
        dgate_ref[...] = jnp.zeros_like(dgate_ref)

    def pair_of(ref):
        return [ref[:, pair * BLOCK : (pair + 1) * BLOCK] for pair in pairs]

    query, keyv, value, upstream = (pair_of(ref) for ref in (q_ref, k_ref, v_ref, up_ref))
    keys = [jnp.transpose(item) for item in keyv]
    gate = [gate_ref[pl.ds(base + head, 1), :] for head in heads]
    bias = [bias_ref[head * BLOCK : (head + 1) * BLOCK, :].astype(F32) for head in heads]
    scores = [dot_nt(keyv[head // 2] * half_mask(head % 2), query[head // 2]) for head in heads]
    grads = [dot_nt(value[head // 2] * half_mask(head % 2), upstream[head // 2]) for head in heads]
    probs = [
        jnp.exp(
            scores[head]
            + gate[head] * bias[head]
            + fill_ref[...]
            - lse_ref[pl.ds(base + head, 1), :]
        )
        for head in heads
    ]
    shared = [jnp.sum(probs[head] * grads[head], axis=0, keepdims=True) for head in heads]
    moves = [probs[head] * (grads[head] - shared[head]) for head in heads]
    val_terms = [
        dot_nn(probs[head].astype(BF), upstream[head // 2] * half_mask(head % 2)) for head in heads
    ]
    low = [item.astype(BF) for item in moves]
    key_terms = [dot_nn(low[head], query[head // 2] * half_mask(head % 2)) for head in heads]
    halves = [
        dot_nn(keys[head // 2][(head % 2) * HEAD_DIM : (head % 2 + 1) * HEAD_DIM, :], low[head])
        for head in heads
    ]
    for head in heads:
        dgate_ref[pl.ds(base + head, 1), :] = jnp.sum(
            moves[head] * bias[head], axis=0, keepdims=True
        )
    pieces = [jnp.concatenate(split_low(moves[head] * gate[head]), axis=0) for head in heads]
    placed = [dot_nn(piece, pick_ref[...]) for piece in pieces]
    columns = [jnp.broadcast_to(column, (SEEN, ROWS)) for column in hop_columns(hop_ref[...])]
    for head in heads:
        both = placed[head][:BLOCK, :] + placed[head][BLOCK:, :]
        diag_ref[head] = jnp.zeros_like(diag_ref[head])
        for index, column in enumerate(columns):
            begin = ROWS - index * BLOCK
            diag_ref[head, :, begin : begin + ROWS] += column * both
    turns = [
        dot_nn(flip_ref[...], jnp.concatenate(split_low(diag_ref[head]), axis=0)) for head in heads
    ]
    for head in heads:
        dspan_ref[pl.ds(base + head, 1), :] = diagonal_sums(turns[head])
    for pair in pairs:
        cols = slice(pair * BLOCK, (pair + 1) * BLOCK)
        grad_query = jnp.transpose(jnp.concatenate(halves[2 * pair : 2 * pair + 2], axis=0))
        grad_query = grad_query * HEAD_DIM ** (-0.5)
        val_total = val_terms[2 * pair] + val_terms[2 * pair + 1]
        key_total = key_terms[2 * pair] + key_terms[2 * pair + 1]
        for part, value in enumerate((grad_query, key_total, val_total)):
            begin = pl.multiple_of(part * D + base * HEAD_DIM + pair * BLOCK, BLOCK)
            out_ref[:, pl.ds(begin, BLOCK)] = value.astype(BF)
        sum_ref[0:1, cols] = jnp.sum(grad_query, axis=0, keepdims=True)
        sum_ref[1:2, cols] = jnp.sum(val_total, axis=0, keepdims=True)


def attention_backward(qkv, upstream, gate, span, fill, lse, pick, bias):
    length = qkv.shape[0]
    heads = 2 if pick is None else SEEN_HEADS
    specs = head_specs(length, heads)
    shapes = [
        jax.ShapeDtypeStruct((length, 3 * D), BF),
        jax.ShapeDtypeStruct((8, D), F32),
        jax.ShapeDtypeStruct((16, length), F32),
        jax.ShapeDtypeStruct((16, SPAN), F32),
    ]
    out_specs = [
        whole_spec((length, 3 * D)),
        pl.BlockSpec((8, heads * HEAD_DIM), lambda i: (0, i)),
        whole_spec((16, length)),
        whole_spec((16, SPAN)),
    ]
    if pick is None:
        args = [qkv, qkv, qkv, upstream, gate, span, fill, lse]
        kernel, more = attention_backward_kernel, []
        scratch = [
            pltpu.VMEM((2, length, length), F32),
            pltpu.VMEM((2, length, length), F32),
            pltpu.VMEM((2, length, length), BF),
            pltpu.VMEM((2, length, length), BF),
            pltpu.VMEM((2, BLOCK, SPAN), F32),
        ]
    else:
        args = [qkv, qkv, qkv, upstream, gate, fill, lse, pick[0], pick[2], pick[3], bias]
        kernel = seen_backward_kernel
        more = [pl.BlockSpec((heads * BLOCK, BLOCK), lambda i: (i, 0))]
        scratch = [pltpu.VMEM((heads, BLOCK, SPAN), F32)]
    return pl.pallas_call(
        kernel,
        grid=(HEADS // heads,),
        in_specs=specs
        + [specs[0]]
        + [whole_spec(a.shape) for a in args[4 : len(args) - len(more)]]
        + more,
        out_specs=out_specs,
        out_shape=shapes,
        scratch_shapes=scratch,
        compiler_params=params_of(),
    )(*args)


STAGES = 4


def weight_grads_kernel(table_ref, *refs, plan):
    count = len(plan)
    lefts, rights, outs = refs[:count], refs[count : 2 * count], refs[2 * count : 3 * count]
    left_bufs, right_bufs = refs[3 * count : 4 * count], refs[4 * count : 5 * count]
    turn_ref, stage_ref, in_sems, out_sems = refs[5 * count :]
    loads = []
    for number in range(count):
        loads.append(
            [
                pltpu.make_async_copy(source, target, in_sems.at[side, number])
                for side, (source, target) in enumerate(
                    ((lefts[number], left_bufs[number]), (rights[number], right_bufs[number]))
                )
            ]
        )
    for pair in loads:
        for copy in pair:
            copy.start()

    def out_copy(number, index, slot):
        _, _, rows, strips = plan[number]
        size = rows * strips
        return pltpu.make_async_copy(
            stage_ref.at[slot, pl.ds(0, size)],
            outs[number].at[pl.ds(pl.multiple_of(index * size, TILE), size)],
            out_sems.at[slot],
        )

    pending = [None] * STAGES
    for number, (offset, steps, rows, strips) in enumerate(plan):
        for copy in loads[number]:
            copy.wait()
        base = number % 2 * 2
        for slot in (base, base + 1):
            if pending[slot] is not None:
                pending[slot].wait()
                pending[slot] = None
        size = rows * strips

        def body(index, carry, number=number, offset=offset, rows=rows, strips=strips, base=base):
            size = rows * strips
            slot = base + index % 2
            begin = pl.multiple_of(table_ref[offset + index], 128)
            grad = dot_tn(left_bufs[number][:, pl.ds(begin, rows)], right_bufs[number][...])
            for strip in range(strips):
                turn_ref[pl.ds(strip, rows, stride=strips), :] = grad[
                    :, strip * 128 : (strip + 1) * 128
                ]

            @pl.when(index >= 2)
            def _():
                out_copy(number, index - 2, slot).wait()

            stage_ref[slot, :size, :] = turn_ref[:size, :].astype(BF)
            out_copy(number, index, slot).start()
            return carry

        lax.fori_loop(0, steps, body, 0)
        for index in range(max(steps - 2, 0), steps):
            pending[base + index % 2] = out_copy(number, index, base + index % 2)
    for copy in pending:
        if copy is not None:
            copy.wait()


def weight_grads(pairs, geometry, code_index):
    slots = range(geometry.dp_count)
    plan, found, tables, shapes = [], [], [[] for _ in range(geometry.code_count)], []
    for left, right, base, rows in pairs:
        strips = right.shape[1] // 128
        chunks = owned_chunks(geometry, base, strips, left.shape[1], rows, rows, slots)
        plan.append((len(tables[0]), len(chunks[0]), rows, strips))
        for table, chunk in zip(tables, chunks):
            table += chunk
        found.append((chunks, base, strips, rows))
        shapes.append(jax.ShapeDtypeStruct((len(chunks[0]) * rows * strips, 128), BF))
    most = max(rows * strips for _, _, rows, strips in plan)
    lefts, rights = [pair[0] for pair in pairs], [pair[1] for pair in pairs]
    anywhere = pl.BlockSpec(memory_space=pl.ANY)
    outs = pl.pallas_call(
        functools.partial(weight_grads_kernel, plan=plan),
        in_specs=[pl.BlockSpec(memory_space=pltpu.SMEM)] + [anywhere] * (2 * len(pairs)),
        out_specs=[anywhere] * len(pairs),
        out_shape=shapes,
        scratch_shapes=[pltpu.VMEM(a.shape, BF) for a in lefts + rights]
        + [
            pltpu.VMEM((most, 128), F32),
            pltpu.VMEM((STAGES, most, 128), BF),
            pltpu.SemaphoreType.DMA((2, len(pairs))),
            pltpu.SemaphoreType.DMA((STAGES,)),
        ],
        compiler_params=pltpu.CompilerParams(vmem_limit_bytes=VMEM_LIMIT),
    )(chunk_table(tables, code_index), *lefts, *rights)
    return list(zip(outs, found))


def unpack_jobs(geometry, specs):
    jobs = []
    for target, (base, depth, strips, rows) in enumerate(specs):
        for low in range(0, depth, rows):
            begin = base + low * strips
            jobs.append((target, low, rows, strips) + geometry.pieces(begin, begin + rows * strips))
    return jobs


DEPTH = 4


def stream_jobs(jobs, source_ref, buffer_ref, edge_ref, sems, work):
    def copies(number):
        main, edges = jobs[number][4:6]
        slot = number % DEPTH
        found = []
        for shard, begin, low, count in main:
            found.append(
                (source_ref.at[shard, pl.ds(begin, count)], buffer_ref.at[slot, pl.ds(low, count)])
            )
        for place, (shard, _) in enumerate(edges):
            found.append((source_ref.at[shard, pl.ds(0, TILE)], edge_ref.at[slot, place]))
        return [
            pltpu.make_async_copy(source, target, sems.at[slot, index])
            for index, (source, target) in enumerate(found)
        ]

    for number in range(min(DEPTH - 1, len(jobs))):
        for copy in copies(number):
            copy.start()
    for number, job in enumerate(jobs):
        if number + DEPTH - 1 < len(jobs):
            for copy in copies(number + DEPTH - 1):
                copy.start()
        for copy in copies(number):
            copy.wait()
        slot = number % DEPTH
        for place, (_, low) in enumerate(job[5]):
            buffer_ref[slot, low : low + TILE, :] += edge_ref[slot, place]
        work(number, job, slot)


def unpack_kernel(*refs, jobs, stages):
    source_ref = refs[0]
    targets = refs[1 : 1 + len(stages)]
    buffer_ref, edge_ref, turn_ref, sems, out_sems = refs[1 + len(stages) : 6 + len(stages)]
    stage_refs = refs[6 + len(stages) :]
    pending = {}

    def work(number, job, slot):
        target, low, rows, strips = job[:4]
        stage_ref, key = stage_refs[stages[target]], (stages[target], slot)
        if key in pending:
            pending.pop(key).wait()
        turn_ref[: rows * strips, :] = buffer_ref[slot, : rows * strips, :].astype(F32)
        for strip in range(strips):
            stage_ref[slot, :rows, strip * 128 : (strip + 1) * 128] = turn_ref[
                pl.ds(strip, rows, stride=strips), :
            ].astype(BF)
        copy = pltpu.make_async_copy(
            stage_ref.at[slot, pl.ds(0, rows)],
            targets[target].at[pl.ds(low, rows)],
            out_sems.at[stages[target], slot],
        )
        copy.start()
        pending[key] = copy

    stream_jobs(jobs, source_ref, buffer_ref, edge_ref, sems, work)
    for copy in pending.values():
        copy.wait()


def unpack(geometry, windows, specs):
    jobs = unpack_jobs(geometry, specs)
    kinds = sorted({spec[2] for spec in specs})
    stages = [kinds.index(spec[2]) for spec in specs]
    most = max(job[2] * job[3] for job in jobs)
    copies = max(len(job[4]) + len(job[5]) for job in jobs)
    edges = max([1] + [len(job[5]) for job in jobs])
    return pl.pallas_call(
        functools.partial(unpack_kernel, jobs=jobs, stages=stages),
        in_specs=[pl.BlockSpec(memory_space=pl.ANY)],
        out_specs=[pl.BlockSpec(memory_space=pl.ANY)] * len(specs),
        out_shape=[jax.ShapeDtypeStruct((s[1], s[2] * 128), BF) for s in specs],
        scratch_shapes=[
            pltpu.VMEM((DEPTH, most, 128), BF),
            pltpu.VMEM((DEPTH, edges, TILE, 128), BF),
            pltpu.VMEM((most, 128), F32),
            pltpu.SemaphoreType.DMA((DEPTH, copies)),
            pltpu.SemaphoreType.DMA((len(kinds), DEPTH)),
        ]
        + [
            pltpu.VMEM((DEPTH, max(s[3] for s in specs if s[2] == kind), kind * 128), BF)
            for kind in kinds
        ],
        compiler_params=pltpu.CompilerParams(vmem_limit_bytes=VMEM_LIMIT),
    )(windows)


def unpack_conv_kernel(
    code_ref, source_ref, target_ref, buffer_ref, edge_ref, turn_ref, stage_ref, sems, out_sems, *,
    jobs, width
):
    first = code_ref[0] * width
    strip = first // 128
    strips = D // 128
    lead = first - strip * 128
    pending = {}

    def work(number, job, slot):
        low, rows = job[1], job[2]
        if slot in pending:
            pending.pop(slot).wait()
        turn_ref[...] = buffer_ref[slot].astype(F32)
        one = turn_ref[pl.ds(strip, rows, stride=strips), :]
        two = turn_ref[pl.ds(jnp.minimum(strip + 1, strips - 1), rows, stride=strips), :]
        pair = pltpu.roll(jnp.concatenate([one, two], axis=1), lax.rem(256 - lead, 256), 1)
        stage_ref[slot] = pair[:, :width].astype(BF)
        copy = pltpu.make_async_copy(
            stage_ref.at[slot], target_ref.at[pl.ds(low, rows)], out_sems.at[slot]
        )
        copy.start()
        pending[slot] = copy

    stream_jobs(jobs, source_ref, buffer_ref, edge_ref, sems, work)
    for copy in pending.values():
        copy.wait()


def unpack_conv(geometry, windows, code_index, rows=768):
    width = D // geometry.code_count
    depth = KERNEL * WIDTH
    jobs = unpack_jobs(geometry, [(geometry.place("conv_w"), depth, D // 128, rows)])
    copies = max(len(job[4]) + len(job[5]) for job in jobs)
    edges = max([1] + [len(job[5]) for job in jobs])
    return pl.pallas_call(
        functools.partial(unpack_conv_kernel, jobs=jobs, width=width),
        in_specs=[
            pl.BlockSpec(memory_space=pltpu.SMEM),
            pl.BlockSpec(memory_space=pl.ANY),
        ],
        out_specs=pl.BlockSpec(memory_space=pl.ANY),
        out_shape=jax.ShapeDtypeStruct((depth, width), BF),
        scratch_shapes=[
            pltpu.VMEM((DEPTH, rows * D // 128, 128), BF),
            pltpu.VMEM((DEPTH, edges, TILE, 128), BF),
            pltpu.VMEM((rows * D // 128, 128), F32),
            pltpu.VMEM((DEPTH, rows, width), BF),
            pltpu.SemaphoreType.DMA((DEPTH, copies)),
            pltpu.SemaphoreType.DMA((DEPTH,)),
        ],
        compiler_params=pltpu.CompilerParams(vmem_limit_bytes=VMEM_LIMIT),
    )(jnp.full((1,), code_index, jnp.int32), windows)


def small_kernel(
    source_ref, patch_ref, glob_ref, vec_ref, up_ref, rest_ref, head_ref,
    buffer_ref, edge_ref, turn_ref, head_turn_ref, sems, *, jobs, phase, lead, whole
):
    strips = D // 128

    def columns(target_ref, begin, count, kind):
        for strip in range(strips):
            target_ref[:, strip * 128 : (strip + 1) * 128] = turn_ref[
                pl.ds(begin + strip, count, stride=strips), :
            ].astype(kind)

    def work(number, job, slot):
        turn_ref[: job[2], :] = buffer_ref[slot, : job[2], :].astype(F32)
        if number == 0:
            columns(patch_ref, phase, PATCH_IN, BF)
            columns(glob_ref, phase + PATCH_IN * strips, 4, F32)
            return
        count = vec_ref.shape[0]
        columns(vec_ref, 0, count, F32)
        wide = FF // 128
        for layer in range(LAYERS):
            begin = (layer + 1) * (count // LAYERS) * strips - wide
            for strip in range(wide):
                up_ref[layer : layer + 1, strip * 128 : (strip + 1) * 128] = turn_ref[
                    begin + strip : begin + strip + 1, :
                ]
        begin = count * strips
        rest_ref[...] = turn_ref[begin : begin + rest_ref.shape[0], :]
        begin += whole
        rows = head_turn_ref.shape[0]
        turned = turn_ref[begin : begin + rows, :]
        if lead:
            lane = lax.broadcasted_iota(jnp.int32, (1, 128), 1)
            turned = jnp.where(
                lane < 128 - lead,
                pltpu.roll(turned, 128 - lead, 1),
                pltpu.roll(turn_ref[begin + 1 : begin + 1 + rows, :], 128 - lead, 1),
            )
        head_turn_ref[...] = turned
        for strip in range(PROJ // 128):
            head_ref[:, strip * 128 : (strip + 1) * 128] = head_turn_ref[
                pl.ds(strip, D, stride=PROJ // 128), :
            ].astype(BF)

    stream_jobs(jobs, source_ref, buffer_ref, edge_ref, sems, work)


def unpack_small(geometry, windows):
    where = starts()
    tail = geometry.place("layer_vec")
    regions = [(0, geometry.place("conv_w")), (tail, geometry.begins[-1] + geometry.window)]
    jobs = [
        (0, 0, high - low, 1) + geometry.pieces(low, high) for low, high in regions
    ]
    most = max(job[2] for job in jobs)
    copies = max(len(job[4]) + len(job[5]) for job in jobs)
    edges = max([1] + [len(job[5]) for job in jobs])
    slots = LAYERS * (8 + FF // D)
    offset = where["w_head"] - where["gate_proj"]
    rest = -(-(-(-offset // 128)) // 8) * 8
    return pl.pallas_call(
        functools.partial(
            small_kernel, jobs=jobs, phase=geometry.phase, lead=offset % 128, whole=offset // 128
        ),
        in_specs=[pl.BlockSpec(memory_space=pl.ANY)],
        out_shape=[
            jax.ShapeDtypeStruct((PATCH_IN, D), BF),
            jax.ShapeDtypeStruct((4, D), F32),
            jax.ShapeDtypeStruct((slots, D), F32),
            jax.ShapeDtypeStruct((LAYERS, FF), F32),
            jax.ShapeDtypeStruct((rest, 128), F32),
            jax.ShapeDtypeStruct((D, PROJ), BF),
        ],
        scratch_shapes=[
            pltpu.VMEM((DEPTH, most, 128), BF),
            pltpu.VMEM((DEPTH, edges, TILE, 128), BF),
            pltpu.VMEM((most, 128), F32),
            pltpu.VMEM((D * PROJ // 128, 128), F32),
            pltpu.SemaphoreType.DMA((DEPTH, copies)),
        ],
        compiler_params=pltpu.CompilerParams(vmem_limit_bytes=VMEM_LIMIT),
    )(windows)


def pack_kernel(code_ref, *refs, plans, empty):
    sources, out_ref, sems = refs[:-2], refs[-2], refs[-1]
    turn = code_ref[1]
    for slot in range(empty):
        out_ref[slot] = jnp.zeros_like(out_ref[slot])
    for code, plan in enumerate(plans):

        @pl.when(code_ref[0] == code)
        def _():
            copies = [
                pltpu.make_async_copy(
                    sources[source].at[pl.ds(begin, count)],
                    out_ref.at[jnp.bitwise_xor(slot, turn), pl.ds(low, count)],
                    sems.at[index],
                )
                for index, (source, begin, slot, low, count) in enumerate(plan)
            ]
            for copy in copies:
                copy.start()
            for copy in copies:
                copy.wait()


def pack_plans(geometry, spans, slots):
    plans = []
    for code in range(geometry.code_count):
        plan = []
        for slot in slots:
            begin = geometry.begins[slot * geometry.code_count + code]
            stop = begin + geometry.window
            row = begin
            while row < stop:
                place, rows, source, inner = next(
                    item for item in spans[code] if item[0] <= row < item[0] + item[1]
                )
                count = min(stop, place + rows) - row
                plan.append((source, inner + row - place, slot, row - begin, count))
                row += count
        plans.append(plan)
    return plans


def pack(geometry, code_index, sources, spans, low, high, turn=0):
    plans = pack_plans(geometry, spans, range(low, high))
    return pl.pallas_call(
        functools.partial(pack_kernel, plans=plans, empty=low),
        in_specs=[pl.BlockSpec(memory_space=pltpu.SMEM)]
        + [pl.BlockSpec(memory_space=pl.ANY)] * len(sources),
        out_specs=pl.BlockSpec(memory_space=pltpu.VMEM),
        out_shape=jax.ShapeDtypeStruct((high, geometry.window, 128), BF),
        scratch_shapes=[pltpu.SemaphoreType.DMA((max(len(plan) for plan in plans),))],
        compiler_params=pltpu.CompilerParams(vmem_limit_bytes=VMEM_LIMIT),
    )(jnp.stack([code_index, jnp.int32(turn)]).astype(jnp.int32), *sources)


def front_slots(geometry):
    stop = geometry.place("w_qkv")
    count = sum(
        geometry.begins[slot * geometry.code_count + geometry.code_count - 1] + geometry.window
        <= stop
        for slot in range(geometry.dp_count)
    )
    if geometry.dp_count & (geometry.dp_count - 1) or not count:
        return 0
    return 1 << (count.bit_length() - 1)


def add_low(left, right):
    return (left.astype(F32) + right.astype(F32)).astype(BF)


def reduce_front(held, dp_count):
    count = held.shape[0]
    bit = count // 2
    while bit:
        moved = lax.ppermute(held[bit:], "dp", [(i, i ^ bit) for i in range(dp_count)])
        held = add_low(held[:bit], moved)
        bit //= 2
    bits = []
    while count < dp_count:
        bits.append(count)
        count *= 2
    middle = held.shape[1] // (2 * TILE) * TILE
    halves = [held[0, :middle], held[0, middle:]]
    for number in range(len(bits)):
        for side, bit in enumerate((bits[number], bits[-1 - number])):
            moved = lax.ppermute(
                halves[side], "dp", [(i, i - bit) for i in range(dp_count) if i & bit]
            )
            halves[side] = add_low(halves[side], moved)
    return jnp.concatenate(halves, axis=0)


def tail_kernel(*refs, lead, whole):
    vectors = refs[:-4]
    small_ref, head_ref, out_ref, turn_ref = refs[-4:]
    begin = 0
    for vector_ref in vectors:
        if len(vector_ref.shape) == 2:
            for row in range(2):
                for low in range(0, D, 128):
                    turn_ref[begin : begin + 1, :] = vector_ref[row : row + 1, low : low + 128]
                    begin += 1
        else:
            for low in range(0, vector_ref.shape[0], 128):
                turn_ref[begin : begin + 1, :] = vector_ref[low : low + 128].reshape(1, 128)
                begin += 1
    turn_ref[begin:, :] = jnp.zeros((turn_ref.shape[0] - begin, 128), F32)
    turn_ref[begin : begin + small_ref.shape[0], :] = small_ref[...]
    begin += whole
    rows = head_ref.shape[0]
    turned = pltpu.roll(head_ref[...], lead, 1) if lead else head_ref[...]
    lane = lax.broadcasted_iota(jnp.int32, (1, 128), 1)
    turn_ref[begin : begin + rows, :] += jnp.where(lane >= lead, turned, 0.0)
    turn_ref[begin + 1 : begin + 1 + rows, :] += jnp.where(lane < lead, turned, 0.0)
    out_ref[...] = turn_ref[...].astype(BF)


def tail_grad(vectors, small, grad_head, rows):
    lead, whole = small.shape[0] % 128, small.shape[0] // 128
    small = jnp.pad(small, (0, -small.shape[0] % 128)).reshape(-1, 128)
    return pl.pallas_call(
        functools.partial(tail_kernel, lead=lead, whole=whole),
        out_shape=jax.ShapeDtypeStruct((rows, 128), BF),
        scratch_shapes=[pltpu.VMEM((rows, 128), F32)],
        compiler_params=pltpu.CompilerParams(vmem_limit_bytes=VMEM_LIMIT),
    )(*vectors, small, grad_head)


def blocks_of_code(block):
    count = lax.axis_size("code")
    return [block] + [
        lax.ppermute(block, "code", [(i, (i + step) % count) for i in range(count)])
        for step in range(1, count)
    ]


def side_kernel(code_ref, *refs):
    blocks, out_ref = refs[:-1], refs[-1]
    count, width = len(blocks), blocks[0].shape[1]
    for code in range(count):

        @pl.when(code_ref[0] == code)
        def _():
            for source in range(count):
                out_ref[:, source * width : (source + 1) * width] = blocks[
                    (code - source) % count
                ][...]


def side_by_side(block, code_index):
    blocks = blocks_of_code(block)
    rows, width = block.shape
    return pl.pallas_call(
        side_kernel,
        in_specs=[pl.BlockSpec(memory_space=pltpu.SMEM)]
        + [pl.BlockSpec(memory_space=pltpu.VMEM)] * len(blocks),
        out_specs=pl.BlockSpec(memory_space=pltpu.VMEM),
        out_shape=jax.ShapeDtypeStruct((rows, width * len(blocks)), block.dtype),
    )(jnp.full((1,), code_index, jnp.int32), *blocks)


def sum_over(value, axis):
    count = lax.axis_size(axis)
    if count & (count - 1):
        return lax.psum(value, axis)
    bit = 1
    while bit < count:
        value = value + lax.ppermute(value, axis, [(i, i ^ bit) for i in range(count)])
        bit *= 2
    return value


def sum_over_all(value):
    count = lax.axis_size("dp") * lax.axis_size("code")
    sent = jnp.broadcast_to(value[None], (count,) + value.shape)
    return jnp.sum(lax.all_to_all(sent, ("dp", "code"), 0, 0), axis=0)


def norm_forward(before, norm_gain, norm_shift):
    centred = before - jnp.mean(before, axis=-1, keepdims=True)
    inv_std = lax.rsqrt(jnp.mean(centred * centred, axis=-1, keepdims=True) + NORM_EPSILON)
    normed = centred * inv_std
    return (normed * norm_gain + norm_shift, normed, inv_std)


def norm_backward(upstream, normed, inv_std, norm_gain):
    scaled = upstream * norm_gain
    centred_grad = (
        scaled
        - jnp.mean(scaled, axis=-1, keepdims=True)
        - normed * jnp.mean(scaled * normed, axis=-1, keepdims=True)
    )
    return (
        centred_grad * inv_std,
        jnp.sum(upstream * normed, axis=0),
        jnp.sum(upstream, axis=0),
    )


def gelu(pre_act):
    return 0.5 * pre_act * (1.0 + lax.erf(pre_act * 0.7071067811865476))


def gelu_grad(pre_act):
    return (
        0.5 * (1.0 + lax.erf(pre_act * 0.7071067811865476))
        + pre_act * jnp.exp(-0.5 * pre_act * pre_act) * 0.3989422804014327
    )


def vec_part(vector, slot_index):
    return vector[slot_index : slot_index + 1]


def gate_maps():
    rows = (np.arange(D)[:, None] % HEAD_DIM == np.arange(HEAD_DIM)[None, :]).astype(np.float32)
    groups = np.arange(8)[:, None] // 4 == np.arange(2 * HEADS)[None, :] // HEADS
    own = np.arange(D)[:, None] // HEAD_DIM == np.arange(2 * HEADS)[None, :] % HEADS
    return rows, groups.astype(np.float32), own.astype(np.float32)


def exact_dot(left, right, dims=((1,), (0,))):
    return lax.dot_general(left, right, (dims, ((), ())), precision=HIGHEST)


def gate_columns(gate_weight):
    rows, groups, own = gate_maps()
    wide = gate_weight.astype(F32)
    sums = exact_dot(wide, jnp.asarray(groups))
    return exact_dot(jnp.asarray(rows), sums[:HEAD_DIM]) * own, sums[HEAD_DIM:]


def gate_forward(in_low, weights):
    columns, bias = weights["gate_columns"]
    high = columns.astype(BF)
    rest = (columns - high.astype(F32)).astype(BF)
    logit = dot_nn(in_low, jnp.concatenate([high, rest], axis=1))
    logit = logit[:, : 2 * HEADS] + logit[:, 2 * HEADS :] + bias
    pair = jax.nn.sigmoid(logit)
    first, second = pair[:, :HEADS], pair[:, HEADS:]
    gate_vals = first * (second * weights["gate_scale"].astype(F32) - 1.0) + 2.0
    return (gate_vals, first, second)


def gate_backward(grad_gate, first, second, in_low, weights):
    scale_vec = weights["gate_scale"].astype(F32)
    grad_scale = jnp.sum(grad_gate * first * second, axis=0)
    grad_one = grad_gate * (second * scale_vec - 1.0) * first * (1.0 - first)
    grad_two = grad_gate * first * scale_vec * second * (1.0 - second)
    both = jnp.concatenate([grad_one, grad_two], axis=1)
    rows, groups, own = gate_maps()
    high = both.astype(BF)
    rest = (both - high.astype(F32)).astype(BF)
    product = dot_tn(in_low, jnp.concatenate([high, rest], axis=1))
    product = (product[:, : 2 * HEADS] + product[:, 2 * HEADS :]) * own
    summed = exact_dot(jnp.asarray(rows), product, ((0,), (0,)))
    summed = jnp.concatenate([summed, jnp.sum(both, axis=0, keepdims=True)], axis=0)
    grad_proj = exact_dot(summed, jnp.asarray(groups), ((1,), (1,)))
    columns_high, columns_rest = split_low(weights["gate_columns"][0])
    grad_heads = dot_nt(
        jnp.concatenate([high, rest, high], axis=1),
        jnp.concatenate([columns_high, columns_high, columns_rest], axis=1),
    )
    return (grad_heads, grad_proj, grad_scale)


def layer_forward(hidden, fill, weights, span, pick):
    vector = weights["layer_vec"]
    in_low = hidden.astype(BF)
    shift = jnp.concatenate(
        [vec_part(vector, 0), jnp.zeros((1, D), F32), vec_part(vector, 1)], axis=1
    )
    scale = np.ones((1, 3 * D), np.float32)
    scale[:, :D] = HEAD_DIM ** (-0.5)
    qkv_low = ((dot_nn(in_low, weights["w_qkv"]) + shift) * scale).astype(BF)
    gate_vals, first, second = gate_forward(in_low, weights)
    gate_wide = jnp.pad(jnp.transpose(gate_vals), ((0, 16 - HEADS), (0, 0)))
    attended, lse, bias = attention_forward(qkv_low, gate_wide, span, fill, pick)
    attn_out = dot_nn(attended, weights["w_out"]) + vec_part(vector, 2)
    mid_rows, normed_one, inv_one = norm_forward(
        DEEP_ALPHA * hidden + attn_out, vec_part(vector, 3), vec_part(vector, 4)
    )
    mid_low = mid_rows.astype(BF)
    pre_act = dot_nn(mid_low, weights["w_up"]) + weights["up_bias"]
    act_low = gelu(pre_act).astype(BF)
    ffn_out = dot_nn(act_low, weights["w_down"]) + vec_part(vector, 5)
    final_rows, normed_two, inv_two = norm_forward(
        DEEP_ALPHA * mid_rows + ffn_out, vec_part(vector, 6), vec_part(vector, 7)
    )
    kept = (in_low, qkv_low, gate_wide, first, second, lse, attended, bias)
    kept += (mid_low, pre_act, act_low, normed_one, inv_one, normed_two, inv_two)
    return (final_rows, kept)


def layer_backward(upstream, kept, fill, weights, span, pick, grad_of):
    in_low, qkv_low, gate_wide, first, second, lse, attended, bias = kept[:8]
    mid_low, pre_act, act_low, normed_one, inv_one, normed_two, inv_two = kept[8:]
    vector = weights["layer_vec"]
    grad_res_two, grad_gain_two, grad_shift_two = norm_backward(
        upstream, normed_two, inv_two, vec_part(vector, 6)
    )
    ffn_low = grad_res_two.astype(BF)
    grad_down = grad_of("w_down", act_low, ffn_low, 512)
    grad_pre = dot_nt(ffn_low, weights["w_down"]) * gelu_grad(pre_act)
    pre_low = grad_pre.astype(BF)
    grad_up = grad_of("w_up", mid_low, pre_low, 256)
    grad_mid = DEEP_ALPHA * grad_res_two + dot_nt(pre_low, weights["w_up"])
    grad_res_one, grad_gain_one, grad_shift_one = norm_backward(
        grad_mid, normed_one, inv_one, vec_part(vector, 3)
    )
    out_low = grad_res_one.astype(BF)
    grad_out = grad_of("w_out", attended, out_low, 384)
    grad_att = dot_nt(out_low, weights["w_out"]).astype(BF)
    proj_low, part_sums, grad_gate, grad_span = attention_backward(
        qkv_low, grad_att, gate_wide, span, fill, lse, pick, bias
    )
    grad_heads, grad_gate_proj, grad_gate_scale = gate_backward(
        jnp.transpose(grad_gate[:HEADS]), first, second, in_low, weights
    )
    grad_qkv = grad_of("w_qkv", in_low, proj_low, 256)
    grad_hidden = DEEP_ALPHA * grad_res_one + dot_nt(proj_low, weights["w_qkv"]) + grad_heads
    grad_vec = [
        part_sums,
        jnp.sum(grad_res_one, axis=0),
        grad_gain_one,
        grad_shift_one,
        jnp.sum(grad_res_two, axis=0),
        grad_gain_two,
        grad_shift_two,
        jnp.sum(grad_pre, axis=0),
    ]
    grad_map = {
        "w_qkv": grad_qkv,
        "w_out": grad_out,
        "w_up": grad_up,
        "w_down": grad_down,
        "layer_vec": grad_vec,
        "gate_proj": grad_gate_proj,
        "gate_scale": grad_gate_scale,
    }
    return (grad_hidden, grad_map, grad_span)


def head_kernel(
    in_ref, weight_ref, code_ref, name_ref, target_ref, loss_ref, rows_ref, flat_ref, low_ref
):
    weight, codebook, names = weight_ref[...], code_ref[...], name_ref[0:1, :]
    loss = jnp.zeros((1, 1), F32)
    for low in range(0, in_ref.shape[0], BLOCK):
        rows = slice(low, low + BLOCK)
        projected = dot_nn(in_ref[rows, :], weight)
        inv_len = lax.rsqrt(jnp.sum(projected * projected, axis=1, keepdims=True) + UNIT_EPSILON)
        unit_rows = projected * inv_len
        logits = LOGIT_SCALE * dot_nt(unit_rows.astype(BF), codebook)
        target = target_ref[rows, 0:1]
        live = jnp.where(target >= 0, 1.0, 0.0)
        hits = jnp.where(names == target, 1.0, 0.0)
        top = jnp.max(logits, axis=1, keepdims=True)
        weights = jnp.exp(logits - top)
        total = jnp.sum(weights, axis=1, keepdims=True)
        picked = jnp.sum(logits * hits, axis=1, keepdims=True)
        loss += jnp.sum((top + jnp.log(total) - picked) * live, axis=0, keepdims=True)
        grad_logits = (weights * (1.0 / total) - hits) * (live * LOGIT_SCALE)
        grad_unit = dot_nn(grad_logits.astype(BF), codebook)
        grad_proj = (
            grad_unit - unit_rows * jnp.sum(unit_rows * grad_unit, axis=1, keepdims=True)
        ) * inv_len
        proj_low = grad_proj.astype(BF)
        low_ref[rows, :] = proj_low
        rows_ref[rows, :] = dot_nt(proj_low, weight)
    loss_ref[...] = jnp.broadcast_to(loss, loss_ref.shape)
    grad = dot_tn(in_ref[...], low_ref[...])
    strips = PROJ // 128
    for strip in range(strips):
        flat_ref[pl.ds(strip, D, stride=strips), :] = grad[:, strip * 128 : (strip + 1) * 128]


def head_pass(hidden, w_head, codebook, names, targets):
    loss, grad_rows, grad_head = pl.pallas_call(
        head_kernel,
        out_shape=[
            jax.ShapeDtypeStruct((8, 128), F32),
            jax.ShapeDtypeStruct((ROWS, D), F32),
            jax.ShapeDtypeStruct((D * PROJ // 128, 128), F32),
        ],
        scratch_shapes=[pltpu.VMEM((ROWS, PROJ), BF)],
        compiler_params=pltpu.CompilerParams(vmem_limit_bytes=VMEM_LIMIT),
    )(hidden.astype(BF), w_head, codebook, names, targets)
    return (loss[0, 0], grad_rows, grad_head)


def local(
    patches,
    lengths,
    patch_masks,
    targets,
    codebook,
    params,
    first_moment,
    second_moment,
    step_count,
):
    dp_count = lax.axis_size("dp")
    code_count = lax.axis_size("code")
    code_index = lax.axis_index("code")
    shard_len = params.shape[0]
    shard_rows = shard_len // 128
    dp_index = lax.axis_index("dp")
    geometry = Geometry(dp_count, code_count, shard_rows)
    own_offset = lax.rem((dp_index * code_count + code_index) * shard_rows + geometry.phase, TILE)
    own_window = lax.dynamic_update_slice(
        jnp.zeros((geometry.window, 128), F32), params.reshape(shard_rows, 128), (own_offset, 0)
    ).astype(BF)
    windows = lax.all_gather(own_window, ("dp", "code"), axis=0, tiled=False)
    where = starts()

    places = jnp.arange(ROWS, dtype=jnp.int32)
    mask_row = jnp.pad(patch_masks[0], (0, ROWS - LONG))
    live_slot = places < jnp.minimum(lengths[0], LONG)
    visible = live_slot & (mask_row == 0)
    rank = jnp.cumsum(visible.astype(jnp.int32)) - 1
    pick = (
        visible[None, :] & (rank[None, :] == jnp.arange(SEEN, dtype=jnp.int32)[:, None])
    )
    pick_low = pick.astype(BF)
    near = jnp.sum(pick_low.reshape(SEEN, ROWS // BLOCK, BLOCK), axis=1)
    hop = jnp.sum(pick.astype(F32).reshape(SEEN, ROWS // BLOCK, BLOCK), axis=2)
    flip = jnp.concatenate([jnp.transpose(near)] * 2, axis=1)
    pick_seen = (pick_low, near, jnp.pad(hop, ((0, 0), (0, BLOCK - ROWS // BLOCK))), flip)
    pick_full = pick.astype(F32)
    seen_valid = jnp.arange(SEEN, dtype=jnp.int32) < lengths[0] // 4
    seen_fill = jnp.broadcast_to(jnp.where(seen_valid, 0.0, MASK_FILL)[:, None], (SEEN, BLOCK))
    live_fill = jnp.broadcast_to(jnp.where(live_slot, 0.0, MASK_FILL)[:, None], (ROWS, BLOCK))
    live_float = live_slot.astype(F32)[:, None]
    all_codes = jnp.concatenate(blocks_of_code(codebook), axis=0)
    code_places = (
        code_index - jnp.arange(code_count, dtype=jnp.int32) + code_count
    ) % code_count * codebook.shape[0]
    code_names = (
        code_places[:, None] + jnp.arange(codebook.shape[0], dtype=jnp.int32)[None, :]
    ).reshape(1, -1)
    patch_rows = jnp.pad(patches[0], ((0, ROWS - LONG), (0, 0)))
    target_codes = jnp.where(mask_row == 1, jnp.pad(targets[0], (0, ROWS - LONG)), -1)
    target_wide = jnp.broadcast_to(target_codes[:, None], (ROWS, 128))
    name_wide = jnp.broadcast_to(code_names, (8, code_names.shape[1]))
    w_patch, glob_vec, vectors, up_bias, rest, w_head = unpack_small(geometry, windows)
    rest = rest.reshape(-1)

    def values(seg_name):
        extent = dict(layout())[seg_name]
        begin = where[seg_name] - where["gate_proj"]
        return rest[begin : begin + math.prod(extent)].reshape(extent)

    gate_proj = values("gate_proj")
    gate_scale = values("gate_scale")
    rel_table = values("rel_table").astype(BF)
    conv_weight = unpack_conv(geometry, windows, code_index)
    specs = [
        spec
        for index in range(LAYERS)
        for spec in (
            (geometry.place("w_qkv", index), D, 3 * D // 128, 128),
            (geometry.place("w_out", index), D, D // 128, 384),
            (geometry.place("w_up", index), D, FF // 128, 128),
            (geometry.place("w_down", index), FF, D // 128, 512),
        )
    ]
    unpacked = unpack(geometry, windows, specs)
    weights = []
    for index in range(LAYERS):
        mats = unpacked[4 * index : 4 * index + 4]
        weights.append(
            dict(zip(("w_qkv", "w_out", "w_up", "w_down"), mats))
            | {
                "layer_vec": vectors[index * (8 + FF // D) :],
                "up_bias": up_bias[index : index + 1],
                "gate_columns": gate_columns(gate_proj[index]),
                "gate_scale": gate_scale[index],
            }
        )

    span_table = span_onehot()
    span = dot_tn(
        jnp.pad(rel_table, ((0, 0), (0, 16 - HEADS))), jnp.asarray(span_table.T, BF)
    )

    embedded = dot_nn(patch_rows, w_patch)
    normed_rows, normed_zero, inv_zero = norm_forward(embedded, glob_vec[0 : 1], glob_vec[1 : 2])
    start_rows = normed_rows * live_float
    conv_in = start_rows.astype(BF)
    width = D // code_count
    own_cols = code_index * width
    own_in = lax.dynamic_slice_in_dim(conv_in, own_cols, width, 1)
    half = KERNEL // 2
    conv_own = conv_call(conv_forward_kernel, own_in[:LONG], conv_weight, half, False)
    seen_own = lax.dot_general(
        pick_full, conv_own, (((1,), (0,)), ((), ())), precision=HIGHEST
    )
    seen_raw = side_by_side(seen_own, code_index)
    seen_pre = seen_raw + glob_vec[2 : 3]
    seen_start = lax.dot_general(
        pick_full, start_rows, (((1,), (0,)), ((), ())), precision=HIGHEST
    )
    seen_rows = seen_start + gelu(seen_pre)
    encoded, kept_first = layer_forward(seen_rows, seen_fill, weights[0], span, pick_seen)
    placed = lax.dot_general(
        pick_full, encoded, (((0,), (0,)), ((), ())), precision=HIGHEST
    )
    hidden = jnp.where(visible[:, None], placed, glob_vec[3 : 4])
    final, kept_second = layer_forward(hidden, live_fill, weights[1], span, None)
    loss_local, upstream, grad_head = head_pass(final, w_head, all_codes, name_wide, target_wide)

    def grad_maker(index):
        return lambda seg_name, left, right, rows: (
            left, right, geometry.place(seg_name, index), rows
        )

    upstream, map_second, span_second = layer_backward(
        upstream, kept_second, live_fill, weights[1], span, None, grad_maker(1)
    )
    grad_mask_emb = jnp.sum(jnp.where(visible[:, None], 0.0, upstream), axis=0)
    grad_encoded = lax.dot_general(
        pick_full, upstream, (((1,), (0,)), ((), ())), precision=HIGHEST
    )
    grad_seen, map_first, span_first = layer_backward(
        grad_encoded, kept_first, seen_fill, weights[0], span, pick_seen, grad_maker(0)
    )
    grad_seen = grad_seen * seen_valid[:, None].astype(F32)
    grad_conv_seen = grad_seen * gelu_grad(seen_pre)
    grad_conv = dot_tn(pick_low, grad_conv_seen.astype(BF)).astype(BF)
    grad_full = lax.dot_general(
        pick_full, grad_seen, (((0,), (0,)), ((), ())), precision=HIGHEST
    )
    own_grad = lax.dynamic_slice_in_dim(grad_conv, own_cols, width, 1)
    grad_in_own = conv_call(conv_input_kernel, own_grad[:LONG], conv_weight, half - 1, True)
    grad_conv_in = side_by_side(grad_in_own.astype(BF), code_index)
    split = front_slots(geometry)
    padded, grads = conv_weight_inputs(conv_in[:LONG], grad_conv)
    rest_grad = conv_weight_grad(
        padded, grads, geometry, code_index, range(split, dp_count), CHUNK // 2
    )
    grad_start = (grad_full + grad_conv_in.astype(F32)) * live_float
    grad_embedded, grad_gain_zero, grad_shift_zero = norm_backward(
        grad_start, normed_zero, inv_zero, glob_vec[0 : 1]
    )
    grad_patch = dot_tn(patch_rows, grad_embedded.astype(BF))
    grad_glob = jnp.stack(
        [grad_gain_zero, grad_shift_zero, jnp.sum(grad_conv_seen, axis=0), grad_mask_emb]
    )
    grad_rel = lax.dot_general(
        jnp.asarray(span_table),
        (span_first + span_second)[:HEADS],
        (((0,), (1,)), ((), ())),
        precision=HIGHEST,
    )
    leader = (code_index == 0).astype(F32)
    count_local = jnp.sum((target_codes >= 0).astype(F32))
    early = jnp.concatenate(
        [
            (grad_rel * leader).reshape(-1, 128),
            jnp.full((1, 128), loss_local * leader),
            jnp.full((1, 128), count_local * leader),
        ]
    )
    early = sum_over(sum_over(jnp.pad(early, ((0, -early.shape[0] % 8), (0, 0))), "dp"), "code")
    both = (map_first, map_second)
    sources, spans = [], [[] for _ in range(code_count)]

    def add_source(found):
        array, (chunks, base, unit, chunk) = found
        for code, items in enumerate(chunk_spans(chunks, base, unit, chunk, len(sources))):
            spans[code] += items
        sources.append(array)

    pairs = [
        layer_map[seg_name]
        for layer_map in both[::-1]
        for seg_name in ("w_down", "w_up", "w_out", "w_qkv")
    ]
    for found in weight_grads(pairs, geometry, code_index):
        add_source(found)
    add_source(rest_grad)
    tail_place = geometry.place("layer_vec")
    vectors = [vector for layer_map in both for vector in layer_map["layer_vec"]]
    small = [layer_map[seg_name] for seg_name in ("gate_proj", "gate_scale") for layer_map in both]
    small = jnp.concatenate([part.reshape(-1) for part in small + [grad_rel]])
    tail_rows = geometry.begins[-1] + geometry.window - tail_place
    tail = tail_grad(vectors, small, grad_head, tail_rows)
    for items in spans:
        items.append((tail_place, tail_rows, len(sources), 0))
    sources.append(tail)
    front = jnp.concatenate([grad_patch.reshape(-1, 128), grad_glob.reshape(-1, 128)], axis=0)
    front = jnp.pad(front, ((geometry.phase, 0), (0, 0))).astype(BF)
    if split:
        own_part = pack(geometry, code_index, sources, spans, split, dp_count)
        reduced = lax.psum_scatter(own_part, "dp", scatter_dimension=0, tiled=False)
        sources, spans = [], [[] for _ in range(code_count)]
        add_source(conv_weight_grad(padded, grads, geometry, code_index, range(split)))
    front, early = lax.optimization_barrier((front, early))
    for items in spans:
        items.append((0, front.shape[0], len(sources), 0))
    sources.append(front)
    turn = dp_index % split if split else 0
    last_part = pack(geometry, code_index, sources, spans, 0, split or dp_count, turn)
    if split:
        first = reduce_front(last_part, dp_count)
        reduced = jnp.where(dp_index < split, first, reduced)
    else:
        reduced = lax.psum_scatter(last_part, "dp", scatter_dimension=0, tiled=False)
    reduced = reduced.reshape(geometry.window, 128).astype(F32)
    reduced = lax.dynamic_slice(reduced, (own_offset, 0), (shard_rows, 128)).reshape(shard_len)
    squares_all = sum_over_all(jnp.full((8, 128), jnp.sum(reduced * reduced)))
    squares_all = squares_all[0, 0]
    rel_rows = BUCKETS * HEADS // 128
    rel_all = early[:rel_rows].reshape(BUCKETS, HEADS)
    loss_all, count_all = early[rel_rows, 0], early[rel_rows + 1, 0]
    grad_norm = jnp.sqrt(squares_all) / count_all
    clip_factor = jnp.minimum(1.0, CLIP_NORM / grad_norm)
    clipped = reduced / count_all * clip_factor
    rel_grad = rel_all / count_all * clip_factor
    step_value = step_count[0].astype(F32)
    new_first = BETA_ONE * first_moment + (1.0 - BETA_ONE) * clipped
    new_second = BETA_TWO * second_moment + (1.0 - BETA_TWO) * clipped * clipped
    first_hat = new_first / (1.0 - BETA_ONE**step_value)
    second_hat = new_second / (1.0 - BETA_TWO**step_value)
    new_params = params - LEARN_RATE * (
        first_hat / (jnp.sqrt(second_hat) + ADAM_EPSILON) + WEIGHT_DECAY * params
    )
    return (
        new_params,
        new_first,
        new_second,
        new_params.astype(BF),
        loss_all / count_all,
        grad_norm,
        rel_grad,
    )


def solution(mesh):
    placed = (
        P("dp", None, None),
        P("dp"),
        P("dp", None),
        P("dp", None),
        P("code", None),
        P(("dp", "code")),
        P(("dp", "code")),
        P(("dp", "code")),
        P(),
    )
    return jax.shard_map(
        local,
        mesh=mesh,
        in_specs=placed,
        out_specs=(
            P(("dp", "code")),
            P(("dp", "code")),
            P(("dp", "code")),
            P(("dp", "code")),
            P(),
            P(),
            P(),
        ),
        check_vma=False,
    )
```

```python
import functools
import math

import jax
import jax.numpy as jnp
import numpy as np
from jax import lax
from jax.experimental import pallas as pl
from jax.experimental.pallas import tpu as pltpu
from jax.sharding import PartitionSpec as P

D = 768
HEADS = 12
HEAD_DIM = 64
FF = 3072
PATCH_IN = 256
PROJ = 256
KERNEL = 128
GROUPS = 16
WIDTH = D // GROUPS
BUCKETS = 320
MAX_DIST = 800
LAYERS = 2
LONG = 496
VISIBLE = 124
ROWS = 512
SEEN = 128
SPAN = 1024

NORM_EPSILON = 1e-05
UNIT_EPSILON = 1e-06
DEEP_ALPHA = 2.2133638394006434
LOGIT_SCALE = 25.0
CLIP_NORM = 0.005
LEARN_RATE = 0.02
BETA_ONE = 0.9
BETA_TWO = 0.999
ADAM_EPSILON = 1e-10
WEIGHT_DECAY = 0.01
MASK_FILL = -1000000000.0
HIGHEST = lax.Precision.HIGHEST
BF = jnp.bfloat16
F32 = jnp.float32
VMEM_LIMIT = 56 << 20


def layout():
    return [
        ("w_patch", (PATCH_IN, D)),
        ("glob_vec", (4, D)),
        ("conv_w", (KERNEL, WIDTH, D)),
        ("w_qkv", (LAYERS, D, 3 * D)),
        ("w_out", (LAYERS, D, D)),
        ("w_up", (LAYERS, D, FF)),
        ("w_down", (LAYERS, FF, D)),
        ("layer_vec", (LAYERS, 8 * D + FF)),
        ("gate_proj", (LAYERS, HEAD_DIM + 1, 8)),
        ("gate_scale", (LAYERS, HEADS)),
        ("rel_table", (BUCKETS, HEADS)),
        ("w_head", (D, PROJ)),
    ]


def starts():
    where = {}
    offset = 0
    for seg_name, extent in layout():
        where[seg_name] = offset
        offset += math.prod(extent)
    return where


TILE = 16


class Geometry:
    def __init__(self, dp_count, code_count, shard_rows):
        self.dp_count, self.code_count, self.shard_rows = dp_count, code_count, shard_rows
        self.shards = dp_count * code_count
        self.phase = -(starts()["conv_w"] // 128) % TILE
        self.window = -(-(shard_rows + TILE - 1) // TILE) * TILE
        self.begins = [(shard_rows * s + self.phase) // TILE * TILE for s in range(self.shards)]
        self.offsets = [(shard_rows * s + self.phase) % TILE for s in range(self.shards)]

    def place(self, seg_name, index=0):
        extent = dict(layout())[seg_name]
        amount = math.prod(extent[1:]) if index else 0
        return (starts()[seg_name] + index * amount) // 128 + self.phase

    def pieces(self, low, high):
        main, edges = [], []
        row = low
        while row < high:
            shard = max(s for s in range(self.shards) if self.begins[s] <= row)
            begin = self.begins[shard]
            if row == begin and shard > 0 and self.offsets[shard]:
                main.append((shard - 1, row - self.begins[shard - 1], row - low, TILE))
                edges.append((shard, row - low))
                row += TILE
                continue
            stop = self.begins[shard + 1] if shard + 1 < self.shards else high
            count = min(stop, high) - row
            main.append((shard, row - begin, row - low, count))
            row += count
        merged = []
        for item in main:
            last = merged[-1] if merged else None
            if last and last[0] == item[0] and last[1] + last[3] == item[1]:
                merged[-1] = last[:3] + (last[3] + item[3],)
            else:
                merged.append(item)
        return merged, edges


def bucket_onehot():
    offsets = np.arange(-(LONG - 1), LONG)
    half_count = BUCKETS // 2
    exact_count = half_count // 2
    distance = np.abs(offsets)
    scaled = (
        np.log(np.maximum(distance, 1) / exact_count)
        / np.log(MAX_DIST / exact_count)
        * (half_count - exact_count)
    )
    larger = np.minimum(exact_count + np.maximum(scaled, 0.0).astype(np.int64), half_count - 1)
    bucket = (offsets > 0) * half_count + np.where(distance < exact_count, distance, larger)
    return (bucket[:, None] == np.arange(BUCKETS)[None, :]).astype(np.float32)


def span_onehot():
    shift = SPAN // 2 - (LONG - 1)
    table = np.zeros((SPAN, BUCKETS), np.float32)
    table[shift : shift + 2 * LONG - 1] = bucket_onehot()[::-1]
    return table


def params_of(grid_rank=1):
    return pltpu.CompilerParams(
        dimension_semantics=("arbitrary",) * grid_rank, vmem_limit_bytes=VMEM_LIMIT
    )


def dot_nn(left, right):
    return lax.dot_general(left, right, (((1,), (0,)), ((), ())), preferred_element_type=F32)


def dot_nt(left, right):
    return lax.dot_general(left, right, (((1,), (1,)), ((), ())), preferred_element_type=F32)


def dot_tn(left, right):
    return lax.dot_general(left, right, (((0,), (0,)), ((), ())), preferred_element_type=F32)


TAPS = 16


def lane_masks(width):
    group = np.arange(width)[None, :] // WIDTH
    return (group == np.arange(width // WIDTH)[:, None]).astype(np.float32)


def shifted_taps(source_ref, target_ref, count):
    width = source_ref.shape[1]
    for tap in range(TAPS):
        target_ref[:, tap * width : (tap + 1) * width] = source_ref[tap : tap + count, :].astype(BF)


def conv_forward_kernel(in_ref, weight_ref, mask_ref, out_ref, taps_ref, block_ref):
    step = pl.program_id(0)
    width = weight_ref.shape[1]

    @pl.when(step == 0)
    def _():
        shifted_taps(in_ref, taps_ref, taps_ref.shape[0])
        block_ref[...] = jnp.zeros_like(block_ref)

    for tap in range(TAPS):
        piece = weight_ref[tap * WIDTH : (tap + 1) * WIDTH, :]
        for group in range(width // WIDTH):
            low = tap * width + group * WIDTH
            block_ref[low : low + WIDTH, :] = piece * mask_ref[group : group + 1, :]
    begin = pl.multiple_of(step * TAPS, TAPS)
    term = dot_nn(taps_ref[pl.ds(begin, ROWS), :], block_ref[...])

    @pl.when(step == 0)
    def _():
        out_ref[...] = term

    @pl.when(step > 0)
    def _():
        out_ref[...] += term


def conv_input_kernel(in_ref, weight_ref, mask_ref, out_ref, taps_ref, block_ref):
    step = pl.program_id(0)
    width = weight_ref.shape[1]

    @pl.when(step == 0)
    def _():
        shifted_taps(in_ref, taps_ref, taps_ref.shape[0])
        block_ref[...] = jnp.zeros_like(block_ref)

    for tap in range(TAPS):
        piece = weight_ref[tap * WIDTH : (tap + 1) * WIDTH, :]
        low = (TAPS - 1 - tap) * width
        for group in range(width // WIDTH):
            block_ref[group * WIDTH : (group + 1) * WIDTH, low : low + width] = (
                piece * mask_ref[group : group + 1, :]
            )
    begin = pl.multiple_of((pl.num_programs(0) - 1 - step) * TAPS, TAPS)
    term = dot_nt(taps_ref[pl.ds(begin, ROWS), :], block_ref[...])

    @pl.when(step == 0)
    def _():
        out_ref[...] = term

    @pl.when(step > 0)
    def _():
        out_ref[...] += term


def conv_call(kernel, conv_in, weight, front, nt):
    width = weight.shape[1]
    steps = KERNEL // TAPS
    count = ROWS + KERNEL - TAPS
    padded = jnp.pad(
        conv_in.astype(F32),
        ((front, count + TAPS - front - conv_in.shape[0]), (0, 0)),
    )
    block = (width, TAPS * width) if nt else (TAPS * width, width)
    return pl.pallas_call(
        kernel,
        grid=(steps,),
        in_specs=[
            pl.BlockSpec(padded.shape, lambda i: (0, 0)),
            pl.BlockSpec((TAPS * WIDTH, width), lambda i: (i, 0)),
            pl.BlockSpec((width // WIDTH, width), lambda i: (0, 0)),
        ],
        out_specs=pl.BlockSpec((ROWS, width), lambda i: (0, 0)),
        out_shape=jax.ShapeDtypeStruct((ROWS, width), F32),
        scratch_shapes=[pltpu.VMEM((count, TAPS * width), BF), pltpu.VMEM(block, BF)],
        compiler_params=params_of(),
    )(padded, weight, jnp.asarray(lane_masks(width), BF))


CHUNK = 6


def conv_weight_kernel(tap_ref, in_ref, grad_ref, mask_ref, out_ref, taps_ref, turn_ref, *, chunk):
    parts = in_ref.shape[0]
    begin = tap_ref[pl.program_id(0)]
    strips = D // 128
    rows = chunk * WIDTH
    for part in range(parts):
        turned = pltpu.roll(in_ref[part], in_ref.shape[2] - begin, 1)
        for tap in range(chunk):
            taps_ref[part, tap * PART : (tap + 1) * PART, :] = turned[:, tap : tap + ROWS].astype(
                BF
            )
    sums = []
    for part in range(parts):
        term = dot_nn(taps_ref[part], grad_ref[part])
        pieces = []
        for tap in range(chunk):
            total = None
            for group in range(mask_ref.shape[0]):
                low = tap * PART + group * WIDTH
                piece = term[low : low + WIDTH, :] * mask_ref[group : group + 1, :]
                total = piece if total is None else total + piece
            pieces.append(total)
        sums.append(jnp.concatenate(pieces, axis=0))
    for strip in range(strips):
        part, low = divmod(strip * 128, PART)
        columns = sums[part][:, low : min(low + 128, PART)]
        if low + 128 > PART:
            columns = jnp.concatenate([columns, sums[part + 1][:, : low + 128 - PART]], axis=1)
        turn_ref[pl.ds(strip, rows, stride=strips), :] = columns
    out_ref[...] = turn_ref[...].astype(BF)


PART = 4 * WIDTH


def owned_chunks(geometry, base, unit, count, chunk, step, slots):
    tables = []
    for code in range(geometry.code_count):
        found = []
        for slot in slots:
            begin = geometry.begins[slot * geometry.code_count + code] - base
            low = max(begin // unit, 0) // step * step
            high = min(-(-(begin + geometry.window) // unit), count)
            while low < high:
                found.append(min(low, count - chunk))
                low += chunk
        tables.append(list(dict.fromkeys(found)))
    most = max([1] + [len(table) for table in tables])
    return [(table or [0]) + (table or [0])[-1:] * (most - max(len(table), 1)) for table in tables]


def chunk_spans(chunks, base, unit, chunk, source):
    return [
        [(base + low * unit, chunk * unit, source, n * chunk * unit) for n, low in enumerate(table)]
        for table in chunks
    ]


def chunk_table(chunks, code_index):
    return lax.dynamic_index_in_dim(jnp.asarray(chunks, jnp.int32), code_index, 0, False)


def conv_weight_inputs(conv_in, grad_low):
    parts = D // PART
    front = KERNEL // 2
    padded = jnp.pad(
        jnp.transpose(conv_in).astype(F32),
        ((0, 0), (front, ROWS + KERNEL - front - conv_in.shape[0])),
    ).reshape(parts, PART, ROWS + KERNEL)
    return padded, jnp.transpose(grad_low.reshape(ROWS, parts, PART), (1, 0, 2))


def conv_weight_grad(padded, grads, geometry, code_index, slots, chunk=CHUNK):
    parts = D // PART
    masks = jnp.asarray(lane_masks(PART), F32)
    base, unit = geometry.place("conv_w"), WIDTH * D // 128
    chunks = owned_chunks(geometry, base, unit, KERNEL, chunk, 1, slots)
    table = chunk_table(chunks, code_index)
    rows = chunk * unit
    out = pl.pallas_call(
        functools.partial(conv_weight_kernel, chunk=chunk),
        grid_spec=pltpu.PrefetchScalarGridSpec(
            num_scalar_prefetch=1,
            grid=(len(chunks[0]),),
            in_specs=[
                pl.BlockSpec(padded.shape, lambda i, t: (0, 0, 0)),
                pl.BlockSpec(grads.shape, lambda i, t: (0, 0, 0)),
                pl.BlockSpec(masks.shape, lambda i, t: (0, 0)),
            ],
            out_specs=pl.BlockSpec((rows, 128), lambda i, t: (i, 0)),
            scratch_shapes=[
                pltpu.VMEM((parts, chunk * PART, ROWS), BF),
                pltpu.VMEM((rows, 128), F32),
            ],
        ),
        out_shape=jax.ShapeDtypeStruct((len(chunks[0]) * rows, 128), BF),
        compiler_params=params_of(),
    )(table, padded, grads, masks)
    return out, (chunks, base, unit, chunk)


BLOCK = 128


def half_mask(side):
    lane = lax.broadcasted_iota(jnp.int32, (1, BLOCK), 1)
    return jnp.where(lane // HEAD_DIM == side, 1.0, 0.0).astype(BF)


def toeplitz(span_ref, head):
    row = jnp.broadcast_to(span_ref[pl.ds(head, 1), :], (BLOCK, SPAN))
    return pltpu.roll(row, 0, 1, stride=1, stride_axis=0)


def hop_columns(hop):
    return [hop[:, index : index + 1] for index in range(ROWS // BLOCK)]


def seen_biases(turned, pick, near, hop):
    moved = [dot_nn(near, item.astype(BF)) for item in turned]
    columns = [jnp.broadcast_to(column, (SEEN, ROWS)) for column in hop_columns(hop)]
    tables = []
    for item in moved:
        table = None
        for index, column in enumerate(columns):
            low = index * BLOCK
            part = column * item[:, ROWS - low : SPAN - low]
            table = part if table is None else table + part
        tables.append(table.astype(BF))
    return [dot_nt(table, pick) for table in tables]


def wide(column, length):
    return jnp.concatenate([column] * (length // BLOCK), axis=1)


def attention_forward_kernel(
    q_ref, k_ref, v_ref, gate_ref, span_ref, fill_ref, out_ref, lse_ref, score_ref, turn_ref
):
    step = pl.program_id(0)
    length = q_ref.shape[0]
    values = jnp.transpose(v_ref[...])
    sides = range(2)
    turned = [toeplitz(span_ref, step * 2 + side) for side in sides]
    for side in sides:
        score_ref[side] = dot_nt(k_ref[...] * half_mask(side), q_ref[...])
    tops = []
    for side in sides:
        gate = gate_ref[pl.ds(step * 2 + side, 1), :]
        top = None
        for low in range(0, length, BLOCK):
            rows = slice(low, low + BLOCK)
            bias = turned[side][:, ROWS - low : SPAN - low]
            scores = score_ref[side, rows, :] + gate * bias + wide(fill_ref[rows, :], length)
            score_ref[side, rows, :] = scores
            most = jnp.max(scores, axis=0, keepdims=True)
            top = most if top is None else jnp.maximum(top, most)
        tops.append(top)
    totals = []
    for side in sides:
        total = None
        for low in range(0, length, BLOCK):
            rows = slice(low, low + BLOCK)
            weights = jnp.exp(score_ref[side, rows, :] - tops[side])
            part = jnp.sum(weights, axis=0, keepdims=True)
            total = part if total is None else total + part
            turn_ref[side, rows, :] = weights.astype(BF)
        totals.append(total)
    mixed = []
    for side in sides:
        lse_ref[pl.ds(step * 2 + side, 1), :] = tops[side] + jnp.log(totals[side])
        part = dot_nn(values[side * HEAD_DIM : (side + 1) * HEAD_DIM, :], turn_ref[side])
        mixed.append(part * (1.0 / totals[side]))
    out_ref[...] = jnp.transpose(jnp.concatenate(mixed, axis=0)).astype(BF)


SEEN_HEADS = 12


def seen_forward_kernel(
    q_ref, k_ref, v_ref, gate_ref, span_ref, fill_ref, pick_ref, near_ref, hop_ref,
    out_ref, lse_ref, bias_ref,
):
    heads = range(SEEN_HEADS)
    base = pl.program_id(0) * SEEN_HEADS
    pick, near, hop = pick_ref[...], near_ref[...], hop_ref[...]
    pairs = range(SEEN_HEADS // 2)
    query = [q_ref[:, pair * BLOCK : (pair + 1) * BLOCK] for pair in pairs]
    keyv = [k_ref[:, pair * BLOCK : (pair + 1) * BLOCK] for pair in pairs]
    values = [jnp.transpose(v_ref[:, pair * BLOCK : (pair + 1) * BLOCK]) for pair in pairs]
    turned = [toeplitz(span_ref, base + head) for head in heads]
    bias = seen_biases(turned, pick, near, hop)
    scores = [dot_nt(keyv[head // 2] * half_mask(head % 2), query[head // 2]) for head in heads]
    for head in heads:
        bias_ref[head * BLOCK : (head + 1) * BLOCK, :] = bias[head].astype(BF)
    scores = [
        scores[head] + gate_ref[pl.ds(base + head, 1), :] * bias[head] + fill_ref[...]
        for head in heads
    ]
    tops = [jnp.max(item, axis=0, keepdims=True) for item in scores]
    weights = [jnp.exp(scores[head] - tops[head]) for head in heads]
    totals = [jnp.sum(item, axis=0, keepdims=True) for item in weights]
    mixed = []
    for head in heads:
        lse_ref[pl.ds(base + head, 1), :] = tops[head] + jnp.log(totals[head])
        low = (head % 2) * HEAD_DIM
        part = dot_nn(values[head // 2][low : low + HEAD_DIM, :], weights[head].astype(BF))
        mixed.append(part * (1.0 / totals[head]))
    for pair in pairs:
        both = jnp.concatenate(mixed[2 * pair : 2 * pair + 2], axis=0)
        out_ref[:, pair * BLOCK : (pair + 1) * BLOCK] = jnp.transpose(both).astype(BF)


def head_specs(length, heads):
    count = HEADS // heads
    return [
        pl.BlockSpec((length, heads * HEAD_DIM), lambda i, part=part: (0, part * count + i))
        for part in range(3)
    ]


def whole_spec(shape):
    return pl.BlockSpec(shape, lambda i: (0,) * len(shape))


def attention_forward(qkv, gate, span, fill, pick):
    length = qkv.shape[0]
    heads = 2 if pick is None else SEEN_HEADS
    specs = head_specs(length, heads)
    args = [qkv, qkv, qkv, gate, span, fill] + list(pick[:3] if pick else ())
    shapes = [
        jax.ShapeDtypeStruct((length, D), BF),
        jax.ShapeDtypeStruct((16, length), F32),
    ]
    out_specs = [specs[0], whole_spec((16, length))]
    scratch = []
    if pick is None:
        kernel = attention_forward_kernel
        scratch = [pltpu.VMEM((2, length, length), F32), pltpu.VMEM((2, length, length), BF)]
    else:
        kernel = seen_forward_kernel
        out_specs.append(pl.BlockSpec((SEEN_HEADS * BLOCK, BLOCK), lambda i: (i, 0)))
        shapes.append(jax.ShapeDtypeStruct((HEADS * BLOCK, BLOCK), BF))
    found = pl.pallas_call(
        kernel,
        grid=(HEADS // heads,),
        in_specs=specs + [whole_spec(a.shape) for a in args[3:]],
        out_specs=out_specs,
        out_shape=shapes,
        scratch_shapes=scratch,
        compiler_params=params_of(),
    )(*args)
    return found[0], found[1], None if pick is None else found[2]


def diagonal_sums(turn):
    half = BLOCK // 2
    while half:
        turn = turn[:half, :] + pltpu.roll(turn[half:, :], SPAN - half, 1)
        half //= 2
    return turn


def attention_backward_kernel(
    q_ref, k_ref, v_ref, up_ref, gate_ref, span_ref, fill_ref, lse_ref,
    out_ref, sum_ref, dgate_ref, dspan_ref, prob_ref, grad_ref, turn_ref, low_ref, diag_ref,
):
    step = pl.program_id(0)
    length = q_ref.shape[0]
    sides = range(2)

    @pl.when(step == 0)
    def _():
        dspan_ref[...] = jnp.zeros_like(dspan_ref)
        dgate_ref[...] = jnp.zeros_like(dgate_ref)

    keys = jnp.transpose(k_ref[...])
    turned = [toeplitz(span_ref, step * 2 + side) for side in sides]
    for side in sides:
        prob_ref[side] = dot_nt(k_ref[...] * half_mask(side), q_ref[...])
        grad_ref[side] = dot_nt(v_ref[...] * half_mask(side), up_ref[...])
        diag_ref[side] = jnp.zeros_like(diag_ref[side])
    shared = []
    for side in sides:
        gate = gate_ref[pl.ds(step * 2 + side, 1), :]
        lse = lse_ref[pl.ds(step * 2 + side, 1), :]
        total = None
        for low in range(0, length, BLOCK):
            rows = slice(low, low + BLOCK)
            bias = turned[side][:, ROWS - low : SPAN - low]
            scores = prob_ref[side, rows, :] + gate * bias + wide(fill_ref[rows, :], length)
            probs = jnp.exp(scores - lse)
            prob_ref[side, rows, :] = probs
            low_ref[side, rows, :] = probs.astype(BF)
            part = jnp.sum(probs * grad_ref[side, rows, :], axis=0, keepdims=True)
            total = part if total is None else total + part
        shared.append(total)
    val_total = sum(dot_nn(low_ref[side], up_ref[...] * half_mask(side)) for side in sides)
    for side in sides:
        gate = gate_ref[pl.ds(step * 2 + side, 1), :]
        dgate = None
        for low in range(0, length, BLOCK):
            rows = slice(low, low + BLOCK)
            bias = turned[side][:, ROWS - low : SPAN - low]
            grad_scores = prob_ref[side, rows, :] * (grad_ref[side, rows, :] - shared[side])
            turn_ref[side, rows, :] = grad_scores.astype(BF)
            part = jnp.sum(grad_scores * bias, axis=0, keepdims=True)
            dgate = part if dgate is None else dgate + part
            diag_ref[side, :, ROWS - low : SPAN - low] += grad_scores * gate
        dgate_ref[pl.ds(step * 2 + side, 1), :] = dgate
    key_total = sum(dot_nn(turn_ref[side], q_ref[...] * half_mask(side)) for side in sides)
    halves = [
        dot_nn(keys[side * HEAD_DIM : (side + 1) * HEAD_DIM, :], turn_ref[side]) for side in sides
    ]
    for side in sides:
        dspan_ref[pl.ds(step * 2 + side, 1), :] = diagonal_sums(diag_ref[side])
    grad_query = jnp.transpose(jnp.concatenate(halves, axis=0)) * HEAD_DIM ** (-0.5)
    for part, value in enumerate((grad_query, key_total, val_total)):
        begin = pl.multiple_of(part * D + step * BLOCK, BLOCK)
        out_ref[:, pl.ds(begin, BLOCK)] = value.astype(BF)
    sum_ref[0:1, :] = jnp.sum(grad_query, axis=0, keepdims=True)
    sum_ref[1:2, :] = jnp.sum(val_total, axis=0, keepdims=True)


def split_low(value):
    high = value.astype(BF)
    return high, (value - high.astype(F32)).astype(BF)


def seen_backward_kernel(
    q_ref, k_ref, v_ref, up_ref, gate_ref, fill_ref, lse_ref, pick_ref, hop_ref, flip_ref,
    bias_ref, out_ref, sum_ref, dgate_ref, dspan_ref, diag_ref,
):
    heads, pairs = range(SEEN_HEADS), range(SEEN_HEADS // 2)
    base = pl.program_id(0) * SEEN_HEADS

    @pl.when(base == 0)
    def _():
        dspan_ref[...] = jnp.zeros_like(dspan_ref)
        dgate_ref[...] = jnp.zeros_like(dgate_ref)

    def pair_of(ref):
        return [ref[:, pair * BLOCK : (pair + 1) * BLOCK] for pair in pairs]

    query, keyv, value, upstream = (pair_of(ref) for ref in (q_ref, k_ref, v_ref, up_ref))
    keys = [jnp.transpose(item) for item in keyv]
    gate = [gate_ref[pl.ds(base + head, 1), :] for head in heads]
    bias = [bias_ref[head * BLOCK : (head + 1) * BLOCK, :].astype(F32) for head in heads]
    scores = [dot_nt(keyv[head // 2] * half_mask(head % 2), query[head // 2]) for head in heads]
    grads = [dot_nt(value[head // 2] * half_mask(head % 2), upstream[head // 2]) for head in heads]
    probs = [
        jnp.exp(
            scores[head]
            + gate[head] * bias[head]
            + fill_ref[...]
            - lse_ref[pl.ds(base + head, 1), :]
        )
        for head in heads
    ]
    shared = [jnp.sum(probs[head] * grads[head], axis=0, keepdims=True) for head in heads]
    moves = [probs[head] * (grads[head] - shared[head]) for head in heads]
    val_terms = [
        dot_nn(probs[head].astype(BF), upstream[head // 2] * half_mask(head % 2)) for head in heads
    ]
    low = [item.astype(BF) for item in moves]
    key_terms = [dot_nn(low[head], query[head // 2] * half_mask(head % 2)) for head in heads]
    halves = [
        dot_nn(keys[head // 2][(head % 2) * HEAD_DIM : (head % 2 + 1) * HEAD_DIM, :], low[head])
        for head in heads
    ]
    for head in heads:
        dgate_ref[pl.ds(base + head, 1), :] = jnp.sum(
            moves[head] * bias[head], axis=0, keepdims=True
        )
    pieces = [jnp.concatenate(split_low(moves[head] * gate[head]), axis=0) for head in heads]
    placed = [dot_nn(piece, pick_ref[...]) for piece in pieces]
    columns = [jnp.broadcast_to(column, (SEEN, ROWS)) for column in hop_columns(hop_ref[...])]
    for head in heads:
        both = placed[head][:BLOCK, :] + placed[head][BLOCK:, :]
        diag_ref[head] = jnp.zeros_like(diag_ref[head])
        for index, column in enumerate(columns):
            begin = ROWS - index * BLOCK
            diag_ref[head, :, begin : begin + ROWS] += column * both
    turns = [
        dot_nn(flip_ref[...], jnp.concatenate(split_low(diag_ref[head]), axis=0)) for head in heads
    ]
    for head in heads:
        dspan_ref[pl.ds(base + head, 1), :] = diagonal_sums(turns[head])
    for pair in pairs:
        cols = slice(pair * BLOCK, (pair + 1) * BLOCK)
        grad_query = jnp.transpose(jnp.concatenate(halves[2 * pair : 2 * pair + 2], axis=0))
        grad_query = grad_query * HEAD_DIM ** (-0.5)
        val_total = val_terms[2 * pair] + val_terms[2 * pair + 1]
        key_total = key_terms[2 * pair] + key_terms[2 * pair + 1]
        for part, value in enumerate((grad_query, key_total, val_total)):
            begin = pl.multiple_of(part * D + base * HEAD_DIM + pair * BLOCK, BLOCK)
            out_ref[:, pl.ds(begin, BLOCK)] = value.astype(BF)
        sum_ref[0:1, cols] = jnp.sum(grad_query, axis=0, keepdims=True)
        sum_ref[1:2, cols] = jnp.sum(val_total, axis=0, keepdims=True)


def attention_backward(qkv, upstream, gate, span, fill, lse, pick, bias):
    length = qkv.shape[0]
    heads = 2 if pick is None else SEEN_HEADS
    specs = head_specs(length, heads)
    shapes = [
        jax.ShapeDtypeStruct((length, 3 * D), BF),
        jax.ShapeDtypeStruct((8, D), F32),
        jax.ShapeDtypeStruct((16, length), F32),
        jax.ShapeDtypeStruct((16, SPAN), F32),
    ]
    out_specs = [
        whole_spec((length, 3 * D)),
        pl.BlockSpec((8, heads * HEAD_DIM), lambda i: (0, i)),
        whole_spec((16, length)),
        whole_spec((16, SPAN)),
    ]
    if pick is None:
        args = [qkv, qkv, qkv, upstream, gate, span, fill, lse]
        kernel, more = attention_backward_kernel, []
        scratch = [
            pltpu.VMEM((2, length, length), F32),
            pltpu.VMEM((2, length, length), F32),
            pltpu.VMEM((2, length, length), BF),
            pltpu.VMEM((2, length, length), BF),
            pltpu.VMEM((2, BLOCK, SPAN), F32),
        ]
    else:
        args = [qkv, qkv, qkv, upstream, gate, fill, lse, pick[0], pick[2], pick[3], bias]
        kernel = seen_backward_kernel
        more = [pl.BlockSpec((heads * BLOCK, BLOCK), lambda i: (i, 0))]
        scratch = [pltpu.VMEM((heads, BLOCK, SPAN), F32)]
    return pl.pallas_call(
        kernel,
        grid=(HEADS // heads,),
        in_specs=specs
        + [specs[0]]
        + [whole_spec(a.shape) for a in args[4 : len(args) - len(more)]]
        + more,
        out_specs=out_specs,
        out_shape=shapes,
        scratch_shapes=scratch,
        compiler_params=params_of(),
    )(*args)


STAGES = 4


def weight_grads_kernel(table_ref, *refs, plan):
    count = len(plan)
    lefts, rights, outs = refs[:count], refs[count : 2 * count], refs[2 * count : 3 * count]
    left_bufs, right_bufs = refs[3 * count : 4 * count], refs[4 * count : 5 * count]
    turn_ref, stage_ref, in_sems, out_sems = refs[5 * count :]
    loads = []
    for number in range(count):
        loads.append(
            [
                pltpu.make_async_copy(source, target, in_sems.at[side, number])
                for side, (source, target) in enumerate(
                    ((lefts[number], left_bufs[number]), (rights[number], right_bufs[number]))
                )
            ]
        )
    for pair in loads:
        for copy in pair:
            copy.start()

    def out_copy(number, index, slot):
        _, _, rows, strips = plan[number]
        size = rows * strips
        return pltpu.make_async_copy(
            stage_ref.at[slot, pl.ds(0, size)],
            outs[number].at[pl.ds(pl.multiple_of(index * size, TILE), size)],
            out_sems.at[slot],
        )

    pending = [None] * STAGES
    for number, (offset, steps, rows, strips) in enumerate(plan):
        for copy in loads[number]:
            copy.wait()
        base = number % 2 * 2
        for slot in (base, base + 1):
            if pending[slot] is not None:
                pending[slot].wait()
                pending[slot] = None
        size = rows * strips

        def body(index, carry, number=number, offset=offset, rows=rows, strips=strips, base=base):
            size = rows * strips
            slot = base + index % 2
            begin = pl.multiple_of(table_ref[offset + index], 128)
            grad = dot_tn(left_bufs[number][:, pl.ds(begin, rows)], right_bufs[number][...])
            for strip in range(strips):
                turn_ref[pl.ds(strip, rows, stride=strips), :] = grad[
                    :, strip * 128 : (strip + 1) * 128
                ]

            @pl.when(index >= 2)
            def _():
                out_copy(number, index - 2, slot).wait()

            stage_ref[slot, :size, :] = turn_ref[:size, :].astype(BF)
            out_copy(number, index, slot).start()
            return carry

        lax.fori_loop(0, steps, body, 0)
        for index in range(max(steps - 2, 0), steps):
            pending[base + index % 2] = out_copy(number, index, base + index % 2)
    for copy in pending:
        if copy is not None:
            copy.wait()


def weight_grads(pairs, geometry, code_index):
    slots = range(geometry.dp_count)
    plan, found, tables, shapes = [], [], [[] for _ in range(geometry.code_count)], []
    for left, right, base, rows in pairs:
        strips = right.shape[1] // 128
        chunks = owned_chunks(geometry, base, strips, left.shape[1], rows, rows, slots)
        plan.append((len(tables[0]), len(chunks[0]), rows, strips))
        for table, chunk in zip(tables, chunks):
            table += chunk
        found.append((chunks, base, strips, rows))
        shapes.append(jax.ShapeDtypeStruct((len(chunks[0]) * rows * strips, 128), BF))
    most = max(rows * strips for _, _, rows, strips in plan)
    lefts, rights = [pair[0] for pair in pairs], [pair[1] for pair in pairs]
    anywhere = pl.BlockSpec(memory_space=pl.ANY)
    outs = pl.pallas_call(
        functools.partial(weight_grads_kernel, plan=plan),
        in_specs=[pl.BlockSpec(memory_space=pltpu.SMEM)] + [anywhere] * (2 * len(pairs)),
        out_specs=[anywhere] * len(pairs),
        out_shape=shapes,
        scratch_shapes=[pltpu.VMEM(a.shape, BF) for a in lefts + rights]
        + [
            pltpu.VMEM((most, 128), F32),
            pltpu.VMEM((STAGES, most, 128), BF),
            pltpu.SemaphoreType.DMA((2, len(pairs))),
            pltpu.SemaphoreType.DMA((STAGES,)),
        ],
        compiler_params=pltpu.CompilerParams(vmem_limit_bytes=VMEM_LIMIT),
    )(chunk_table(tables, code_index), *lefts, *rights)
    return list(zip(outs, found))


def unpack_jobs(geometry, specs):
    jobs = []
    for target, (base, depth, strips, rows) in enumerate(specs):
        for low in range(0, depth, rows):
            begin = base + low * strips
            jobs.append((target, low, rows, strips) + geometry.pieces(begin, begin + rows * strips))
    return jobs


DEPTH = 4


def stream_jobs(jobs, source_ref, buffer_ref, edge_ref, sems, work):
    def copies(number):
        main, edges = jobs[number][4:6]
        slot = number % DEPTH
        found = []
        for shard, begin, low, count in main:
            found.append(
                (source_ref.at[shard, pl.ds(begin, count)], buffer_ref.at[slot, pl.ds(low, count)])
            )
        for place, (shard, _) in enumerate(edges):
            found.append((source_ref.at[shard, pl.ds(0, TILE)], edge_ref.at[slot, place]))
        return [
            pltpu.make_async_copy(source, target, sems.at[slot, index])
            for index, (source, target) in enumerate(found)
        ]

    for number in range(min(DEPTH - 1, len(jobs))):
        for copy in copies(number):
            copy.start()
    for number, job in enumerate(jobs):
        if number + DEPTH - 1 < len(jobs):
            for copy in copies(number + DEPTH - 1):
                copy.start()
        for copy in copies(number):
            copy.wait()
        slot = number % DEPTH
        for place, (_, low) in enumerate(job[5]):
            buffer_ref[slot, low : low + TILE, :] += edge_ref[slot, place]
        work(number, job, slot)


def unpack_kernel(*refs, jobs, stages):
    source_ref = refs[0]
    targets = refs[1 : 1 + len(stages)]
    buffer_ref, edge_ref, turn_ref, sems, out_sems = refs[1 + len(stages) : 6 + len(stages)]
    stage_refs = refs[6 + len(stages) :]
    pending = {}

    def work(number, job, slot):
        target, low, rows, strips = job[:4]
        stage_ref, key = stage_refs[stages[target]], (stages[target], slot)
        if key in pending:
            pending.pop(key).wait()
        turn_ref[: rows * strips, :] = buffer_ref[slot, : rows * strips, :].astype(F32)
        for strip in range(strips):
            stage_ref[slot, :rows, strip * 128 : (strip + 1) * 128] = turn_ref[
                pl.ds(strip, rows, stride=strips), :
            ].astype(BF)
        copy = pltpu.make_async_copy(
            stage_ref.at[slot, pl.ds(0, rows)],
            targets[target].at[pl.ds(low, rows)],
            out_sems.at[stages[target], slot],
        )
        copy.start()
        pending[key] = copy

    stream_jobs(jobs, source_ref, buffer_ref, edge_ref, sems, work)
    for copy in pending.values():
        copy.wait()


def unpack(geometry, windows, specs):
    jobs = unpack_jobs(geometry, specs)
    kinds = sorted({spec[2] for spec in specs})
    stages = [kinds.index(spec[2]) for spec in specs]
    most = max(job[2] * job[3] for job in jobs)
    copies = max(len(job[4]) + len(job[5]) for job in jobs)
    edges = max([1] + [len(job[5]) for job in jobs])
    return pl.pallas_call(
        functools.partial(unpack_kernel, jobs=jobs, stages=stages),
        in_specs=[pl.BlockSpec(memory_space=pl.ANY)],
        out_specs=[pl.BlockSpec(memory_space=pl.ANY)] * len(specs),
        out_shape=[jax.ShapeDtypeStruct((s[1], s[2] * 128), BF) for s in specs],
        scratch_shapes=[
            pltpu.VMEM((DEPTH, most, 128), BF),
            pltpu.VMEM((DEPTH, edges, TILE, 128), BF),
            pltpu.VMEM((most, 128), F32),
            pltpu.SemaphoreType.DMA((DEPTH, copies)),
            pltpu.SemaphoreType.DMA((len(kinds), DEPTH)),
        ]
        + [
            pltpu.VMEM((DEPTH, max(s[3] for s in specs if s[2] == kind), kind * 128), BF)
            for kind in kinds
        ],
        compiler_params=pltpu.CompilerParams(vmem_limit_bytes=VMEM_LIMIT),
    )(windows)


def unpack_conv_kernel(
    code_ref, source_ref, target_ref, buffer_ref, edge_ref, turn_ref, stage_ref, sems, out_sems, *,
    jobs, width
):
    first = code_ref[0] * width
    strip = first // 128
    strips = D // 128
    lead = first - strip * 128
    pending = {}

    def work(number, job, slot):
        low, rows = job[1], job[2]
        if slot in pending:
            pending.pop(slot).wait()
        turn_ref[...] = buffer_ref[slot].astype(F32)
        one = turn_ref[pl.ds(strip, rows, stride=strips), :]
        two = turn_ref[pl.ds(jnp.minimum(strip + 1, strips - 1), rows, stride=strips), :]
        pair = pltpu.roll(jnp.concatenate([one, two], axis=1), lax.rem(256 - lead, 256), 1)
        stage_ref[slot] = pair[:, :width].astype(BF)
        copy = pltpu.make_async_copy(
            stage_ref.at[slot], target_ref.at[pl.ds(low, rows)], out_sems.at[slot]
        )
        copy.start()
        pending[slot] = copy

    stream_jobs(jobs, source_ref, buffer_ref, edge_ref, sems, work)
    for copy in pending.values():
        copy.wait()


def unpack_conv(geometry, windows, code_index, rows=768):
    width = D // geometry.code_count
    depth = KERNEL * WIDTH
    jobs = unpack_jobs(geometry, [(geometry.place("conv_w"), depth, D // 128, rows)])
    copies = max(len(job[4]) + len(job[5]) for job in jobs)
    edges = max([1] + [len(job[5]) for job in jobs])
    return pl.pallas_call(
        functools.partial(unpack_conv_kernel, jobs=jobs, width=width),
        in_specs=[
            pl.BlockSpec(memory_space=pltpu.SMEM),
            pl.BlockSpec(memory_space=pl.ANY),
        ],
        out_specs=pl.BlockSpec(memory_space=pl.ANY),
        out_shape=jax.ShapeDtypeStruct((depth, width), BF),
        scratch_shapes=[
            pltpu.VMEM((DEPTH, rows * D // 128, 128), BF),
            pltpu.VMEM((DEPTH, edges, TILE, 128), BF),
            pltpu.VMEM((rows * D // 128, 128), F32),
            pltpu.VMEM((DEPTH, rows, width), BF),
            pltpu.SemaphoreType.DMA((DEPTH, copies)),
            pltpu.SemaphoreType.DMA((DEPTH,)),
        ],
        compiler_params=pltpu.CompilerParams(vmem_limit_bytes=VMEM_LIMIT),
    )(jnp.full((1,), code_index, jnp.int32), windows)


def small_kernel(
    source_ref, patch_ref, glob_ref, vec_ref, up_ref, rest_ref, head_ref,
    buffer_ref, edge_ref, turn_ref, head_turn_ref, sems, *, jobs, phase, lead, whole
):
    strips = D // 128

    def columns(target_ref, begin, count, kind):
        for strip in range(strips):
            target_ref[:, strip * 128 : (strip + 1) * 128] = turn_ref[
                pl.ds(begin + strip, count, stride=strips), :
            ].astype(kind)

    def work(number, job, slot):
        turn_ref[: job[2], :] = buffer_ref[slot, : job[2], :].astype(F32)
        if number == 0:
            columns(patch_ref, phase, PATCH_IN, BF)
            columns(glob_ref, phase + PATCH_IN * strips, 4, F32)
            return
        count = vec_ref.shape[0]
        columns(vec_ref, 0, count, F32)
        wide = FF // 128
        for layer in range(LAYERS):
            begin = (layer + 1) * (count // LAYERS) * strips - wide
            for strip in range(wide):
                up_ref[layer : layer + 1, strip * 128 : (strip + 1) * 128] = turn_ref[
                    begin + strip : begin + strip + 1, :
                ]
        begin = count * strips
        rest_ref[...] = turn_ref[begin : begin + rest_ref.shape[0], :]
        begin += whole
        rows = head_turn_ref.shape[0]
        turned = turn_ref[begin : begin + rows, :]
        if lead:
            lane = lax.broadcasted_iota(jnp.int32, (1, 128), 1)
            turned = jnp.where(
                lane < 128 - lead,
                pltpu.roll(turned, 128 - lead, 1),
                pltpu.roll(turn_ref[begin + 1 : begin + 1 + rows, :], 128 - lead, 1),
            )
        head_turn_ref[...] = turned
        for strip in range(PROJ // 128):
            head_ref[:, strip * 128 : (strip + 1) * 128] = head_turn_ref[
                pl.ds(strip, D, stride=PROJ // 128), :
            ].astype(BF)

    stream_jobs(jobs, source_ref, buffer_ref, edge_ref, sems, work)


def unpack_small(geometry, windows):
    where = starts()
    tail = geometry.place("layer_vec")
    regions = [(0, geometry.place("conv_w")), (tail, geometry.begins[-1] + geometry.window)]
    jobs = [
        (0, 0, high - low, 1) + geometry.pieces(low, high) for low, high in regions
    ]
    most = max(job[2] for job in jobs)
    copies = max(len(job[4]) + len(job[5]) for job in jobs)
    edges = max([1] + [len(job[5]) for job in jobs])
    slots = LAYERS * (8 + FF // D)
    offset = where["w_head"] - where["gate_proj"]
    rest = -(-(-(-offset // 128)) // 8) * 8
    return pl.pallas_call(
        functools.partial(
            small_kernel, jobs=jobs, phase=geometry.phase, lead=offset % 128, whole=offset // 128
        ),
        in_specs=[pl.BlockSpec(memory_space=pl.ANY)],
        out_shape=[
            jax.ShapeDtypeStruct((PATCH_IN, D), BF),
            jax.ShapeDtypeStruct((4, D), F32),
            jax.ShapeDtypeStruct((slots, D), F32),
            jax.ShapeDtypeStruct((LAYERS, FF), F32),
            jax.ShapeDtypeStruct((rest, 128), F32),
            jax.ShapeDtypeStruct((D, PROJ), BF),
        ],
        scratch_shapes=[
            pltpu.VMEM((DEPTH, most, 128), BF),
            pltpu.VMEM((DEPTH, edges, TILE, 128), BF),
            pltpu.VMEM((most, 128), F32),
            pltpu.VMEM((D * PROJ // 128, 128), F32),
            pltpu.SemaphoreType.DMA((DEPTH, copies)),
        ],
        compiler_params=pltpu.CompilerParams(vmem_limit_bytes=VMEM_LIMIT),
    )(windows)


def pack_kernel(code_ref, *refs, plans, empty):
    sources, out_ref, sems = refs[:-2], refs[-2], refs[-1]
    turn = code_ref[1]
    for slot in range(empty):
        out_ref[slot] = jnp.zeros_like(out_ref[slot])
    for code, plan in enumerate(plans):

        @pl.when(code_ref[0] == code)
        def _():
            copies = [
                pltpu.make_async_copy(
                    sources[source].at[pl.ds(begin, count)],
                    out_ref.at[jnp.bitwise_xor(slot, turn), pl.ds(low, count)],
                    sems.at[index],
                )
                for index, (source, begin, slot, low, count) in enumerate(plan)
            ]
            for copy in copies:
                copy.start()
            for copy in copies:
                copy.wait()


def pack_plans(geometry, spans, slots):
    plans = []
    for code in range(geometry.code_count):
        plan = []
        for slot in slots:
            begin = geometry.begins[slot * geometry.code_count + code]
            stop = begin + geometry.window
            row = begin
            while row < stop:
                place, rows, source, inner = next(
                    item for item in spans[code] if item[0] <= row < item[0] + item[1]
                )
                count = min(stop, place + rows) - row
                plan.append((source, inner + row - place, slot, row - begin, count))
                row += count
        plans.append(plan)
    return plans


def pack(geometry, code_index, sources, spans, low, high, turn=0):
    plans = pack_plans(geometry, spans, range(low, high))
    return pl.pallas_call(
        functools.partial(pack_kernel, plans=plans, empty=low),
        in_specs=[pl.BlockSpec(memory_space=pltpu.SMEM)]
        + [pl.BlockSpec(memory_space=pl.ANY)] * len(sources),
        out_specs=pl.BlockSpec(memory_space=pltpu.VMEM),
        out_shape=jax.ShapeDtypeStruct((high, geometry.window, 128), BF),
        scratch_shapes=[pltpu.SemaphoreType.DMA((max(len(plan) for plan in plans),))],
        compiler_params=pltpu.CompilerParams(vmem_limit_bytes=VMEM_LIMIT),
    )(jnp.stack([code_index, jnp.int32(turn)]).astype(jnp.int32), *sources)


def front_slots(geometry):
    stop = geometry.place("w_qkv")
    count = sum(
        geometry.begins[slot * geometry.code_count + geometry.code_count - 1] + geometry.window
        <= stop
        for slot in range(geometry.dp_count)
    )
    if geometry.dp_count & (geometry.dp_count - 1) or not count:
        return 0
    return 1 << (count.bit_length() - 1)


def add_low(left, right):
    return (left.astype(F32) + right.astype(F32)).astype(BF)


def reduce_front(held, dp_count):
    count = held.shape[0]
    bit = count // 2
    while bit:
        moved = lax.ppermute(held[bit:], "dp", [(i, i ^ bit) for i in range(dp_count)])
        held = add_low(held[:bit], moved)
        bit //= 2
    bits = []
    while count < dp_count:
        bits.append(count)
        count *= 2
    middle = held.shape[1] // (2 * TILE) * TILE
    halves = [held[0, :middle], held[0, middle:]]
    for number in range(len(bits)):
        for side, bit in enumerate((bits[number], bits[-1 - number])):
            moved = lax.ppermute(
                halves[side], "dp", [(i, i - bit) for i in range(dp_count) if i & bit]
            )
            halves[side] = add_low(halves[side], moved)
    return jnp.concatenate(halves, axis=0)


def tail_kernel(*refs, lead, whole):
    vectors = refs[:-4]
    small_ref, head_ref, out_ref, turn_ref = refs[-4:]
    begin = 0
    for vector_ref in vectors:
        if len(vector_ref.shape) == 2:
            for row in range(2):
                for low in range(0, D, 128):
                    turn_ref[begin : begin + 1, :] = vector_ref[row : row + 1, low : low + 128]
                    begin += 1
        else:
            for low in range(0, vector_ref.shape[0], 128):
                turn_ref[begin : begin + 1, :] = vector_ref[low : low + 128].reshape(1, 128)
                begin += 1
    turn_ref[begin:, :] = jnp.zeros((turn_ref.shape[0] - begin, 128), F32)
    turn_ref[begin : begin + small_ref.shape[0], :] = small_ref[...]
    begin += whole
    rows = head_ref.shape[0]
    turned = pltpu.roll(head_ref[...], lead, 1) if lead else head_ref[...]
    lane = lax.broadcasted_iota(jnp.int32, (1, 128), 1)
    turn_ref[begin : begin + rows, :] += jnp.where(lane >= lead, turned, 0.0)
    turn_ref[begin + 1 : begin + 1 + rows, :] += jnp.where(lane < lead, turned, 0.0)
    out_ref[...] = turn_ref[...].astype(BF)


def tail_grad(vectors, small, grad_head, rows):
    lead, whole = small.shape[0] % 128, small.shape[0] // 128
    small = jnp.pad(small, (0, -small.shape[0] % 128)).reshape(-1, 128)
    return pl.pallas_call(
        functools.partial(tail_kernel, lead=lead, whole=whole),
        out_shape=jax.ShapeDtypeStruct((rows, 128), BF),
        scratch_shapes=[pltpu.VMEM((rows, 128), F32)],
        compiler_params=pltpu.CompilerParams(vmem_limit_bytes=VMEM_LIMIT),
    )(*vectors, small, grad_head)


def blocks_of_code(block):
    count = lax.axis_size("code")
    return [block] + [
        lax.ppermute(block, "code", [(i, (i + step) % count) for i in range(count)])
        for step in range(1, count)
    ]


def side_kernel(code_ref, *refs):
    blocks, out_ref = refs[:-1], refs[-1]
    count, width = len(blocks), blocks[0].shape[1]
    for code in range(count):

        @pl.when(code_ref[0] == code)
        def _():
            for source in range(count):
                out_ref[:, source * width : (source + 1) * width] = blocks[
                    (code - source) % count
                ][...]


def side_by_side(block, code_index):
    blocks = blocks_of_code(block)
    rows, width = block.shape
    return pl.pallas_call(
        side_kernel,
        in_specs=[pl.BlockSpec(memory_space=pltpu.SMEM)]
        + [pl.BlockSpec(memory_space=pltpu.VMEM)] * len(blocks),
        out_specs=pl.BlockSpec(memory_space=pltpu.VMEM),
        out_shape=jax.ShapeDtypeStruct((rows, width * len(blocks)), block.dtype),
    )(jnp.full((1,), code_index, jnp.int32), *blocks)


def sum_over(value, axis):
    count = lax.axis_size(axis)
    if count & (count - 1):
        return lax.psum(value, axis)
    bit = 1
    while bit < count:
        value = value + lax.ppermute(value, axis, [(i, i ^ bit) for i in range(count)])
        bit *= 2
    return value


def sum_over_all(value):
    count = lax.axis_size("dp") * lax.axis_size("code")
    sent = jnp.broadcast_to(value[None], (count,) + value.shape)
    return jnp.sum(lax.all_to_all(sent, ("dp", "code"), 0, 0), axis=0)


def norm_forward(before, norm_gain, norm_shift):
    centred = before - jnp.mean(before, axis=-1, keepdims=True)
    inv_std = lax.rsqrt(jnp.mean(centred * centred, axis=-1, keepdims=True) + NORM_EPSILON)
    normed = centred * inv_std
    return (normed * norm_gain + norm_shift, normed, inv_std)


def norm_backward(upstream, normed, inv_std, norm_gain):
    scaled = upstream * norm_gain
    centred_grad = (
        scaled
        - jnp.mean(scaled, axis=-1, keepdims=True)
        - normed * jnp.mean(scaled * normed, axis=-1, keepdims=True)
    )
    return (
        centred_grad * inv_std,
        jnp.sum(upstream * normed, axis=0),
        jnp.sum(upstream, axis=0),
    )


def gelu(pre_act):
    return 0.5 * pre_act * (1.0 + lax.erf(pre_act * 0.7071067811865476))


def gelu_grad(pre_act):
    return (
        0.5 * (1.0 + lax.erf(pre_act * 0.7071067811865476))
        + pre_act * jnp.exp(-0.5 * pre_act * pre_act) * 0.3989422804014327
    )


def vec_part(vector, slot_index):
    return vector[slot_index : slot_index + 1]


def gate_maps():
    rows = (np.arange(D)[:, None] % HEAD_DIM == np.arange(HEAD_DIM)[None, :]).astype(np.float32)
    groups = np.arange(8)[:, None] // 4 == np.arange(2 * HEADS)[None, :] // HEADS
    own = np.arange(D)[:, None] // HEAD_DIM == np.arange(2 * HEADS)[None, :] % HEADS
    return rows, groups.astype(np.float32), own.astype(np.float32)


def exact_dot(left, right, dims=((1,), (0,))):
    return lax.dot_general(left, right, (dims, ((), ())), precision=HIGHEST)


def gate_columns(gate_weight):
    rows, groups, own = gate_maps()
    wide = gate_weight.astype(F32)
    sums = exact_dot(wide, jnp.asarray(groups))
    return exact_dot(jnp.asarray(rows), sums[:HEAD_DIM]) * own, sums[HEAD_DIM:]


def gate_forward(in_low, weights):
    columns, bias = weights["gate_columns"]
    high = columns.astype(BF)
    rest = (columns - high.astype(F32)).astype(BF)
    logit = dot_nn(in_low, jnp.concatenate([high, rest], axis=1))
    logit = logit[:, : 2 * HEADS] + logit[:, 2 * HEADS :] + bias
    pair = jax.nn.sigmoid(logit)
    first, second = pair[:, :HEADS], pair[:, HEADS:]
    gate_vals = first * (second * weights["gate_scale"].astype(F32) - 1.0) + 2.0
    return (gate_vals, first, second)


def gate_backward(grad_gate, first, second, in_low, weights):
    scale_vec = weights["gate_scale"].astype(F32)
    grad_scale = jnp.sum(grad_gate * first * second, axis=0)
    grad_one = grad_gate * (second * scale_vec - 1.0) * first * (1.0 - first)
    grad_two = grad_gate * first * scale_vec * second * (1.0 - second)
    both = jnp.concatenate([grad_one, grad_two], axis=1)
    rows, groups, own = gate_maps()
    high = both.astype(BF)
    rest = (both - high.astype(F32)).astype(BF)
    product = dot_tn(in_low, jnp.concatenate([high, rest], axis=1))
    product = (product[:, : 2 * HEADS] + product[:, 2 * HEADS :]) * own
    summed = exact_dot(jnp.asarray(rows), product, ((0,), (0,)))
    summed = jnp.concatenate([summed, jnp.sum(both, axis=0, keepdims=True)], axis=0)
    grad_proj = exact_dot(summed, jnp.asarray(groups), ((1,), (1,)))
    columns_high, columns_rest = split_low(weights["gate_columns"][0])
    grad_heads = dot_nt(
        jnp.concatenate([high, rest, high], axis=1),
        jnp.concatenate([columns_high, columns_high, columns_rest], axis=1),
    )
    return (grad_heads, grad_proj, grad_scale)


def layer_forward(hidden, fill, weights, span, pick):
    vector = weights["layer_vec"]
    in_low = hidden.astype(BF)
    shift = jnp.concatenate(
        [vec_part(vector, 0), jnp.zeros((1, D), F32), vec_part(vector, 1)], axis=1
    )
    scale = np.ones((1, 3 * D), np.float32)
    scale[:, :D] = HEAD_DIM ** (-0.5)
    qkv_low = ((dot_nn(in_low, weights["w_qkv"]) + shift) * scale).astype(BF)
    gate_vals, first, second = gate_forward(in_low, weights)
    gate_wide = jnp.pad(jnp.transpose(gate_vals), ((0, 16 - HEADS), (0, 0)))
    attended, lse, bias = attention_forward(qkv_low, gate_wide, span, fill, pick)
    attn_out = dot_nn(attended, weights["w_out"]) + vec_part(vector, 2)
    mid_rows, normed_one, inv_one = norm_forward(
        DEEP_ALPHA * hidden + attn_out, vec_part(vector, 3), vec_part(vector, 4)
    )
    mid_low = mid_rows.astype(BF)
    pre_act = dot_nn(mid_low, weights["w_up"]) + weights["up_bias"]
    act_low = gelu(pre_act).astype(BF)
    ffn_out = dot_nn(act_low, weights["w_down"]) + vec_part(vector, 5)
    final_rows, normed_two, inv_two = norm_forward(
        DEEP_ALPHA * mid_rows + ffn_out, vec_part(vector, 6), vec_part(vector, 7)
    )
    kept = (in_low, qkv_low, gate_wide, first, second, lse, attended, bias)
    kept += (mid_low, pre_act, act_low, normed_one, inv_one, normed_two, inv_two)
    return (final_rows, kept)


def layer_backward(upstream, kept, fill, weights, span, pick, grad_of):
    in_low, qkv_low, gate_wide, first, second, lse, attended, bias = kept[:8]
    mid_low, pre_act, act_low, normed_one, inv_one, normed_two, inv_two = kept[8:]
    vector = weights["layer_vec"]
    grad_res_two, grad_gain_two, grad_shift_two = norm_backward(
        upstream, normed_two, inv_two, vec_part(vector, 6)
    )
    ffn_low = grad_res_two.astype(BF)
    grad_down = grad_of("w_down", act_low, ffn_low, 512)
    grad_pre = dot_nt(ffn_low, weights["w_down"]) * gelu_grad(pre_act)
    pre_low = grad_pre.astype(BF)
    grad_up = grad_of("w_up", mid_low, pre_low, 256)
    grad_mid = DEEP_ALPHA * grad_res_two + dot_nt(pre_low, weights["w_up"])
    grad_res_one, grad_gain_one, grad_shift_one = norm_backward(
        grad_mid, normed_one, inv_one, vec_part(vector, 3)
    )
    out_low = grad_res_one.astype(BF)
    grad_out = grad_of("w_out", attended, out_low, 384)
    grad_att = dot_nt(out_low, weights["w_out"]).astype(BF)
    proj_low, part_sums, grad_gate, grad_span = attention_backward(
        qkv_low, grad_att, gate_wide, span, fill, lse, pick, bias
    )
    grad_heads, grad_gate_proj, grad_gate_scale = gate_backward(
        jnp.transpose(grad_gate[:HEADS]), first, second, in_low, weights
    )
    grad_qkv = grad_of("w_qkv", in_low, proj_low, 256)
    grad_hidden = DEEP_ALPHA * grad_res_one + dot_nt(proj_low, weights["w_qkv"]) + grad_heads
    grad_vec = [
        part_sums,
        jnp.sum(grad_res_one, axis=0),
        grad_gain_one,
        grad_shift_one,
        jnp.sum(grad_res_two, axis=0),
        grad_gain_two,
        grad_shift_two,
        jnp.sum(grad_pre, axis=0),
    ]
    grad_map = {
        "w_qkv": grad_qkv,
        "w_out": grad_out,
        "w_up": grad_up,
        "w_down": grad_down,
        "layer_vec": grad_vec,
        "gate_proj": grad_gate_proj,
        "gate_scale": grad_gate_scale,
    }
    return (grad_hidden, grad_map, grad_span)


def head_kernel(
    in_ref, weight_ref, code_ref, name_ref, target_ref, loss_ref, rows_ref, flat_ref, low_ref
):
    weight, codebook, names = weight_ref[...], code_ref[...], name_ref[0:1, :]
    loss = jnp.zeros((1, 1), F32)
    for low in range(0, in_ref.shape[0], BLOCK):
        rows = slice(low, low + BLOCK)
        projected = dot_nn(in_ref[rows, :], weight)
        inv_len = lax.rsqrt(jnp.sum(projected * projected, axis=1, keepdims=True) + UNIT_EPSILON)
        unit_rows = projected * inv_len
        logits = LOGIT_SCALE * dot_nt(unit_rows.astype(BF), codebook)
        target = target_ref[rows, 0:1]
        live = jnp.where(target >= 0, 1.0, 0.0)
        hits = jnp.where(names == target, 1.0, 0.0)
        top = jnp.max(logits, axis=1, keepdims=True)
        weights = jnp.exp(logits - top)
        total = jnp.sum(weights, axis=1, keepdims=True)
        picked = jnp.sum(logits * hits, axis=1, keepdims=True)
        loss += jnp.sum((top + jnp.log(total) - picked) * live, axis=0, keepdims=True)
        grad_logits = (weights * (1.0 / total) - hits) * (live * LOGIT_SCALE)
        grad_unit = dot_nn(grad_logits.astype(BF), codebook)
        grad_proj = (
            grad_unit - unit_rows * jnp.sum(unit_rows * grad_unit, axis=1, keepdims=True)
        ) * inv_len
        proj_low = grad_proj.astype(BF)
        low_ref[rows, :] = proj_low
        rows_ref[rows, :] = dot_nt(proj_low, weight)
    loss_ref[...] = jnp.broadcast_to(loss, loss_ref.shape)
    grad = dot_tn(in_ref[...], low_ref[...])
    strips = PROJ // 128
    for strip in range(strips):
        flat_ref[pl.ds(strip, D, stride=strips), :] = grad[:, strip * 128 : (strip + 1) * 128]


def head_pass(hidden, w_head, codebook, names, targets):
    loss, grad_rows, grad_head = pl.pallas_call(
        head_kernel,
        out_shape=[
            jax.ShapeDtypeStruct((8, 128), F32),
            jax.ShapeDtypeStruct((ROWS, D), F32),
            jax.ShapeDtypeStruct((D * PROJ // 128, 128), F32),
        ],
        scratch_shapes=[pltpu.VMEM((ROWS, PROJ), BF)],
        compiler_params=pltpu.CompilerParams(vmem_limit_bytes=VMEM_LIMIT),
    )(hidden.astype(BF), w_head, codebook, names, targets)
    return (loss[0, 0], grad_rows, grad_head)


def local(
    patches,
    lengths,
    patch_masks,
    targets,
    codebook,
    params,
    first_moment,
    second_moment,
    step_count,
):
    dp_count = lax.axis_size("dp")
    code_count = lax.axis_size("code")
    code_index = lax.axis_index("code")
    shard_len = params.shape[0]
    shard_rows = shard_len // 128
    dp_index = lax.axis_index("dp")
    geometry = Geometry(dp_count, code_count, shard_rows)
    own_offset = lax.rem((dp_index * code_count + code_index) * shard_rows + geometry.phase, TILE)
    spare = geometry.window - shard_rows
    own_window = lax.dynamic_slice(
        jnp.pad(params.reshape(shard_rows, 128), ((TILE, spare), (0, 0))),
        (TILE - own_offset, 0),
        (geometry.window, 128),
    ).astype(BF)
    windows = lax.all_gather(own_window, ("dp", "code"), axis=0, tiled=False)
    where = starts()

    places = jnp.arange(ROWS, dtype=jnp.int32)
    mask_row = jnp.pad(patch_masks[0], (0, ROWS - LONG))
    live_slot = places < jnp.minimum(lengths[0], LONG)
    visible = live_slot & (mask_row == 0)
    rank = jnp.cumsum(visible.astype(jnp.int32)) - 1
    pick = (
        visible[None, :] & (rank[None, :] == jnp.arange(SEEN, dtype=jnp.int32)[:, None])
    )
    pick_low = pick.astype(BF)
    near = jnp.sum(pick_low.reshape(SEEN, ROWS // BLOCK, BLOCK), axis=1)
    hop = jnp.sum(pick.astype(F32).reshape(SEEN, ROWS // BLOCK, BLOCK), axis=2)
    flip = jnp.concatenate([jnp.transpose(near)] * 2, axis=1)
    pick_seen = (pick_low, near, jnp.pad(hop, ((0, 0), (0, BLOCK - ROWS // BLOCK))), flip)
    pick_full = pick.astype(F32)
    seen_valid = jnp.arange(SEEN, dtype=jnp.int32) < lengths[0] // 4
    seen_fill = jnp.broadcast_to(jnp.where(seen_valid, 0.0, MASK_FILL)[:, None], (SEEN, BLOCK))
    live_fill = jnp.broadcast_to(jnp.where(live_slot, 0.0, MASK_FILL)[:, None], (ROWS, BLOCK))
    live_float = live_slot.astype(F32)[:, None]
    all_codes = jnp.concatenate(blocks_of_code(codebook), axis=0)
    code_places = (
        code_index - jnp.arange(code_count, dtype=jnp.int32) + code_count
    ) % code_count * codebook.shape[0]
    code_names = (
        code_places[:, None] + jnp.arange(codebook.shape[0], dtype=jnp.int32)[None, :]
    ).reshape(1, -1)
    patch_rows = jnp.pad(patches[0], ((0, ROWS - LONG), (0, 0)))
    target_codes = jnp.where(mask_row == 1, jnp.pad(targets[0], (0, ROWS - LONG)), -1)
    target_wide = jnp.broadcast_to(target_codes[:, None], (ROWS, 128))
    name_wide = jnp.broadcast_to(code_names, (8, code_names.shape[1]))
    w_patch, glob_vec, vectors, up_bias, rest, w_head = unpack_small(geometry, windows)
    rest = rest.reshape(-1)

    def values(seg_name):
        extent = dict(layout())[seg_name]
        begin = where[seg_name] - where["gate_proj"]
        return rest[begin : begin + math.prod(extent)].reshape(extent)

    gate_proj = values("gate_proj")
    gate_scale = values("gate_scale")
    rel_table = values("rel_table").astype(BF)
    conv_weight = unpack_conv(geometry, windows, code_index)
    specs = [
        spec
        for index in range(LAYERS)
        for spec in (
            (geometry.place("w_qkv", index), D, 3 * D // 128, 128),
            (geometry.place("w_out", index), D, D // 128, 384),
            (geometry.place("w_up", index), D, FF // 128, 128),
            (geometry.place("w_down", index), FF, D // 128, 512),
        )
    ]
    unpacked = unpack(geometry, windows, specs)
    weights = []
    for index in range(LAYERS):
        mats = unpacked[4 * index : 4 * index + 4]
        weights.append(
            dict(zip(("w_qkv", "w_out", "w_up", "w_down"), mats))
            | {
                "layer_vec": vectors[index * (8 + FF // D) :],
                "up_bias": up_bias[index : index + 1],
                "gate_columns": gate_columns(gate_proj[index]),
                "gate_scale": gate_scale[index],
            }
        )

    span_table = span_onehot()
    span = dot_tn(
        jnp.pad(rel_table, ((0, 0), (0, 16 - HEADS))), jnp.asarray(span_table.T, BF)
    )

    embedded = dot_nn(patch_rows, w_patch)
    normed_rows, normed_zero, inv_zero = norm_forward(embedded, glob_vec[0 : 1], glob_vec[1 : 2])
    start_rows = normed_rows * live_float
    conv_in = start_rows.astype(BF)
    width = D // code_count
    own_cols = code_index * width
    own_in = lax.dynamic_slice_in_dim(conv_in, own_cols, width, 1)
    half = KERNEL // 2
    conv_own = conv_call(conv_forward_kernel, own_in[:LONG], conv_weight, half, False)
    seen_own = lax.dot_general(
        pick_full, conv_own, (((1,), (0,)), ((), ())), precision=HIGHEST
    )
    seen_raw = side_by_side(seen_own, code_index)
    seen_pre = seen_raw + glob_vec[2 : 3]
    seen_start = lax.dot_general(
        pick_full, start_rows, (((1,), (0,)), ((), ())), precision=HIGHEST
    )
    seen_rows = seen_start + gelu(seen_pre)
    encoded, kept_first = layer_forward(seen_rows, seen_fill, weights[0], span, pick_seen)
    placed = lax.dot_general(
        pick_full, encoded, (((0,), (0,)), ((), ())), precision=HIGHEST
    )
    hidden = jnp.where(visible[:, None], placed, glob_vec[3 : 4])
    final, kept_second = layer_forward(hidden, live_fill, weights[1], span, None)
    loss_local, upstream, grad_head = head_pass(final, w_head, all_codes, name_wide, target_wide)

    def grad_maker(index):
        return lambda seg_name, left, right, rows: (
            left, right, geometry.place(seg_name, index), rows
        )

    upstream, map_second, span_second = layer_backward(
        upstream, kept_second, live_fill, weights[1], span, None, grad_maker(1)
    )
    grad_mask_emb = jnp.sum(jnp.where(visible[:, None], 0.0, upstream), axis=0)
    grad_encoded = lax.dot_general(
        pick_full, upstream, (((1,), (0,)), ((), ())), precision=HIGHEST
    )
    grad_seen, map_first, span_first = layer_backward(
        grad_encoded, kept_first, seen_fill, weights[0], span, pick_seen, grad_maker(0)
    )
    grad_seen = grad_seen * seen_valid[:, None].astype(F32)
    grad_conv_seen = grad_seen * gelu_grad(seen_pre)
    grad_conv = dot_tn(pick_low, grad_conv_seen.astype(BF)).astype(BF)
    grad_full = lax.dot_general(
        pick_full, grad_seen, (((0,), (0,)), ((), ())), precision=HIGHEST
    )
    own_grad = lax.dynamic_slice_in_dim(grad_conv, own_cols, width, 1)
    grad_in_own = conv_call(conv_input_kernel, own_grad[:LONG], conv_weight, half - 1, True)
    grad_conv_in = side_by_side(grad_in_own.astype(BF), code_index)
    split = front_slots(geometry)
    padded, grads = conv_weight_inputs(conv_in[:LONG], grad_conv)
    rest_grad = conv_weight_grad(
        padded, grads, geometry, code_index, range(split, dp_count), CHUNK // 2
    )
    grad_start = (grad_full + grad_conv_in.astype(F32)) * live_float
    grad_embedded, grad_gain_zero, grad_shift_zero = norm_backward(
        grad_start, normed_zero, inv_zero, glob_vec[0 : 1]
    )
    grad_patch = dot_tn(patch_rows, grad_embedded.astype(BF))
    grad_glob = jnp.stack(
        [grad_gain_zero, grad_shift_zero, jnp.sum(grad_conv_seen, axis=0), grad_mask_emb]
    )
    grad_rel = lax.dot_general(
        jnp.asarray(span_table),
        (span_first + span_second)[:HEADS],
        (((0,), (1,)), ((), ())),
        precision=HIGHEST,
    )
    leader = (code_index == 0).astype(F32)
    count_local = jnp.sum((target_codes >= 0).astype(F32))
    early = jnp.concatenate(
        [
            (grad_rel * leader).reshape(-1, 128),
            jnp.full((1, 128), loss_local * leader),
            jnp.full((1, 128), count_local * leader),
        ]
    )
    early = sum_over(sum_over(jnp.pad(early, ((0, -early.shape[0] % 8), (0, 0))), "dp"), "code")
    both = (map_first, map_second)
    sources, spans = [], [[] for _ in range(code_count)]

    def add_source(found):
        array, (chunks, base, unit, chunk) = found
        for code, items in enumerate(chunk_spans(chunks, base, unit, chunk, len(sources))):
            spans[code] += items
        sources.append(array)

    pairs = [
        layer_map[seg_name]
        for layer_map in both[::-1]
        for seg_name in ("w_down", "w_up", "w_out", "w_qkv")
    ]
    for found in weight_grads(pairs, geometry, code_index):
        add_source(found)
    add_source(rest_grad)
    tail_place = geometry.place("layer_vec")
    vectors = [vector for layer_map in both for vector in layer_map["layer_vec"]]
    small = [layer_map[seg_name] for seg_name in ("gate_proj", "gate_scale") for layer_map in both]
    small = jnp.concatenate([part.reshape(-1) for part in small + [grad_rel]])
    tail_rows = geometry.begins[-1] + geometry.window - tail_place
    tail = tail_grad(vectors, small, grad_head, tail_rows)
    for items in spans:
        items.append((tail_place, tail_rows, len(sources), 0))
    sources.append(tail)
    front = jnp.concatenate([grad_patch.reshape(-1, 128), grad_glob.reshape(-1, 128)], axis=0)
    front = jnp.pad(front, ((geometry.phase, 0), (0, 0))).astype(BF)
    if split:
        own_part = pack(geometry, code_index, sources, spans, split, dp_count)
        reduced = lax.psum_scatter(own_part, "dp", scatter_dimension=0, tiled=False)
        sources, spans = [], [[] for _ in range(code_count)]
        add_source(conv_weight_grad(padded, grads, geometry, code_index, range(split)))
    front, early = lax.optimization_barrier((front, early))
    for items in spans:
        items.append((0, front.shape[0], len(sources), 0))
    sources.append(front)
    turn = dp_index % split if split else 0
    last_part = pack(geometry, code_index, sources, spans, 0, split or dp_count, turn)
    if split:
        first = reduce_front(last_part, dp_count)
        reduced = jnp.where(dp_index < split, first, reduced)
    else:
        reduced = lax.psum_scatter(last_part, "dp", scatter_dimension=0, tiled=False)
    reduced = reduced.reshape(geometry.window, 128).astype(F32)
    reduced = lax.dynamic_slice(reduced, (own_offset, 0), (shard_rows, 128)).reshape(shard_len)
    squares_all = sum_over_all(jnp.full((8, 128), jnp.sum(reduced * reduced)))
    squares_all = squares_all[0, 0]
    rel_rows = BUCKETS * HEADS // 128
    rel_all = early[:rel_rows].reshape(BUCKETS, HEADS)
    loss_all, count_all = early[rel_rows, 0], early[rel_rows + 1, 0]
    grad_norm = jnp.sqrt(squares_all) / count_all
    clip_factor = jnp.minimum(1.0, CLIP_NORM / grad_norm)
    clipped = reduced / count_all * clip_factor
    rel_grad = rel_all / count_all * clip_factor
    step_value = step_count[0].astype(F32)
    new_first = BETA_ONE * first_moment + (1.0 - BETA_ONE) * clipped
    new_second = BETA_TWO * second_moment + (1.0 - BETA_TWO) * clipped * clipped
    first_hat = new_first / (1.0 - BETA_ONE**step_value)
    second_hat = new_second / (1.0 - BETA_TWO**step_value)
    new_params = params - LEARN_RATE * (
        first_hat / (jnp.sqrt(second_hat) + ADAM_EPSILON) + WEIGHT_DECAY * params
    )
    return (
        new_params,
        new_first,
        new_second,
        new_params.astype(BF),
        loss_all / count_all,
        grad_norm,
        rel_grad,
    )


def solution(mesh):
    placed = (
        P("dp", None, None),
        P("dp"),
        P("dp", None),
        P("dp", None),
        P("code", None),
        P(("dp", "code")),
        P(("dp", "code")),
        P(("dp", "code")),
        P(),
    )
    return jax.shard_map(
        local,
        mesh=mesh,
        in_specs=placed,
        out_specs=(
            P(("dp", "code")),
            P(("dp", "code")),
            P(("dp", "code")),
            P(("dp", "code")),
            P(),
            P(),
            P(),
        ),
        check_vma=False,
    )
```
